512 devices in a mesh: gx: 32 (over z, core), gy: 16 (over x, y).
Axes of the slice: x: 4, y: 4, z: 16, core: 2. Of those that a mesh axis runs over, the one named last changes fastest.
Arguments:
- prior: float32 [3, 2, 4, 128, 128, 128], P(None, None, None, 'gx', 'gy'), may hold values from -1.25 to 1.25
- coefficient: float32 [128, 128, 128], P('gx', 'gy'), may hold values from 0.2 to 2
Outputs:
- new_blocks: float32 [2, 2, 4, 128, 128, 128], P(None, None, None, 'gx', 'gy')
The draws below stay inside these ranges and needn't reach their ends.
All inputs are finite; a program needn't handle non-finite values.
Results may differ from the reference program's by a relative error of at most 0.0003.
Values sent between devices are 32-bit elements; how exact they have to be, the bound alone decides.
No kernel may reach another device: no remote copies, remote signals or barrier semaphores. Data moves between devices by JAX's collectives and lax.ppermute only.
A program may use at most 64 MiB of HBM per device.

```python
import math
import jax
import jax.numpy as jnp
from jax import lax

NZ = 128
SOURCES = 4
ITERS = 2
SWEEPS = 4
NX = 128
NY = 128


def mixed_phases(first_key, second_key, weight):
    shape = (3, SOURCES, NX, NY, NZ)
    theta = jax.random.uniform(first_key, shape, jnp.float32, -3.14159265, 3.14159265)
    common = jax.random.uniform(second_key, (NX, NY, NZ), jnp.float32, -3.14159265, 3.14159265)
    scale = 1.0 / jnp.sqrt(1.0 + weight * weight)
    real_part = (jnp.cos(theta) + weight * jnp.cos(common)[None, None]) * scale
    imag_part = (jnp.sin(theta) + weight * jnp.sin(common)[None, None]) * scale
    return jnp.stack([real_part, imag_part], 1)


def draw_prior(key, part):
    key = jax.random.fold_in(key, 11)
    first_key, second_key = jax.random.split(key)
    return mixed_phases(first_key, second_key, 0.15)


def block_scale(rng, dims, pieces, least, largest):
    def one(axis_at, parts):
        heights = jax.random.uniform(jax.random.fold_in(jax.random.fold_in(rng, 6), axis_at), (parts,), jnp.float32, least / len(pieces), largest / len(pieces))
        return jnp.repeat(jnp.exp(heights), dims[axis_at] // parts).reshape((-1,) + (1,) * (len(dims) - axis_at - 1))

    level = one(*pieces[0])
    for cut in pieces[1:]:
        level = level * one(*cut)
    return level


def setup_inputs(seed: int = 0) -> dict:
    streams_of = jax.random.split(jax.random.key(seed), 3)
    return {
        "prior": draw_prior(jax.random.fold_in(streams_of[2], 71), 0),
        "coefficient": jnp.clip(jnp.exp(math.log(2.0) - 2.3025851 * jax.random.uniform(streams_of[1], (NX, NY, NZ), jnp.float32) ** block_scale(streams_of[1], (NX, NY, NZ), ((0, 32), (1, 16)), -0.2, 0.2)), 0.2, 2.0),
    }


HIGHEST = lax.Precision.HIGHEST

def flatten_fields(block):
    return block.reshape(block.shape[0] * block.shape[1] * block.shape[2], -1)

def real_gram(left, right):
    return lax.dot_general(flatten_fields(left), flatten_fields(right), (((1,), (1,)), ((), ())), precision=HIGHEST)

def to_complex(gram, left_count, right_count):
    sources = gram.shape[1] // (2 * right_count)
    grid = gram.reshape(left_count, 2, sources, right_count, 2, sources)
    real_part = grid[:, 0, :, :, 0, :] + grid[:, 1, :, :, 1, :]
    imag_part = grid[:, 0, :, :, 1, :] - grid[:, 1, :, :, 0, :]
    shape = (left_count * sources, right_count * sources)
    return (real_part.reshape(shape), imag_part.reshape(shape))

def combine(fields, real_coef, imag_coef):
    count = fields.shape[0]
    sources = real_coef.shape[1]
    upper = jnp.concatenate([real_coef, imag_coef], 1).reshape(count, 1, sources, 2 * sources)
    lower = jnp.concatenate([-imag_coef, real_coef], 1).reshape(count, 1, sources, 2 * sources)
    mapping = jnp.concatenate([upper, lower], 1).reshape(count * 2 * sources, 2 * sources)
    result = lax.dot_general(mapping, flatten_fields(fields), (((0,), (0,)), ((), ())), precision=HIGHEST)
    return result.reshape(fields.shape[1:])

def cholesky_inverse(gram_real, gram_imag):
    count = gram_real.shape[0]
    upper_re = [[None] * count for _ in range(count)]
    upper_im = [[None] * count for _ in range(count)]
    for s in range(count):
        pivot = gram_real[s, s]
        for k in range(s):
            pivot = pivot - upper_re[k][s] * upper_re[k][s] - upper_im[k][s] * upper_im[k][s]
        diagonal = jnp.sqrt(pivot)
        upper_re[s][s] = diagonal
        upper_im[s][s] = 0.0 * diagonal
        for t in range(s + 1, count):
            entry_re = gram_real[s, t]
            entry_im = gram_imag[s, t]
            for k in range(s):
                entry_re = entry_re - (upper_re[k][s] * upper_re[k][t] + upper_im[k][s] * upper_im[k][t])
                entry_im = entry_im - (upper_re[k][s] * upper_im[k][t] - upper_im[k][s] * upper_re[k][t])
            upper_re[s][t] = entry_re / diagonal
            upper_im[s][t] = entry_im / diagonal
    zero_value = 0.0 * gram_real[0, 0]
    inverse_re = [[zero_value] * count for _ in range(count)]
    inverse_im = [[zero_value] * count for _ in range(count)]
    for t in range(count):
        inverse_re[t][t] = 1.0 / upper_re[t][t]
        for s in range(t):
            accum_re = zero_value
            accum_im = zero_value
            for k in range(s, t):
                accum_re = accum_re + inverse_re[s][k] * upper_re[k][t] - inverse_im[s][k] * upper_im[k][t]
                accum_im = accum_im + inverse_re[s][k] * upper_im[k][t] + inverse_im[s][k] * upper_re[k][t]
            inverse_re[s][t] = -accum_re / upper_re[t][t]
            inverse_im[s][t] = -accum_im / upper_re[t][t]
    stacked_re = jnp.stack([jnp.stack(row) for row in inverse_re])
    stacked_im = jnp.stack([jnp.stack(row) for row in inverse_im])
    return (stacked_re, stacked_im)

def apply_inverse(field, coefficient):
    real_diag = 6.0 - coefficient
    imag_diag = 0.5 * coefficient
    denom = real_diag * real_diag + imag_diag * imag_diag
    out_real = (real_diag * field[0] + imag_diag * field[1]) / denom
    out_imag = (real_diag * field[1] - imag_diag * field[0]) / denom
    return jnp.stack([out_real, out_imag])

def neighbours(field):
    padded = jnp.pad(field, ((0, 0), (0, 0), (1, 1), (1, 1), (1, 1)))
    total = padded[:, :, 2:, 1:-1, 1:-1] + padded[:, :, :-2, 1:-1, 1:-1]
    total = total + padded[:, :, 1:-1, 2:, 1:-1] + padded[:, :, 1:-1, :-2, 1:-1]
    total = total + padded[:, :, 1:-1, 1:-1, 2:] + padded[:, :, 1:-1, 1:-1, :-2]
    return total

def smoothed_image(block, coefficient):
    solution = 0.8 * apply_inverse(block, coefficient)
    for sweep in range(SWEEPS - 1):
        solution = 0.2 * solution + 0.8 * apply_inverse(block + neighbours(solution), coefficient)
    return (6.0 - coefficient) * solution - neighbours(solution)

def orthogonalize(window, fresh, cells):
    count = window.shape[0]
    first = real_gram(window, fresh[None]) / cells
    coef_re, coef_im = to_complex(first, count, 1)
    once = fresh - combine(window, coef_re, coef_im)
    second = real_gram(window, once[None]) / cells
    coef_re, coef_im = to_complex(second, count, 1)
    twice = once - combine(window, coef_re, coef_im)
    norms = real_gram(twice[None], twice[None]) / cells
    gram_re, gram_im = to_complex(norms, 1, 1)
    inverse_re, inverse_im = cholesky_inverse(gram_re, gram_im)
    return combine(twice[None], inverse_re, inverse_im)

def reference(prior, coefficient):
    cells = coefficient.size
    window = prior
    current = prior[2]
    results = []
    for step in range(ITERS):
        fresh = smoothed_image(current, coefficient)
        current = orthogonalize(window, fresh, cells)
        results.append(current)
        window = jnp.concatenate([window[1:], current[None]], 0)
    return jnp.stack(results)
```

```python
import functools

import jax
import jax.numpy as jnp
import numpy as np
from jax import lax
from jax.experimental import pallas as pl
from jax.experimental.pallas import tpu as pltpu
from jax.sharding import Mesh, PartitionSpec as P

LX, LY, NZ = 4, 8, 128
HALO = 4
EX, EY = LX + 2 * HALO, LY + 2 * HALO
WIDTHS = [EX - 2 * d for d in range(1, HALO + 1)]
STARTS = [sum(WIDTHS[:d]) for d in range(HALO)]
RIM = sum(WIDTHS)
BLOCKS = 7
ROWS = 64
F32 = jnp.float32
BF16 = jnp.bfloat16
HIGHEST = lax.Precision.HIGHEST
VMEM = pl.BlockSpec(memory_space=pltpu.VMEM)


def plane_of(parts, index):
    low, own, high = parts
    if index < HALO:
        return low, index
    if index < HALO + LX:
        return own, index - HALO
    return high, index - HALO - LX


def rim_kernel(groups, with_coefficient, *refs):
    own, low, high, up, down = refs[:5]
    for group in range(groups):
        for d in range(1, HALO + 1):
            for i in range(WIDTHS[d - 1]):
                ref, x = plane_of((low, own, high), d + i)
                spot = group * RIM + STARTS[d - 1] + i
                up[spot] = ref[group * LX + x, pl.ds((LY - d) * 8, 8), :]
                down[spot] = ref[group * LX + x, pl.ds((d - 1) * 8, 8), :]
    if with_coefficient:
        up[RIM + 3] = jnp.zeros((8, NZ), F32)
        down[RIM + 3] = jnp.zeros((8, NZ), F32)
        for d in range(1, HALO + 1):
            for i in range(WIDTHS[d - 1]):
                ref, x = plane_of((low, own, high), d + i)
                spot = STARTS[d - 1] + i
                tile, row = RIM + spot // 8, spot % 8
                up[tile, pl.ds(row, 1), :] = ref[x, pl.ds(LY * 8 + LY - d, 1), :]
                down[tile, pl.ds(row, 1), :] = ref[x, pl.ds(LY * 8 + d - 1, 1), :]


def pack_rim(groups, with_coefficient, own, low, high):
    shape = jax.ShapeDtypeStruct((groups * RIM + (4 if with_coefficient else 0), 8, NZ), F32)
    return pl.pallas_call(
        functools.partial(rim_kernel, groups, with_coefficient),
        out_shape=(shape, shape),
        in_specs=[VMEM] * 3,
        out_specs=(VMEM, VMEM),
        name="pack_rim",
    )(own, low, high)


def fill_block(group, parts, from_low, from_high, wide):
    low, own, high = parts
    wide[...] = jnp.zeros(wide.shape, F32)
    for index in range(EX):
        ref, x = plane_of(parts, index)
        wide[index, HALO:HALO + LY] = ref[group * LX + x, pl.ds(0, LY * 8), :].reshape(LY, 8, NZ)
    for d in range(1, HALO + 1):
        spot = group * RIM + STARTS[d - 1]
        for i in range(WIDTHS[d - 1]):
            wide[d + i, HALO - d] = from_low[spot + i]
            wide[d + i, HALO + LY - 1 + d] = from_high[spot + i]


def fill_coefficient(parts, from_low, from_high, wide):
    wide[...] = jnp.zeros(wide.shape, F32)
    for index in range(EX):
        ref, x = plane_of(parts, index)
        wide[index, HALO:HALO + LY] = ref[x, pl.ds(LY * 8, LY), :]
    for d in range(1, HALO + 1):
        for i in range(WIDTHS[d - 1]):
            spot = STARTS[d - 1] + i
            tile, row = RIM + spot // 8, spot % 8
            wide[d + i, pl.ds(HALO - d, 1), :] = from_low[tile, pl.ds(row, 1), :]
            wide[d + i, pl.ds(HALO + LY - 1 + d, 1), :] = from_high[tile, pl.ds(row, 1), :]


def fill_tables(coef, table_re, table_im, diag_re, diag_im):
    value = coef[...]
    real = 6.0 - value
    imag = 0.5 * value
    scale = jnp.where(value > 0.0, 0.8 / (real * real + imag * imag), 0.0)
    diag_re[...] = real * scale
    diag_im[...] = imag * scale
    sign = jnp.where(lax.broadcasted_iota(jnp.int32, (8, NZ), 0) < 4, 1.0, -1.0)

    def body(x, carry):
        for y in range(EY):
            table_re[x, y] = jnp.broadcast_to(diag_re[x, pl.ds(y, 1), :], (8, NZ))
            table_im[x, y] = jnp.broadcast_to(diag_im[x, pl.ds(y, 1), :], (8, NZ)) * sign
        return carry

    lax.fori_loop(0, EX, body, 0)


def depth_sum(value):
    lane = lax.broadcasted_iota(jnp.int32, value.shape, 2)
    above = jnp.where(lane == 0, 0.0, pltpu.roll(value, 1, 2))
    below = jnp.where(lane == NZ - 1, 0.0, pltpu.roll(value, NZ - 1, 2))
    return above + below


def around(ref, x, low, high):
    total = ref[x - 1, low:high] + ref[x + 1, low:high]
    total = total + ref[x, low - 1:high - 1] + ref[x, low + 1:high + 1]
    return total + depth_sum(ref[x, low:high])


def smooth(block, coef, table_re, table_im, first, second, store):
    def solve(value, x, low, high):
        return (table_re[x, low:high] * value
                + table_im[x, low:high] * pltpu.roll(value, 4, 1))

    def start(x, carry):
        first[x] = solve(block[x], x, 0, EY)
        return carry

    lax.fori_loop(0, EX, start, 0)
    here, there = first, second
    for k in range(1, HALO):
        low, high = k, EY - k

        def sweep(x, carry, here=here, there=there, low=low, high=high):
            value = block[x, low:high] + around(here, x, low, high)
            there[x, low:high] = 0.2 * here[x, low:high] + solve(value, x, low, high)
            return carry

        lax.fori_loop(k, EX - k, sweep, 0)
        here, there = there, here

    def image(x, carry):
        low, high = HALO, HALO + LY
        for y in range(low, high):
            diag = 6.0 - coef[x, pl.ds(y, 1), :]
            total = here[x - 1, y] + here[x + 1, y] + here[x, y - 1] + here[x, y + 1]
            total = total + depth_sum(here[x, y:y + 1])[0]
            store(x - HALO, y - HALO, diag * here[x, y] - total)
        return carry

    lax.fori_loop(HALO, HALO + LX, image, 0)


BIG = pltpu.VMEM((EX, EY, 8, NZ), F32)
FLAT = pltpu.VMEM((EX, EY, NZ), F32)
SMOOTH_SCRATCH = [BIG, BIG, BIG, BIG, BIG, FLAT, FLAT]


def first_kernel(own, low, high, from_low, from_high, out, coef, block, first, second,
                 table_re, table_im, diag_re, diag_im):
    parts = (low, own, high)
    fill_block(0, parts, from_low, from_high, block)
    fill_coefficient(parts, from_low, from_high, coef)
    fill_tables(coef, table_re, table_im, diag_re, diag_im)

    def store(x, y, value):
        out[x, pl.ds(y * 8, 8), :] = value

    smooth(block, coef, table_re, table_im, first, second, store)


def first_image(*args):
    return pl.pallas_call(
        first_kernel,
        out_shape=(jax.ShapeDtypeStruct((LX, LY * 8, NZ), F32),
                   jax.ShapeDtypeStruct((EX, EY, NZ), F32)),
        in_specs=[VMEM] * 5,
        out_specs=(VMEM, VMEM),
        scratch_shapes=SMOOTH_SCRATCH,
        compiler_params=pltpu.CompilerParams(vmem_limit_bytes=24 << 20),
        cost_estimate=pl.CostEstimate(flops=6_000_000, bytes_accessed=2_000_000, transcendentals=0),
        name="first_image",
    )(*args)


def old_kernel(own, low, high, from_low, from_high, coef, out, block, first, second,
               table_re, table_im, diag_re, diag_im):
    fill_tables(coef, table_re, table_im, diag_re, diag_im)
    for group in range(2):
        fill_block(group, (low, own, high), from_low, from_high, block)

        def store(x, y, value, group=group):
            out[group * LX + x, pl.ds(y * 8, 8), :] = value

        smooth(block, coef, table_re, table_im, first, second, store)


def old_images(*args):
    return pl.pallas_call(
        old_kernel,
        out_shape=jax.ShapeDtypeStruct((2 * LX, LY * 8, NZ), F32),
        in_specs=[VMEM] * 6,
        out_specs=VMEM,
        scratch_shapes=SMOOTH_SCRATCH,
        compiler_params=pltpu.CompilerParams(vmem_limit_bytes=24 << 20),
        cost_estimate=pl.CostEstimate(flops=12_000_000, bytes_accessed=4_000_000, transcendentals=0),
        name="old_images",
    )(*args)


def split3(value):
    high = value.astype(BF16)
    rest = value - high.astype(F32)
    middle = rest.astype(BF16)
    low = (rest - middle.astype(F32)).astype(BF16)
    return high, middle, low


def basis_plane(old, recent, w, old_image, w_image, x):
    refs = [(old, x), (old, LX + x), (recent, x), (w, x), (old_image, x), (old_image, LX + x), (w_image, x)]
    rows = []
    for ref, index in refs:
        rows.append(jnp.concatenate([ref[index, pl.ds(y * 8, 8), :] for y in range(LY)], axis=1))
    rows.append(jnp.zeros((8, LY * NZ), F32))
    return jnp.concatenate(rows, axis=0)


def lane_roll(value, amount):
    return pltpu.roll(value, amount % NZ, 1)


SLOTS = [(0, 0), (0, 56), (1, 0), (1, 40), (1, 72), (1, 96), (0, 104)]


def pack_gram(gram):
    lane = lax.broadcasted_iota(jnp.int32, (8, NZ), 1)
    row = lax.broadcasted_iota(jnp.int32, (8, NZ), 0)
    packed = jnp.zeros((8, NZ), F32)
    for b in range(BLOCKS):
        rows = gram[8 * b:8 * b + 8]
        turned = jnp.where(lane % 8 < 4, lane_roll(rows, -4), -lane_roll(rows, 4))
        both = rows + pltpu.roll(turned, 4, 0)
        half, start = SLOTS[b]
        moved = lane_roll(both, start - 8 * b)
        if half:
            moved = pltpu.roll(moved, 4, 0)
        keep = (lane >= start) & (lane < start + 8 * (BLOCKS - b)) & (row // 4 == half)
        packed = packed + jnp.where(keep, moved, 0.0)
    return packed


def unpack_gram(packed):
    lane = lax.broadcasted_iota(jnp.int32, (8, NZ), 1)
    row = lax.broadcasted_iota(jnp.int32, (8, NZ), 0)
    rows = []
    for b in range(BLOCKS):
        half, start = SLOTS[b]
        moved = lane_roll(packed, 8 * b - start)
        if half:
            moved = pltpu.roll(moved, 4, 0)
        keep = (lane >= 8 * b) & (lane < 8 * BLOCKS) & (row < 4)
        moved = jnp.where(keep, moved, 0.0)
        turned = jnp.where(lane % 8 < 4, -lane_roll(moved, -4), lane_roll(moved, 4))
        rows.append(moved + pltpu.roll(turned, 4, 0))
    rows.append(jnp.zeros((NZ - 8 * BLOCKS, NZ), F32))
    upper = jnp.concatenate(rows, axis=0)
    tall = lax.broadcasted_iota(jnp.int32, (NZ, NZ), 0)
    wide = lax.broadcasted_iota(jnp.int32, (NZ, NZ), 1)
    return jnp.where(tall // 8 <= wide // 8, upper, upper.T)


def gram_kernel(peers, own, low, high, from_low, from_high, coef, old, recent, old_image, w_image, out,
                block, first, second, table_re, table_im, diag_re, diag_im):
    fill_tables(coef, table_re, table_im, diag_re, diag_im)
    fill_block(0, (low, own, high), from_low, from_high, block)

    def store(x, y, value):
        w_image[x, pl.ds(y * 8, 8), :] = value

    smooth(block, coef, table_re, table_im, first, second, store)

    def plane(x, total):
        stacked = jnp.concatenate(split3(basis_plane(old, recent, own, old_image, w_image, x)), axis=0)
        return total + lax.dot_general(stacked, stacked, (((1,), (1,)), ((), ())), preferred_element_type=F32)

    total = lax.fori_loop(0, LX, plane, jnp.zeros((3 * ROWS, 3 * ROWS), F32))
    tall = total[0:ROWS] + total[ROWS:2 * ROWS] + total[2 * ROWS:3 * ROWS]
    gram = tall[:, 0:ROWS] + tall[:, ROWS:2 * ROWS] + tall[:, 2 * ROWS:3 * ROWS]
    gram = jnp.concatenate([gram, jnp.zeros((ROWS, NZ - ROWS), F32)], axis=1)
    packed = pack_gram(gram)
    for peer in range(peers):
        out[peer] = packed


def image_and_gram(peers, *args):
    return pl.pallas_call(
        functools.partial(gram_kernel, peers),
        out_shape=(jax.ShapeDtypeStruct((LX, LY * 8, NZ), F32),
                   jax.ShapeDtypeStruct((peers, 8, NZ), F32)),
        in_specs=[VMEM] * 9,
        out_specs=(VMEM, VMEM),
        scratch_shapes=SMOOTH_SCRATCH,
        compiler_params=pltpu.CompilerParams(vmem_limit_bytes=32 << 20),
        name="image_and_gram",
    )(*args)


def sum_kernel(parts, out):
    total = jnp.sum(parts[...], axis=0)
    for peer in range(out.shape[0]):
        out[peer] = total


def sum_and_spread(parts, peers):
    return pl.pallas_call(
        sum_kernel,
        out_shape=jax.ShapeDtypeStruct((peers, 8, NZ), F32),
        in_specs=[VMEM],
        out_specs=VMEM,
        name="sum_and_spread",
    )(parts)


def mul(left, right):
    return lax.dot_general(left, right, (((1,), (0,)), ((), ())), precision=HIGHEST, preferred_element_type=F32)


def mul_t(left, right):
    return lax.dot_general(left, right, (((1,), (1,)), ((), ())), precision=HIGHEST, preferred_element_type=F32)


def inverse_factor(gram):
    lane = lax.broadcasted_iota(jnp.int32, (8, NZ), 1)
    row = lax.broadcasted_iota(jnp.int32, (8, NZ), 0)
    work = jnp.where(lane < 8, gram, jnp.where(lane == row + 8, 1.0, 0.0))
    rank = 2 * (row % 4) + row // 4
    for step in range(8):
        k = (step % 2) * 4 + step // 2
        line = work[k:k + 1, :]
        pivot = line[:, k:k + 1]
        column = work[:, k:k + 1]
        root = 1.0 / jnp.sqrt(pivot)
        line = line * root
        factor = column * root
        work = jnp.where(rank > step, work - factor * line, jnp.where(rank == step, line, work))
    return jnp.where(lane < 8, lane_roll(work, -8), 0.0)


def coefficients(gram):
    lane = lax.broadcasted_iota(jnp.int32, (8, NZ), 1)
    row = lax.broadcasted_iota(jnp.int32, (8, NZ), 0)
    tall = lax.broadcasted_iota(jnp.int32, (NZ, NZ), 0)
    wide = lax.broadcasted_iota(jnp.int32, (NZ, NZ), 1)

    def normalise(rows):
        small = mul_t(mul(rows, gram), rows_in(rows))
        return mul(inverse_factor(small)[:, 0:8], rows)

    def rows_in(rows):
        return jnp.concatenate([rows, jnp.zeros((NZ - 8, NZ), F32)], axis=0)

    once = jnp.where(lane < 24, gram[24:32], 0.0)
    again = jnp.where(lane < 24, mul(once, gram), 0.0)
    fresh = jnp.where(lane == row + 24, 1.0, 0.0)
    new = normalise(fresh - (2.0 * once - again))
    image = (jnp.where((lane >= 32) & (lane < 48), lane_roll(new, 32), 0.0)
             + jnp.where((lane >= 24) & (lane < 32), lane_roll(new, 8), 0.0)
             + jnp.where((lane >= 48) & (lane < 56), lane_roll(new, 24), 0.0))
    window = jnp.where((tall < 16) & (wide == tall + 8), 1.0, 0.0)
    window = jnp.concatenate([window[0:16], new, window[24:]], axis=0)

    def project(rows):
        return mul(mul_t(mul(rows, gram), window), window)

    once = project(image)
    again = project(once)
    newest = normalise(image - (2.0 * once - again))
    return new, newest


def final_kernel(cells, parts, old, recent, w, old_image, w_image, out):
    gram = unpack_gram(jnp.sum(parts[...], axis=0) * (1.0 / cells))
    new, newest = coefficients(gram)
    mapping = jnp.concatenate([new, newest], axis=0)[:, 0:ROWS]
    pieces = [jnp.concatenate([piece] * 3, axis=1) for piece in split3(mapping)]
    stacked_map = jnp.concatenate(pieces, axis=0)

    def plane(x, carry):
        stacked = jnp.concatenate(split3(basis_plane(old, recent, w, old_image, w_image, x)), axis=0)
        full = lax.dot_general(stacked_map, stacked, (((1,), (0,)), ((), ())), preferred_element_type=F32)
        result = full[32:48] + full[16:32] + full[0:16]
        for k in range(2):
            tiles = jnp.stack([result[8 * k:8 * k + 8, y * NZ:(y + 1) * NZ] for y in range(LY)])
            out[k, :, x] = jnp.swapaxes(tiles, 0, 1)
        return carry

    lax.fori_loop(0, LX, plane, 0)


def finish(cells, *args):
    return pl.pallas_call(
        functools.partial(final_kernel, cells),
        out_shape=jax.ShapeDtypeStruct((2, 8, LX, LY, NZ), F32),
        in_specs=[VMEM] * 6,
        out_specs=VMEM,
        compiler_params=pltpu.CompilerParams(vmem_limit_bytes=32 << 20),
        name="finish",
    )(*args)


GX = ("z", "core")


def from_both(axis, count, to_higher, to_lower):
    return (
        lax.ppermute(to_higher, axis, [(i, i + 1) for i in range(count - 1)]),
        lax.ppermute(to_lower, axis, [(i + 1, i) for i in range(count - 1)]),
    )


def per_device(nx, ny, nz, prior, coefficient):
    cells = coefficient.size * nx * ny
    by_cell = prior.transpose(0, 3, 4, 1, 2, 5).reshape(3, LX, LY * 8, NZ)
    recent = by_cell[2]
    old = by_cell[:2].reshape(2 * LX, LY * 8, NZ)

    start = jnp.concatenate([recent, coefficient], axis=1)
    low, high = from_both(GX, nx, start, start)
    up, down = pack_rim(1, True, start, low, high)
    below, above = from_both("gy", ny, up, down)
    w, coef = first_image(start, low, high, below, above)

    old_low, old_high = from_both(GX, nx, old, old)
    up, down = pack_rim(2, False, old, old_low, old_high)
    old_below, old_above = from_both("gy", ny, up, down)

    low, high = from_both(GX, nx, w, w)
    up, down = pack_rim(1, False, w, low, high)
    below, above = from_both("gy", ny, up, down)
    old_image = old_images(old, old_low, old_high, old_below, old_above, coef)

    w_image, spread = image_and_gram(2 * ny, w, low, high, below, above, coef, old, recent, old_image)
    got = lax.all_to_all(spread, ("core", "gy"), 0, 0)
    got = lax.all_to_all(sum_and_spread(got, nz), "z", 0, 0)
    out = finish(cells, got, old, recent, w, old_image, w_image)
    return out.reshape(2, 2, 4, LX, LY, NZ)


def solution(mesh):
    nx, ny = mesh.shape["gx"], mesh.shape["gy"]
    fine = Mesh(np.asarray(mesh.devices).reshape(nx // 2, 2, ny), ("z", "core", "gy"))
    in_specs = (P(None, None, None, GX, "gy", None), P(GX, "gy", None))
    out_specs = P(None, None, None, GX, "gy", None)
    return jax.shard_map(
        functools.partial(per_device, nx, ny, nx // 2),
        mesh=fine, in_specs=in_specs, out_specs=out_specs, check_vma=False,
    )
```

```python
import functools

import jax
import jax.numpy as jnp
import numpy as np
from jax import lax
from jax.experimental import pallas as pl
from jax.experimental.pallas import tpu as pltpu
from jax.sharding import Mesh, PartitionSpec as P

LX, LY, NZ = 4, 8, 128
HALO = 4
EX, EY = LX + 2 * HALO, LY + 2 * HALO
WIDTHS = [EX - 2 * d for d in range(1, HALO + 1)]
STARTS = [sum(WIDTHS[:d]) for d in range(HALO)]
RIM = sum(WIDTHS)
BLOCKS = 7
ROWS = 64
F32 = jnp.float32
BF16 = jnp.bfloat16
HIGHEST = lax.Precision.HIGHEST
VMEM = pl.BlockSpec(memory_space=pltpu.VMEM)


def plane_of(parts, index):
    low, own, high = parts
    if index < HALO:
        return low, index
    if index < HALO + LX:
        return own, index - HALO
    return high, index - HALO - LX


def rim_kernel(groups, with_coefficient, *refs):
    own, low, high, up, down = refs[:5]
    for group in range(groups):
        for d in range(1, HALO + 1):
            for i in range(WIDTHS[d - 1]):
                ref, x = plane_of((low, own, high), d + i)
                spot = group * RIM + STARTS[d - 1] + i
                up[spot] = ref[x, pl.ds((group * LY + LY - d) * 8, 8), :]
                down[spot] = ref[x, pl.ds((group * LY + d - 1) * 8, 8), :]
    if with_coefficient:
        base, line = groups * RIM, groups * LY * 8
        up[base + 3] = jnp.zeros((8, NZ), F32)
        down[base + 3] = jnp.zeros((8, NZ), F32)
        for d in range(1, HALO + 1):
            for i in range(WIDTHS[d - 1]):
                ref, x = plane_of((low, own, high), d + i)
                spot = STARTS[d - 1] + i
                tile, row = base + spot // 8, spot % 8
                up[tile, pl.ds(row, 1), :] = ref[x, pl.ds(line + LY - d, 1), :]
                down[tile, pl.ds(row, 1), :] = ref[x, pl.ds(line + d - 1, 1), :]


def pack_rim(groups, with_coefficient, own, low, high):
    shape = jax.ShapeDtypeStruct((groups * RIM + (4 if with_coefficient else 0), 8, NZ), F32)
    return pl.pallas_call(
        functools.partial(rim_kernel, groups, with_coefficient),
        out_shape=(shape, shape),
        in_specs=[VMEM] * 3,
        out_specs=(VMEM, VMEM),
        compiler_params=pltpu.CompilerParams(vmem_limit_bytes=1 << 20),
        name="pack_rim",
    )(own, low, high)


def fill_block(group, parts, from_low, from_high, wide):
    wide[...] = jnp.zeros(wide.shape, F32)
    for index in range(EX):
        ref, x = plane_of(parts, index)
        wide[index, HALO:HALO + LY] = ref[x, pl.ds(group * LY * 8, LY * 8), :].reshape(LY, 8, NZ)
    for d in range(1, HALO + 1):
        spot = group * RIM + STARTS[d - 1]
        for i in range(WIDTHS[d - 1]):
            wide[d + i, HALO - d] = from_low[spot + i]
            wide[d + i, HALO + LY - 1 + d] = from_high[spot + i]


def fill_coefficient(groups, parts, from_low, from_high, wide):
    wide[...] = jnp.zeros(wide.shape, F32)
    for index in range(EX):
        ref, x = plane_of(parts, index)
        wide[index, HALO:HALO + LY] = ref[x, pl.ds(groups * LY * 8, LY), :]
    for d in range(1, HALO + 1):
        for i in range(WIDTHS[d - 1]):
            spot = STARTS[d - 1] + i
            tile, row = groups * RIM + spot // 8, spot % 8
            wide[d + i, pl.ds(HALO - d, 1), :] = from_low[tile, pl.ds(row, 1), :]
            wide[d + i, pl.ds(HALO + LY - 1 + d, 1), :] = from_high[tile, pl.ds(row, 1), :]


def fill_tables(coef, table_re, table_im, diag_re, diag_im):
    value = coef[...]
    real = 6.0 - value
    imag = 0.5 * value
    scale = jnp.where(value > 0.0, 0.8 / (real * real + imag * imag), 0.0)
    diag_re[...] = real * scale
    diag_im[...] = imag * scale
    sign = jnp.where(lax.broadcasted_iota(jnp.int32, (8, NZ), 0) < 4, 1.0, -1.0)

    def body(x, carry):
        for y in range(EY):
            table_re[x, y] = jnp.broadcast_to(diag_re[x, pl.ds(y, 1), :], (8, NZ))
            table_im[x, y] = jnp.broadcast_to(diag_im[x, pl.ds(y, 1), :], (8, NZ)) * sign
        return carry

    lax.fori_loop(0, EX, body, 0)


def depth_sum(value):
    lane = lax.broadcasted_iota(jnp.int32, value.shape, 2)
    above = jnp.where(lane == 0, 0.0, pltpu.roll(value, 1, 2))
    below = jnp.where(lane == NZ - 1, 0.0, pltpu.roll(value, NZ - 1, 2))
    return above + below


def around(ref, x, low, high):
    total = ref[x - 1, low:high] + ref[x + 1, low:high]
    total = total + ref[x, low - 1:high - 1] + ref[x, low + 1:high + 1]
    return total + depth_sum(ref[x, low:high])


def smooth(block, coef, table_re, table_im, first, second, store):
    def solve(value, x, low, high):
        return (table_re[x, low:high] * value
                + table_im[x, low:high] * pltpu.roll(value, 4, 1))

    def start(x, carry):
        first[x] = solve(block[x], x, 0, EY)
        return carry

    lax.fori_loop(0, EX, start, 0)
    here, there = first, second
    for k in range(1, HALO):
        low, high = k, EY - k

        def sweep(x, carry, here=here, there=there, low=low, high=high):
            value = block[x, low:high] + around(here, x, low, high)
            there[x, low:high] = 0.2 * here[x, low:high] + solve(value, x, low, high)
            return carry

        lax.fori_loop(k, EX - k, sweep, 0)
        here, there = there, here

    def image(x, carry):
        low, high = HALO, HALO + LY
        for y in range(low, high):
            diag = 6.0 - coef[x, pl.ds(y, 1), :]
            total = here[x - 1, y] + here[x + 1, y] + here[x, y - 1] + here[x, y + 1]
            total = total + depth_sum(here[x, y:y + 1])[0]
            store(x - HALO, y - HALO, diag * here[x, y] - total)
        return carry

    lax.fori_loop(HALO, HALO + LX, image, 0)


BIG = pltpu.VMEM((EX, EY, 8, NZ), F32)
FLAT = pltpu.VMEM((EX, EY, NZ), F32)
SMOOTH_SCRATCH = [BIG, BIG, BIG, BIG, BIG, FLAT, FLAT]


def first_kernel(own, low, high, from_low, from_high, out, coef, block, first, second,
                 table_re, table_im, diag_re, diag_im):
    parts = (low, own, high)
    fill_block(2, parts, from_low, from_high, block)
    fill_coefficient(3, parts, from_low, from_high, coef)
    fill_tables(coef, table_re, table_im, diag_re, diag_im)

    def store(x, y, value):
        out[x, pl.ds(y * 8, 8), :] = value

    smooth(block, coef, table_re, table_im, first, second, store)


def first_image(*args):
    return pl.pallas_call(
        first_kernel,
        out_shape=(jax.ShapeDtypeStruct((LX, LY * 8, NZ), F32),
                   jax.ShapeDtypeStruct((EX, EY, NZ), F32)),
        in_specs=[VMEM] * 5,
        out_specs=(VMEM, VMEM),
        scratch_shapes=SMOOTH_SCRATCH,
        compiler_params=pltpu.CompilerParams(vmem_limit_bytes=24 << 20),
        cost_estimate=pl.CostEstimate(flops=6_000_000, bytes_accessed=2_000_000, transcendentals=0),
        name="first_image",
    )(*args)


def old_kernel(group, own, low, high, from_low, from_high, coef, out, block, first, second,
               table_re, table_im, diag_re, diag_im):
    fill_tables(coef, table_re, table_im, diag_re, diag_im)
    fill_block(group, (low, own, high), from_low, from_high, block)

    def store(x, y, value):
        out[x, pl.ds(y * 8, 8), :] = value

    smooth(block, coef, table_re, table_im, first, second, store)


def old_image(group, *args):
    return pl.pallas_call(
        functools.partial(old_kernel, group),
        out_shape=jax.ShapeDtypeStruct((LX, LY * 8, NZ), F32),
        in_specs=[VMEM] * 6,
        out_specs=VMEM,
        scratch_shapes=SMOOTH_SCRATCH,
        compiler_params=pltpu.CompilerParams(vmem_limit_bytes=24 << 20),
        cost_estimate=pl.CostEstimate(flops=6_000_000, bytes_accessed=12_000_000, transcendentals=0),
        name="old_image",
    )(*args)


def split3(value):
    high = value.astype(BF16)
    rest = value - high.astype(F32)
    middle = rest.astype(BF16)
    low = (rest - middle.astype(F32)).astype(BF16)
    return high, middle, low


def basis_plane(start, w, image0, image1, w_image, x):
    refs = [(start, 0), (start, LY), (start, 2 * LY), (w, 0), (image0, 0), (image1, 0), (w_image, 0)]
    rows = []
    for ref, first in refs:
        rows.append(jnp.concatenate([ref[x, pl.ds((first + y) * 8, 8), :] for y in range(LY)], axis=1))
    rows.append(jnp.zeros((8, LY * NZ), F32))
    return jnp.concatenate(rows, axis=0)


def lane_roll(value, amount):
    return pltpu.roll(value, amount % NZ, 1)


SLOTS = [(0, 0), (0, 56), (1, 0), (1, 40), (1, 72), (1, 96), (0, 104)]


def pack_gram(gram):
    lane = lax.broadcasted_iota(jnp.int32, (8, NZ), 1)
    row = lax.broadcasted_iota(jnp.int32, (8, NZ), 0)
    packed = jnp.zeros((8, NZ), F32)
    for b in range(BLOCKS):
        rows = gram[8 * b:8 * b + 8]
        turned = jnp.where(lane % 8 < 4, lane_roll(rows, -4), -lane_roll(rows, 4))
        both = rows + pltpu.roll(turned, 4, 0)
        half, start = SLOTS[b]
        moved = lane_roll(both, start - 8 * b)
        if half:
            moved = pltpu.roll(moved, 4, 0)
        keep = (lane >= start) & (lane < start + 8 * (BLOCKS - b)) & (row // 4 == half)
        packed = packed + jnp.where(keep, moved, 0.0)
    return packed


def unpack_gram(packed):
    lane = lax.broadcasted_iota(jnp.int32, (8, NZ), 1)
    row = lax.broadcasted_iota(jnp.int32, (8, NZ), 0)
    rows = []
    for b in range(BLOCKS):
        half, start = SLOTS[b]
        moved = lane_roll(packed, 8 * b - start)
        if half:
            moved = pltpu.roll(moved, 4, 0)
        keep = (lane >= 8 * b) & (lane < 8 * BLOCKS) & (row < 4)
        moved = jnp.where(keep, moved, 0.0)
        turned = jnp.where(lane % 8 < 4, -lane_roll(moved, -4), lane_roll(moved, 4))
        rows.append(moved + pltpu.roll(turned, 4, 0))
    rows.append(jnp.zeros((NZ - 8 * BLOCKS, NZ), F32))
    upper = jnp.concatenate(rows, axis=0)
    tall = lax.broadcasted_iota(jnp.int32, (NZ, NZ), 0)
    wide = lax.broadcasted_iota(jnp.int32, (NZ, NZ), 1)
    return jnp.where(tall // 8 <= wide // 8, upper, upper.T)


def gram_kernel(peers, own, low, high, from_low, from_high, coef, start, image0, image1, w_image, out,
                block, first, second, table_re, table_im, diag_re, diag_im):
    fill_tables(coef, table_re, table_im, diag_re, diag_im)
    fill_block(0, (low, own, high), from_low, from_high, block)

    def store(x, y, value):
        w_image[x, pl.ds(y * 8, 8), :] = value

    smooth(block, coef, table_re, table_im, first, second, store)

    def plane(x, total):
        stacked = jnp.concatenate(split3(basis_plane(start, own, image0, image1, w_image, x)), axis=0)
        return total + lax.dot_general(stacked, stacked, (((1,), (1,)), ((), ())), preferred_element_type=F32)

    total = lax.fori_loop(0, LX, plane, jnp.zeros((3 * ROWS, 3 * ROWS), F32))
    tall = total[0:ROWS] + total[ROWS:2 * ROWS] + total[2 * ROWS:3 * ROWS]
    gram = tall[:, 0:ROWS] + tall[:, ROWS:2 * ROWS] + tall[:, 2 * ROWS:3 * ROWS]
    gram = jnp.concatenate([gram, jnp.zeros((ROWS, NZ - ROWS), F32)], axis=1)
    packed = pack_gram(gram)
    for peer in range(peers):
        out[peer] = packed


def image_and_gram(peers, *args):
    return pl.pallas_call(
        functools.partial(gram_kernel, peers),
        out_shape=(jax.ShapeDtypeStruct((LX, LY * 8, NZ), F32),
                   jax.ShapeDtypeStruct((peers, 8, NZ), F32)),
        in_specs=[VMEM] * 9,
        out_specs=(VMEM, VMEM),
        scratch_shapes=SMOOTH_SCRATCH,
        compiler_params=pltpu.CompilerParams(vmem_limit_bytes=32 << 20),
        name="image_and_gram",
    )(*args)


def sum_kernel(parts, out):
    total = jnp.sum(parts[...], axis=0)
    for peer in range(out.shape[0]):
        out[peer] = total


def sum_and_spread(parts, peers):
    return pl.pallas_call(
        sum_kernel,
        out_shape=jax.ShapeDtypeStruct((peers, 8, NZ), F32),
        in_specs=[VMEM],
        out_specs=VMEM,
        compiler_params=pltpu.CompilerParams(vmem_limit_bytes=1 << 20),
        name="sum_and_spread",
    )(parts)


def mul(left, right):
    return lax.dot_general(left, right, (((1,), (0,)), ((), ())), precision=HIGHEST, preferred_element_type=F32)


def mul_t(left, right):
    return lax.dot_general(left, right, (((1,), (1,)), ((), ())), precision=HIGHEST, preferred_element_type=F32)


def inverse_factor(gram):
    lane = lax.broadcasted_iota(jnp.int32, (8, NZ), 1)
    row = lax.broadcasted_iota(jnp.int32, (8, NZ), 0)
    work = jnp.where(lane < 8, gram, jnp.where(lane == row + 8, 1.0, 0.0))
    rank = 2 * (row % 4) + row // 4
    for step in range(8):
        k = (step % 2) * 4 + step // 2
        line = work[k:k + 1, :]
        pivot = line[:, k:k + 1]
        column = work[:, k:k + 1]
        root = 1.0 / jnp.sqrt(pivot)
        line = line * root
        factor = column * root
        work = jnp.where(rank > step, work - factor * line, jnp.where(rank == step, line, work))
    return jnp.where(lane < 8, lane_roll(work, -8), 0.0)


def coefficients(gram):
    lane = lax.broadcasted_iota(jnp.int32, (8, NZ), 1)
    row = lax.broadcasted_iota(jnp.int32, (8, NZ), 0)
    tall = lax.broadcasted_iota(jnp.int32, (NZ, NZ), 0)
    wide = lax.broadcasted_iota(jnp.int32, (NZ, NZ), 1)

    def normalise(rows):
        small = mul_t(mul(rows, gram), rows_in(rows))
        return mul(inverse_factor(small)[:, 0:8], rows)

    def rows_in(rows):
        return jnp.concatenate([rows, jnp.zeros((NZ - 8, NZ), F32)], axis=0)

    once = jnp.where(lane < 24, gram[24:32], 0.0)
    again = jnp.where(lane < 24, mul(once, gram), 0.0)
    fresh = jnp.where(lane == row + 24, 1.0, 0.0)
    new = normalise(fresh - (2.0 * once - again))
    image = (jnp.where((lane >= 32) & (lane < 48), lane_roll(new, 32), 0.0)
             + jnp.where((lane >= 24) & (lane < 32), lane_roll(new, 8), 0.0)
             + jnp.where((lane >= 48) & (lane < 56), lane_roll(new, 24), 0.0))
    window = jnp.where((tall < 16) & (wide == tall + 8), 1.0, 0.0)
    window = jnp.concatenate([window[0:16], new, window[24:]], axis=0)

    def project(rows):
        return mul(mul_t(mul(rows, gram), window), window)

    once = project(image)
    again = project(once)
    newest = normalise(image - (2.0 * once - again))
    return new, newest


def final_kernel(cells, parts, start, w, image0, image1, w_image, out):
    gram = unpack_gram(jnp.sum(parts[...], axis=0) * (1.0 / cells))
    new, newest = coefficients(gram)
    mapping = jnp.concatenate([new, newest], axis=0)[:, 0:ROWS]
    pieces = [jnp.concatenate([piece] * 3, axis=1) for piece in split3(mapping)]
    stacked_map = jnp.concatenate(pieces, axis=0)

    def plane(x, carry):
        stacked = jnp.concatenate(split3(basis_plane(start, w, image0, image1, w_image, x)), axis=0)
        full = lax.dot_general(stacked_map, stacked, (((1,), (0,)), ((), ())), preferred_element_type=F32)
        result = full[32:48] + full[16:32] + full[0:16]
        for k in range(2):
            tiles = jnp.stack([result[8 * k:8 * k + 8, y * NZ:(y + 1) * NZ] for y in range(LY)])
            out[k, :, x] = jnp.swapaxes(tiles, 0, 1)
        return carry

    lax.fori_loop(0, LX, plane, 0)


def finish(cells, *args):
    return pl.pallas_call(
        functools.partial(final_kernel, cells),
        out_shape=jax.ShapeDtypeStruct((2, 8, LX, LY, NZ), F32),
        in_specs=[VMEM] * 6,
        out_specs=VMEM,
        compiler_params=pltpu.CompilerParams(vmem_limit_bytes=32 << 20),
        name="finish",
    )(*args)


GX = ("z", "core")


def from_both(axis, count, to_higher, to_lower):
    return (
        lax.ppermute(to_higher, axis, [(i, i + 1) for i in range(count - 1)]),
        lax.ppermute(to_lower, axis, [(i + 1, i) for i in range(count - 1)]),
    )


def per_device(nx, ny, nz, prior, coefficient):
    cells = coefficient.size * nx * ny
    by_cell = prior.transpose(3, 0, 4, 1, 2, 5).reshape(LX, 3 * LY * 8, NZ)
    start = jnp.concatenate([by_cell, coefficient], axis=1)
    sides = from_both(GX, nx, start, start)
    up, down = pack_rim(3, True, start, *sides)
    rims = from_both("gy", ny, up, down)
    w, coef = first_image(start, *sides, *rims)

    w_sides = from_both(GX, nx, w, w)
    up, down = pack_rim(1, False, w, *w_sides)
    w_rims = from_both("gy", ny, up, down)
    image0 = old_image(0, start, *sides, *rims, coef)
    image1 = old_image(1, start, *sides, *rims, coef)

    w_image, spread = image_and_gram(2 * ny, w, *w_sides, *w_rims, coef, start, image0, image1)
    got = lax.all_to_all(spread, ("core", "gy"), 0, 0)
    got = lax.all_to_all(sum_and_spread(got, nz), "z", 0, 0)
    out = finish(cells, got, start, w, image0, image1, w_image)
    return out.reshape(2, 2, 4, LX, LY, NZ)


def solution(mesh):
    nx, ny = mesh.shape["gx"], mesh.shape["gy"]
    fine = Mesh(np.asarray(mesh.devices).reshape(nx // 2, 2, ny), ("z", "core", "gy"))
    in_specs = (P(None, None, None, GX, "gy", None), P(GX, "gy", None))
    out_specs = P(None, None, None, GX, "gy", None)
    return jax.shard_map(
        functools.partial(per_device, nx, ny, nx // 2),
        mesh=fine, in_specs=in_specs, out_specs=out_specs, check_vma=False,
    )
```

```python
import functools

import jax
import jax.numpy as jnp
import numpy as np
from jax import lax
from jax.experimental import pallas as pl
from jax.experimental.pallas import tpu as pltpu
from jax.sharding import Mesh, PartitionSpec as P

LX, LY, NZ = 4, 8, 128
HALO = 4
EX, EY = LX + 2 * HALO, LY + 2 * HALO
WIDTHS = [EX - 2 * d for d in range(1, HALO + 1)]
STARTS = [sum(WIDTHS[:d]) for d in range(HALO)]
RIM = sum(WIDTHS)
BLOCKS = 7
ROWS = 64
F32 = jnp.float32
BF16 = jnp.bfloat16
HIGHEST = lax.Precision.HIGHEST
VMEM = pl.BlockSpec(memory_space=pltpu.VMEM)


def plane_of(parts, index):
    low, own, high = parts
    if index < HALO:
        return low, index
    if index < HALO + LX:
        return own, index - HALO
    return high, index - HALO - LX


def rim_kernel(groups, with_coefficient, own, low, high, up, down):
    for group in range(groups):
        for d in range(1, HALO + 1):
            for i in range(WIDTHS[d - 1]):
                ref, x = plane_of((low, own, high), d + i)
                spot = group * RIM + STARTS[d - 1] + i
                up[spot] = ref[x, pl.ds((group * LY + LY - d) * 8, 8), :]
                down[spot] = ref[x, pl.ds((group * LY + d - 1) * 8, 8), :]
    if with_coefficient:
        base, line = groups * RIM, groups * LY * 8
        up[base + 3] = jnp.zeros((8, NZ), F32)
        down[base + 3] = jnp.zeros((8, NZ), F32)
        for d in range(1, HALO + 1):
            for i in range(WIDTHS[d - 1]):
                ref, x = plane_of((low, own, high), d + i)
                spot = STARTS[d - 1] + i
                tile, row = base + spot // 8, spot % 8
                up[tile, pl.ds(row, 1), :] = ref[x, pl.ds(line + LY - d, 1), :]
                down[tile, pl.ds(row, 1), :] = ref[x, pl.ds(line + d - 1, 1), :]


def pack_rim(groups, with_coefficient, own, sides):
    shape = jax.ShapeDtypeStruct((groups * RIM + (4 if with_coefficient else 0), 8, NZ), F32)
    return pl.pallas_call(
        functools.partial(rim_kernel, groups, with_coefficient),
        out_shape=(shape, shape),
        in_specs=[VMEM] * 3,
        out_specs=(VMEM, VMEM),
        compiler_params=pltpu.CompilerParams(vmem_limit_bytes=1 << 20),
        name="pack_rim",
    )(own, *sides)


def turn_kernel(prior, after, old):
    del after
    for k in range(2):
        for x in range(LX):
            fields = prior[k, :, :, x].reshape(8, LY, NZ)
            old[x, pl.ds(k * LY * 8, LY * 8), :] = jnp.swapaxes(fields, 0, 1).reshape(LY * 8, NZ)


def turn_old(prior, after):
    return pl.pallas_call(
        turn_kernel,
        out_shape=jax.ShapeDtypeStruct((LX, 2 * LY * 8, NZ), F32),
        in_specs=[VMEM, pl.BlockSpec(memory_space=pl.ANY)],
        out_specs=VMEM,
        compiler_params=pltpu.CompilerParams(vmem_limit_bytes=1 << 20),
        cost_estimate=pl.CostEstimate(flops=6_000_000, bytes_accessed=12_000_000, transcendentals=0),
        name="turn_old",
    )(prior, after)


def fill_block(group, parts, from_low, from_high, wide):
    wide[...] = jnp.zeros(wide.shape, F32)
    for index in range(EX):
        ref, x = plane_of(parts, index)
        wide[index, HALO:HALO + LY] = ref[x, pl.ds(group * LY * 8, LY * 8), :].reshape(LY, 8, NZ)
    for d in range(1, HALO + 1):
        spot = group * RIM + STARTS[d - 1]
        for i in range(WIDTHS[d - 1]):
            wide[d + i, HALO - d] = from_low[spot + i]
            wide[d + i, HALO + LY - 1 + d] = from_high[spot + i]


def fill_coefficient(groups, parts, from_low, from_high, wide):
    wide[...] = jnp.zeros(wide.shape, F32)
    for index in range(EX):
        ref, x = plane_of(parts, index)
        wide[index, HALO:HALO + LY] = ref[x, pl.ds(groups * LY * 8, LY), :]
    for d in range(1, HALO + 1):
        for i in range(WIDTHS[d - 1]):
            spot = STARTS[d - 1] + i
            tile, row = groups * RIM + spot // 8, spot % 8
            wide[d + i, pl.ds(HALO - d, 1), :] = from_low[tile, pl.ds(row, 1), :]
            wide[d + i, pl.ds(HALO + LY - 1 + d, 1), :] = from_high[tile, pl.ds(row, 1), :]


def fill_tables(coef, table_re, table_im, diag_re, diag_im):
    value = coef[...]
    real = 6.0 - value
    imag = 0.5 * value
    scale = jnp.where(value > 0.0, 0.8 / (real * real + imag * imag), 0.0)
    diag_re[...] = real * scale
    diag_im[...] = imag * scale
    sign = jnp.where(lax.broadcasted_iota(jnp.int32, (8, NZ), 0) < 4, 1.0, -1.0)

    def body(x, carry):
        for y in range(EY):
            table_re[x, y] = jnp.broadcast_to(diag_re[x, pl.ds(y, 1), :], (8, NZ))
            table_im[x, y] = jnp.broadcast_to(diag_im[x, pl.ds(y, 1), :], (8, NZ)) * sign
        return carry

    lax.fori_loop(0, EX, body, 0)


def depth_sum(value):
    lane = lax.broadcasted_iota(jnp.int32, value.shape, 2)
    above = jnp.where(lane == 0, 0.0, pltpu.roll(value, 1, 2))
    below = jnp.where(lane == NZ - 1, 0.0, pltpu.roll(value, NZ - 1, 2))
    return above + below


def around(ref, x, low, high):
    total = ref[x - 1, low:high] + ref[x + 1, low:high]
    total = total + ref[x, low - 1:high - 1] + ref[x, low + 1:high + 1]
    return total + depth_sum(ref[x, low:high])


def smooth(block, coef, table_re, table_im, first, second, store):
    def solve(value, x, low, high):
        return (table_re[x, low:high] * value
                + table_im[x, low:high] * pltpu.roll(value, 4, 1))

    def start(x, carry):
        first[x] = solve(block[x], x, 0, EY)
        return carry

    lax.fori_loop(0, EX, start, 0)
    here, there = first, second
    for k in range(1, HALO):
        low, high = k, EY - k

        def sweep(x, carry, here=here, there=there, low=low, high=high):
            value = block[x, low:high] + around(here, x, low, high)
            there[x, low:high] = 0.2 * here[x, low:high] + solve(value, x, low, high)
            return carry

        lax.fori_loop(k, EX - k, sweep, 0)
        here, there = there, here

    def image(x, carry):
        low, high = HALO, HALO + LY
        for y in range(low, high):
            diag = 6.0 - coef[x, pl.ds(y, 1), :]
            total = here[x - 1, y] + here[x + 1, y] + here[x, y - 1] + here[x, y + 1]
            total = total + depth_sum(here[x, y:y + 1])[0]
            store(x - HALO, y - HALO, diag * here[x, y] - total)
        return carry

    lax.fori_loop(HALO, HALO + LX, image, 0)


BIG = pltpu.VMEM((EX, EY, 8, NZ), F32)
FLAT = pltpu.VMEM((EX, EY, NZ), F32)
SMOOTH_SCRATCH = [BIG, BIG, BIG, BIG, BIG, FLAT, FLAT]


def first_kernel(own, low, high, from_low, from_high, out, coef, block, first, second,
                 table_re, table_im, diag_re, diag_im):
    parts = (low, own, high)
    fill_block(0, parts, from_low, from_high, block)
    fill_coefficient(1, parts, from_low, from_high, coef)
    fill_tables(coef, table_re, table_im, diag_re, diag_im)

    def store(x, y, value):
        out[x, pl.ds(y * 8, 8), :] = value

    smooth(block, coef, table_re, table_im, first, second, store)


def first_image(*args):
    return pl.pallas_call(
        first_kernel,
        out_shape=(jax.ShapeDtypeStruct((LX, LY * 8, NZ), F32),
                   jax.ShapeDtypeStruct((EX, EY, NZ), F32)),
        in_specs=[VMEM] * 5,
        out_specs=(VMEM, VMEM),
        scratch_shapes=SMOOTH_SCRATCH,
        compiler_params=pltpu.CompilerParams(vmem_limit_bytes=24 << 20),
        cost_estimate=pl.CostEstimate(flops=6_000_000, bytes_accessed=2_000_000, transcendentals=0),
        name="first_image",
    )(*args)


def old_kernel(group, own, low, high, from_low, from_high, coef, out, block, first, second,
               table_re, table_im, diag_re, diag_im):
    fill_tables(coef, table_re, table_im, diag_re, diag_im)
    fill_block(group, (low, own, high), from_low, from_high, block)

    def store(x, y, value):
        out[x, pl.ds(y * 8, 8), :] = value

    smooth(block, coef, table_re, table_im, first, second, store)


def old_image(group, *args):
    return pl.pallas_call(
        functools.partial(old_kernel, group),
        out_shape=jax.ShapeDtypeStruct((LX, LY * 8, NZ), F32),
        in_specs=[VMEM] * 6,
        out_specs=VMEM,
        scratch_shapes=SMOOTH_SCRATCH,
        compiler_params=pltpu.CompilerParams(vmem_limit_bytes=24 << 20),
        cost_estimate=pl.CostEstimate(flops=6_000_000, bytes_accessed=12_000_000, transcendentals=0),
        name="old_image",
    )(*args)


def split3(value):
    high = value.astype(BF16)
    rest = value - high.astype(F32)
    middle = rest.astype(BF16)
    low = (rest - middle.astype(F32)).astype(BF16)
    return high, middle, low


def basis_plane(start, old, w, image0, image1, w_image, x):
    refs = [(old, 0), (old, LY), (start, 0), (w, 0), (image0, 0), (image1, 0), (w_image, 0)]
    rows = []
    for ref, first in refs:
        rows.append(jnp.concatenate([ref[x, pl.ds((first + y) * 8, 8), :] for y in range(LY)], axis=1))
    rows.append(jnp.zeros((8, LY * NZ), F32))
    return jnp.concatenate(rows, axis=0)


def lane_roll(value, amount):
    return pltpu.roll(value, amount % NZ, 1)


SLOTS = [(0, 0), (0, 56), (1, 0), (1, 40), (1, 72), (1, 96), (0, 104)]


def pack_gram(gram):
    lane = lax.broadcasted_iota(jnp.int32, (8, NZ), 1)
    row = lax.broadcasted_iota(jnp.int32, (8, NZ), 0)
    packed = jnp.zeros((8, NZ), F32)
    for b in range(BLOCKS):
        rows = gram[8 * b:8 * b + 8]
        turned = jnp.where(lane % 8 < 4, lane_roll(rows, -4), -lane_roll(rows, 4))
        both = rows + pltpu.roll(turned, 4, 0)
        half, start = SLOTS[b]
        moved = lane_roll(both, start - 8 * b)
        if half:
            moved = pltpu.roll(moved, 4, 0)
        keep = (lane >= start) & (lane < start + 8 * (BLOCKS - b)) & (row // 4 == half)
        packed = packed + jnp.where(keep, moved, 0.0)
    return packed


def unpack_gram(packed):
    lane = lax.broadcasted_iota(jnp.int32, (8, NZ), 1)
    row = lax.broadcasted_iota(jnp.int32, (8, NZ), 0)
    rows = []
    for b in range(BLOCKS):
        half, start = SLOTS[b]
        moved = lane_roll(packed, 8 * b - start)
        if half:
            moved = pltpu.roll(moved, 4, 0)
        keep = (lane >= 8 * b) & (lane < 8 * BLOCKS) & (row < 4)
        moved = jnp.where(keep, moved, 0.0)
        turned = jnp.where(lane % 8 < 4, -lane_roll(moved, -4), lane_roll(moved, 4))
        rows.append(moved + pltpu.roll(turned, 4, 0))
    rows.append(jnp.zeros((NZ - 8 * BLOCKS, NZ), F32))
    upper = jnp.concatenate(rows, axis=0)
    tall = lax.broadcasted_iota(jnp.int32, (NZ, NZ), 0)
    wide = lax.broadcasted_iota(jnp.int32, (NZ, NZ), 1)
    return jnp.where(tall // 8 <= wide // 8, upper, upper.T)


def gram_kernel(peers, own, low, high, from_low, from_high, coef, start, old, image0, image1, w_image, out,
                block, first, second, table_re, table_im, diag_re, diag_im):
    fill_tables(coef, table_re, table_im, diag_re, diag_im)
    fill_block(0, (low, own, high), from_low, from_high, block)

    def store(x, y, value):
        w_image[x, pl.ds(y * 8, 8), :] = value

    smooth(block, coef, table_re, table_im, first, second, store)

    def plane(x, total):
        stacked = jnp.concatenate(split3(basis_plane(start, old, own, image0, image1, w_image, x)), axis=0)
        return total + lax.dot_general(stacked, stacked, (((1,), (1,)), ((), ())), preferred_element_type=F32)

    total = lax.fori_loop(0, LX, plane, jnp.zeros((3 * ROWS, 3 * ROWS), F32))
    tall = total[0:ROWS] + total[ROWS:2 * ROWS] + total[2 * ROWS:3 * ROWS]
    gram = tall[:, 0:ROWS] + tall[:, ROWS:2 * ROWS] + tall[:, 2 * ROWS:3 * ROWS]
    gram = jnp.concatenate([gram, jnp.zeros((ROWS, NZ - ROWS), F32)], axis=1)
    packed = pack_gram(gram)
    for peer in range(peers):
        out[peer] = packed


def image_and_gram(peers, *args):
    return pl.pallas_call(
        functools.partial(gram_kernel, peers),
        out_shape=(jax.ShapeDtypeStruct((LX, LY * 8, NZ), F32),
                   jax.ShapeDtypeStruct((peers, 8, NZ), F32)),
        in_specs=[VMEM] * 10,
        out_specs=(VMEM, VMEM),
        scratch_shapes=SMOOTH_SCRATCH,
        compiler_params=pltpu.CompilerParams(vmem_limit_bytes=32 << 20),
        name="image_and_gram",
    )(*args)


def sum_kernel(parts, out):
    total = jnp.sum(parts[...], axis=0)
    for peer in range(out.shape[0]):
        out[peer] = total


def sum_and_spread(parts, peers):
    return pl.pallas_call(
        sum_kernel,
        out_shape=jax.ShapeDtypeStruct((peers, 8, NZ), F32),
        in_specs=[VMEM],
        out_specs=VMEM,
        compiler_params=pltpu.CompilerParams(vmem_limit_bytes=1 << 20),
        name="sum_and_spread",
    )(parts)


def mul(left, right):
    return lax.dot_general(left, right, (((1,), (0,)), ((), ())), precision=HIGHEST, preferred_element_type=F32)


def mul_t(left, right):
    return lax.dot_general(left, right, (((1,), (1,)), ((), ())), precision=HIGHEST, preferred_element_type=F32)


def inverse_factor(gram):
    lane = lax.broadcasted_iota(jnp.int32, (8, NZ), 1)
    row = lax.broadcasted_iota(jnp.int32, (8, NZ), 0)
    work = jnp.where(lane < 8, gram, jnp.where(lane == row + 8, 1.0, 0.0))
    rank = 2 * (row % 4) + row // 4
    for step in range(8):
        k = (step % 2) * 4 + step // 2
        line = work[k:k + 1, :]
        pivot = line[:, k:k + 1]
        column = work[:, k:k + 1]
        root = 1.0 / jnp.sqrt(pivot)
        line = line * root
        factor = column * root
        work = jnp.where(rank > step, work - factor * line, jnp.where(rank == step, line, work))
    return jnp.where(lane < 8, lane_roll(work, -8), 0.0)


def coefficients(gram):
    lane = lax.broadcasted_iota(jnp.int32, (8, NZ), 1)
    row = lax.broadcasted_iota(jnp.int32, (8, NZ), 0)
    tall = lax.broadcasted_iota(jnp.int32, (NZ, NZ), 0)
    wide = lax.broadcasted_iota(jnp.int32, (NZ, NZ), 1)

    def normalise(rows):
        small = mul_t(mul(rows, gram), rows_in(rows))
        return mul(inverse_factor(small)[:, 0:8], rows)

    def rows_in(rows):
        return jnp.concatenate([rows, jnp.zeros((NZ - 8, NZ), F32)], axis=0)

    once = jnp.where(lane < 24, gram[24:32], 0.0)
    again = jnp.where(lane < 24, mul(once, gram), 0.0)
    fresh = jnp.where(lane == row + 24, 1.0, 0.0)
    new = normalise(fresh - (2.0 * once - again))
    image = (jnp.where((lane >= 32) & (lane < 48), lane_roll(new, 32), 0.0)
             + jnp.where((lane >= 24) & (lane < 32), lane_roll(new, 8), 0.0)
             + jnp.where((lane >= 48) & (lane < 56), lane_roll(new, 24), 0.0))
    window = jnp.where((tall < 16) & (wide == tall + 8), 1.0, 0.0)
    window = jnp.concatenate([window[0:16], new, window[24:]], axis=0)

    def project(rows):
        return mul(mul_t(mul(rows, gram), window), window)

    once = project(image)
    again = project(once)
    newest = normalise(image - (2.0 * once - again))
    return new, newest


def final_kernel(cells, parts, start, old, w, image0, image1, w_image, out):
    gram = unpack_gram(jnp.sum(parts[...], axis=0) * (1.0 / cells))
    new, newest = coefficients(gram)
    mapping = jnp.concatenate([new, newest], axis=0)[:, 0:ROWS]
    pieces = [jnp.concatenate([piece] * 3, axis=1) for piece in split3(mapping)]
    stacked_map = jnp.concatenate(pieces, axis=0)

    def plane(x, carry):
        stacked = jnp.concatenate(split3(basis_plane(start, old, w, image0, image1, w_image, x)), axis=0)
        full = lax.dot_general(stacked_map, stacked, (((1,), (0,)), ((), ())), preferred_element_type=F32)
        result = full[32:48] + full[16:32] + full[0:16]
        for k in range(2):
            tiles = jnp.stack([result[8 * k:8 * k + 8, y * NZ:(y + 1) * NZ] for y in range(LY)])
            out[k, :, x] = jnp.swapaxes(tiles, 0, 1)
        return carry

    lax.fori_loop(0, LX, plane, 0)


def finish(cells, *args):
    return pl.pallas_call(
        functools.partial(final_kernel, cells),
        out_shape=jax.ShapeDtypeStruct((2, 8, LX, LY, NZ), F32),
        in_specs=[VMEM] * 7,
        out_specs=VMEM,
        compiler_params=pltpu.CompilerParams(vmem_limit_bytes=32 << 20),
        name="finish",
    )(*args)


GX = ("z", "core")


def from_both(axis, count, to_higher, to_lower):
    return (
        lax.ppermute(to_higher, axis, [(i, i + 1) for i in range(count - 1)]),
        lax.ppermute(to_lower, axis, [(i + 1, i) for i in range(count - 1)]),
    )


def per_device(nx, ny, nz, prior, coefficient):
    cells = coefficient.size * nx * ny
    recent = prior[2].transpose(2, 3, 0, 1, 4).reshape(LX, LY * 8, NZ)
    start = jnp.concatenate([recent, coefficient], axis=1)
    sides = from_both(GX, nx, start, start)
    up, down = pack_rim(1, True, start, sides)
    rims = from_both("gy", ny, up, down)
    old = turn_old(prior, rims[0])
    w, coef = first_image(start, *sides, *rims)

    old_sides = from_both(GX, nx, old, old)
    old_rims = from_both("gy", ny, *pack_rim(2, False, old, old_sides))
    w_sides = from_both(GX, nx, w, w)
    w_rims = from_both("gy", ny, *pack_rim(1, False, w, w_sides))
    image0 = old_image(0, old, *old_sides, *old_rims, coef)
    image1 = old_image(1, old, *old_sides, *old_rims, coef)

    w_image, spread = image_and_gram(2 * ny, w, *w_sides, *w_rims, coef, start, old, image0, image1)
    got = lax.all_to_all(spread, ("core", "gy"), 0, 0)
    got = lax.all_to_all(sum_and_spread(got, nz), "z", 0, 0)
    out = finish(cells, got, start, old, w, image0, image1, w_image)
    return out.reshape(2, 2, 4, LX, LY, NZ)


def solution(mesh):
    nx, ny = mesh.shape["gx"], mesh.shape["gy"]
    fine = Mesh(np.asarray(mesh.devices).reshape(nx // 2, 2, ny), ("z", "core", "gy"))
    in_specs = (P(None, None, None, GX, "gy", None), P(GX, "gy", None))
    out_specs = P(None, None, None, GX, "gy", None)
    return jax.shard_map(
        functools.partial(per_device, nx, ny, nx // 2),
        mesh=fine, in_specs=in_specs, out_specs=out_specs, check_vma=False,
    )
```

```python
import functools

import jax
import jax.numpy as jnp
import numpy as np
from jax import lax
from jax.experimental import pallas as pl
from jax.experimental.pallas import tpu as pltpu
from jax.sharding import Mesh, PartitionSpec as P

LX, LY, NZ = 4, 8, 128
HALO = 4
EX, EY = LX + 2 * HALO, LY + 2 * HALO
WIDTHS = [EX - 2 * d for d in range(1, HALO + 1)]
STARTS = [sum(WIDTHS[:d]) for d in range(HALO)]
RIM = sum(WIDTHS)
BLOCKS = 7
ROWS = 64
F32 = jnp.float32
BF16 = jnp.bfloat16
HIGHEST = lax.Precision.HIGHEST
VMEM = pl.BlockSpec(memory_space=pltpu.VMEM)


def plane_of(parts, index):
    low, own, high = parts
    if index < HALO:
        return low, index
    if index < HALO + LX:
        return own, index - HALO
    return high, index - HALO - LX


def fill_rim(parts, group, up, down, slot):
    for d in range(1, HALO + 1):
        for i in range(WIDTHS[d - 1]):
            ref, x = plane_of(parts, d + i)
            spot = slot * RIM + STARTS[d - 1] + i
            up[spot] = ref[x, pl.ds((group * LY + LY - d) * 8, 8), :]
            down[spot] = ref[x, pl.ds((group * LY + d - 1) * 8, 8), :]


def first_rim_kernel(own, low, high, up, down, old_up, old_down):
    parts = (low, own, high)
    fill_rim(parts, 2, up, down, 0)
    line = 3 * LY * 8
    up[RIM + 3] = jnp.zeros((8, NZ), F32)
    down[RIM + 3] = jnp.zeros((8, NZ), F32)
    for d in range(1, HALO + 1):
        for i in range(WIDTHS[d - 1]):
            ref, x = plane_of(parts, d + i)
            spot = STARTS[d - 1] + i
            tile, row = RIM + spot // 8, spot % 8
            up[tile, pl.ds(row, 1), :] = ref[x, pl.ds(line + LY - d, 1), :]
            down[tile, pl.ds(row, 1), :] = ref[x, pl.ds(line + d - 1, 1), :]
    fill_rim(parts, 0, old_up, old_down, 0)
    fill_rim(parts, 1, old_up, old_down, 1)


def rim_kernel(own, low, high, up, down):
    fill_rim((low, own, high), 0, up, down, 0)


def pack_rim(kernel, sizes, own, sides):
    shapes = tuple(jax.ShapeDtypeStruct((size, 8, NZ), F32) for size in sizes)
    return pl.pallas_call(
        kernel,
        out_shape=shapes,
        in_specs=[VMEM] * 3,
        out_specs=(VMEM,) * len(shapes),
        compiler_params=pltpu.CompilerParams(vmem_limit_bytes=1 << 20),
        name="pack_rim",
    )(own, *sides)


def fill_block(group, slot, parts, from_low, from_high, wide):
    wide[...] = jnp.zeros(wide.shape, F32)
    for index in range(EX):
        ref, x = plane_of(parts, index)
        wide[index, HALO:HALO + LY] = ref[x, pl.ds(group * LY * 8, LY * 8), :].reshape(LY, 8, NZ)
    for d in range(1, HALO + 1):
        spot = slot * RIM + STARTS[d - 1]
        for i in range(WIDTHS[d - 1]):
            wide[d + i, HALO - d] = from_low[spot + i]
            wide[d + i, HALO + LY - 1 + d] = from_high[spot + i]


def fill_coefficient(groups, parts, from_low, from_high, wide):
    wide[...] = jnp.zeros(wide.shape, F32)
    for index in range(EX):
        ref, x = plane_of(parts, index)
        wide[index, HALO:HALO + LY] = ref[x, pl.ds(groups * LY * 8, LY), :]
    for d in range(1, HALO + 1):
        for i in range(WIDTHS[d - 1]):
            spot = STARTS[d - 1] + i
            tile, row = RIM + spot // 8, spot % 8
            wide[d + i, pl.ds(HALO - d, 1), :] = from_low[tile, pl.ds(row, 1), :]
            wide[d + i, pl.ds(HALO + LY - 1 + d, 1), :] = from_high[tile, pl.ds(row, 1), :]


def fill_tables(coef, table_re, table_im, diag_re, diag_im):
    value = coef[...]
    real = 6.0 - value
    imag = 0.5 * value
    scale = jnp.where(value > 0.0, 0.8 / (real * real + imag * imag), 0.0)
    diag_re[...] = real * scale
    diag_im[...] = imag * scale
    sign = jnp.where(lax.broadcasted_iota(jnp.int32, (8, NZ), 0) < 4, 1.0, -1.0)

    def body(x, carry):
        for y in range(EY):
            table_re[x, y] = jnp.broadcast_to(diag_re[x, pl.ds(y, 1), :], (8, NZ))
            table_im[x, y] = jnp.broadcast_to(diag_im[x, pl.ds(y, 1), :], (8, NZ)) * sign
        return carry

    lax.fori_loop(0, EX, body, 0)


def depth_sum(value):
    lane = lax.broadcasted_iota(jnp.int32, value.shape, 2)
    above = jnp.where(lane == 0, 0.0, pltpu.roll(value, 1, 2))
    below = jnp.where(lane == NZ - 1, 0.0, pltpu.roll(value, NZ - 1, 2))
    return above + below


def around(ref, x, low, high):
    total = ref[x - 1, low:high] + ref[x + 1, low:high]
    total = total + ref[x, low - 1:high - 1] + ref[x, low + 1:high + 1]
    return total + depth_sum(ref[x, low:high])


def smooth(block, coef, table_re, table_im, first, second, store):
    def solve(value, x, low, high):
        return (table_re[x, low:high] * value
                + table_im[x, low:high] * pltpu.roll(value, 4, 1))

    def start(x, carry):
        first[x] = solve(block[x], x, 0, EY)
        return carry

    lax.fori_loop(0, EX, start, 0)
    here, there = first, second
    for k in range(1, HALO):
        low, high = k, EY - k

        def sweep(x, carry, here=here, there=there, low=low, high=high):
            value = block[x, low:high] + around(here, x, low, high)
            there[x, low:high] = 0.2 * here[x, low:high] + solve(value, x, low, high)
            return carry

        lax.fori_loop(k, EX - k, sweep, 0)
        here, there = there, here

    def image(x, carry):
        low, high = HALO, HALO + LY
        for y in range(low, high):
            diag = 6.0 - coef[x, pl.ds(y, 1), :]
            total = here[x - 1, y] + here[x + 1, y] + here[x, y - 1] + here[x, y + 1]
            total = total + depth_sum(here[x, y:y + 1])[0]
            store(x - HALO, y - HALO, diag * here[x, y] - total)
        return carry

    lax.fori_loop(HALO, HALO + LX, image, 0)


BIG = pltpu.VMEM((EX, EY, 8, NZ), F32)
FLAT = pltpu.VMEM((EX, EY, NZ), F32)
SMOOTH_SCRATCH = [BIG, BIG, BIG, BIG, BIG, FLAT, FLAT]


def first_kernel(own, low, high, from_low, from_high, out, coef, block, first, second,
                 table_re, table_im, diag_re, diag_im):
    parts = (low, own, high)
    fill_block(2, 0, parts, from_low, from_high, block)
    fill_coefficient(3, parts, from_low, from_high, coef)
    fill_tables(coef, table_re, table_im, diag_re, diag_im)

    def store(x, y, value):
        out[x, pl.ds(y * 8, 8), :] = value

    smooth(block, coef, table_re, table_im, first, second, store)


def first_image(*args):
    return pl.pallas_call(
        first_kernel,
        out_shape=(jax.ShapeDtypeStruct((LX, LY * 8, NZ), F32),
                   jax.ShapeDtypeStruct((EX, EY, NZ), F32)),
        in_specs=[VMEM] * 5,
        out_specs=(VMEM, VMEM),
        scratch_shapes=SMOOTH_SCRATCH,
        compiler_params=pltpu.CompilerParams(vmem_limit_bytes=24 << 20),
        cost_estimate=pl.CostEstimate(flops=6_000_000, bytes_accessed=2_000_000, transcendentals=0),
        name="first_image",
    )(*args)


def old_kernel(group, own, low, high, from_low, from_high, coef, out, block, first, second,
               table_re, table_im, diag_re, diag_im):
    fill_tables(coef, table_re, table_im, diag_re, diag_im)
    fill_block(group, group, (low, own, high), from_low, from_high, block)

    def store(x, y, value):
        out[x, pl.ds(y * 8, 8), :] = value

    smooth(block, coef, table_re, table_im, first, second, store)


def old_image(group, *args):
    return pl.pallas_call(
        functools.partial(old_kernel, group),
        out_shape=jax.ShapeDtypeStruct((LX, LY * 8, NZ), F32),
        in_specs=[VMEM] * 6,
        out_specs=VMEM,
        scratch_shapes=SMOOTH_SCRATCH,
        compiler_params=pltpu.CompilerParams(vmem_limit_bytes=24 << 20),
        cost_estimate=pl.CostEstimate(flops=6_000_000, bytes_accessed=12_000_000, transcendentals=0),
        name="old_image",
    )(*args)


def split3(value):
    high = value.astype(BF16)
    rest = value - high.astype(F32)
    middle = rest.astype(BF16)
    low = (rest - middle.astype(F32)).astype(BF16)
    return high, middle, low


def basis_plane(start, w, image0, image1, w_image, x):
    refs = [(start, 0), (start, LY), (start, 2 * LY), (w, 0), (image0, 0), (image1, 0), (w_image, 0)]
    rows = []
    for ref, first in refs:
        rows.append(jnp.concatenate([ref[x, pl.ds((first + y) * 8, 8), :] for y in range(LY)], axis=1))
    rows.append(jnp.zeros((8, LY * NZ), F32))
    return jnp.concatenate(rows, axis=0)


def lane_roll(value, amount):
    return pltpu.roll(value, amount % NZ, 1)


SLOTS = [(0, 0), (0, 56), (1, 0), (1, 40), (1, 72), (1, 96), (0, 104)]


def pack_gram(gram):
    lane = lax.broadcasted_iota(jnp.int32, (8, NZ), 1)
    row = lax.broadcasted_iota(jnp.int32, (8, NZ), 0)
    packed = jnp.zeros((8, NZ), F32)
    for b in range(BLOCKS):
        rows = gram[8 * b:8 * b + 8]
        turned = jnp.where(lane % 8 < 4, lane_roll(rows, -4), -lane_roll(rows, 4))
        both = rows + pltpu.roll(turned, 4, 0)
        half, start = SLOTS[b]
        moved = lane_roll(both, start - 8 * b)
        if half:
            moved = pltpu.roll(moved, 4, 0)
        keep = (lane >= start) & (lane < start + 8 * (BLOCKS - b)) & (row // 4 == half)
        packed = packed + jnp.where(keep, moved, 0.0)
    return packed


def unpack_gram(packed):
    lane = lax.broadcasted_iota(jnp.int32, (8, NZ), 1)
    row = lax.broadcasted_iota(jnp.int32, (8, NZ), 0)
    rows = []
    for b in range(BLOCKS):
        half, start = SLOTS[b]
        moved = lane_roll(packed, 8 * b - start)
        if half:
            moved = pltpu.roll(moved, 4, 0)
        keep = (lane >= 8 * b) & (lane < 8 * BLOCKS) & (row < 4)
        moved = jnp.where(keep, moved, 0.0)
        turned = jnp.where(lane % 8 < 4, -lane_roll(moved, -4), lane_roll(moved, 4))
        rows.append(moved + pltpu.roll(turned, 4, 0))
    rows.append(jnp.zeros((NZ - 8 * BLOCKS, NZ), F32))
    upper = jnp.concatenate(rows, axis=0)
    tall = lax.broadcasted_iota(jnp.int32, (NZ, NZ), 0)
    wide = lax.broadcasted_iota(jnp.int32, (NZ, NZ), 1)
    return jnp.where(tall // 8 <= wide // 8, upper, upper.T)


def gram_kernel(peers, own, low, high, from_low, from_high, coef, start, image0, image1, w_image, out,
                block, first, second, table_re, table_im, diag_re, diag_im):
    fill_tables(coef, table_re, table_im, diag_re, diag_im)
    fill_block(0, 0, (low, own, high), from_low, from_high, block)

    def store(x, y, value):
        w_image[x, pl.ds(y * 8, 8), :] = value

    smooth(block, coef, table_re, table_im, first, second, store)

    def plane(x, total):
        stacked = jnp.concatenate(split3(basis_plane(start, own, image0, image1, w_image, x)), axis=0)
        return total + lax.dot_general(stacked, stacked, (((1,), (1,)), ((), ())), preferred_element_type=F32)

    total = lax.fori_loop(0, LX, plane, jnp.zeros((3 * ROWS, 3 * ROWS), F32))
    tall = total[0:ROWS] + total[ROWS:2 * ROWS] + total[2 * ROWS:3 * ROWS]
    gram = tall[:, 0:ROWS] + tall[:, ROWS:2 * ROWS] + tall[:, 2 * ROWS:3 * ROWS]
    gram = jnp.concatenate([gram, jnp.zeros((ROWS, NZ - ROWS), F32)], axis=1)
    packed = pack_gram(gram)
    for peer in range(peers):
        out[peer] = packed


def image_and_gram(peers, *args):
    return pl.pallas_call(
        functools.partial(gram_kernel, peers),
        out_shape=(jax.ShapeDtypeStruct((LX, LY * 8, NZ), F32),
                   jax.ShapeDtypeStruct((peers, 8, NZ), F32)),
        in_specs=[VMEM] * 9,
        out_specs=(VMEM, VMEM),
        scratch_shapes=SMOOTH_SCRATCH,
        compiler_params=pltpu.CompilerParams(vmem_limit_bytes=32 << 20),
        name="image_and_gram",
    )(*args)


def sum_kernel(parts, out):
    total = jnp.sum(parts[...], axis=0)
    for peer in range(out.shape[0]):
        out[peer] = total


def sum_and_spread(parts, peers):
    return pl.pallas_call(
        sum_kernel,
        out_shape=jax.ShapeDtypeStruct((peers, 8, NZ), F32),
        in_specs=[VMEM],
        out_specs=VMEM,
        compiler_params=pltpu.CompilerParams(vmem_limit_bytes=1 << 20),
        name="sum_and_spread",
    )(parts)


def mul(left, right):
    return lax.dot_general(left, right, (((1,), (0,)), ((), ())), precision=HIGHEST, preferred_element_type=F32)


def mul_t(left, right):
    return lax.dot_general(left, right, (((1,), (1,)), ((), ())), precision=HIGHEST, preferred_element_type=F32)


def inverse_factor(gram):
    lane = lax.broadcasted_iota(jnp.int32, (8, NZ), 1)
    row = lax.broadcasted_iota(jnp.int32, (8, NZ), 0)
    work = jnp.where(lane < 8, gram, jnp.where(lane == row + 8, 1.0, 0.0))
    rank = 2 * (row % 4) + row // 4
    for step in range(8):
        k = (step % 2) * 4 + step // 2
        line = work[k:k + 1, :]
        pivot = line[:, k:k + 1]
        column = work[:, k:k + 1]
        root = 1.0 / jnp.sqrt(pivot)
        line = line * root
        factor = column * root
        work = jnp.where(rank > step, work - factor * line, jnp.where(rank == step, line, work))
    return jnp.where(lane < 8, lane_roll(work, -8), 0.0)


def coefficients(gram):
    lane = lax.broadcasted_iota(jnp.int32, (8, NZ), 1)
    row = lax.broadcasted_iota(jnp.int32, (8, NZ), 0)
    tall = lax.broadcasted_iota(jnp.int32, (NZ, NZ), 0)
    wide = lax.broadcasted_iota(jnp.int32, (NZ, NZ), 1)

    def normalise(rows):
        small = mul_t(mul(rows, gram), rows_in(rows))
        return mul(inverse_factor(small)[:, 0:8], rows)

    def rows_in(rows):
        return jnp.concatenate([rows, jnp.zeros((NZ - 8, NZ), F32)], axis=0)

    once = jnp.where(lane < 24, gram[24:32], 0.0)
    again = jnp.where(lane < 24, mul(once, gram), 0.0)
    fresh = jnp.where(lane == row + 24, 1.0, 0.0)
    new = normalise(fresh - (2.0 * once - again))
    image = (jnp.where((lane >= 32) & (lane < 48), lane_roll(new, 32), 0.0)
             + jnp.where((lane >= 24) & (lane < 32), lane_roll(new, 8), 0.0)
             + jnp.where((lane >= 48) & (lane < 56), lane_roll(new, 24), 0.0))
    window = jnp.where((tall < 16) & (wide == tall + 8), 1.0, 0.0)
    window = jnp.concatenate([window[0:16], new, window[24:]], axis=0)

    def project(rows):
        return mul(mul_t(mul(rows, gram), window), window)

    once = project(image)
    again = project(once)
    newest = normalise(image - (2.0 * once - again))
    return new, newest


def final_kernel(cells, parts, start, w, image0, image1, w_image, out):
    gram = unpack_gram(jnp.sum(parts[...], axis=0) * (1.0 / cells))
    new, newest = coefficients(gram)
    mapping = jnp.concatenate([new, newest], axis=0)[:, 0:ROWS]
    pieces = [jnp.concatenate([piece] * 3, axis=1) for piece in split3(mapping)]
    stacked_map = jnp.concatenate(pieces, axis=0)

    def plane(x, carry):
        stacked = jnp.concatenate(split3(basis_plane(start, w, image0, image1, w_image, x)), axis=0)
        full = lax.dot_general(stacked_map, stacked, (((1,), (0,)), ((), ())), preferred_element_type=F32)
        result = full[32:48] + full[16:32] + full[0:16]
        for k in range(2):
            tiles = jnp.stack([result[8 * k:8 * k + 8, y * NZ:(y + 1) * NZ] for y in range(LY)])
            out[k, :, x] = jnp.swapaxes(tiles, 0, 1)
        return carry

    lax.fori_loop(0, LX, plane, 0)


def finish(cells, *args):
    return pl.pallas_call(
        functools.partial(final_kernel, cells),
        out_shape=jax.ShapeDtypeStruct((2, 8, LX, LY, NZ), F32),
        in_specs=[VMEM] * 6,
        out_specs=VMEM,
        compiler_params=pltpu.CompilerParams(vmem_limit_bytes=32 << 20),
        name="finish",
    )(*args)


GX = ("z", "core")


def from_both(axis, count, to_higher, to_lower):
    return (
        lax.ppermute(to_higher, axis, [(i, i + 1) for i in range(count - 1)]),
        lax.ppermute(to_lower, axis, [(i + 1, i) for i in range(count - 1)]),
    )


def per_device(nx, ny, nz, prior, coefficient):
    cells = coefficient.size * nx * ny
    by_cell = prior.transpose(3, 0, 4, 1, 2, 5).reshape(LX, 3 * LY * 8, NZ)
    start = jnp.concatenate([by_cell, coefficient], axis=1)
    sides = from_both(GX, nx, start, start)
    up, down, old_up, old_down = pack_rim(first_rim_kernel, [RIM + 4] * 2 + [2 * RIM] * 2, start, sides)
    rims = from_both("gy", ny, up, down)
    old_rims = from_both("gy", ny, old_up, old_down)
    w, coef = first_image(start, *sides, *rims)

    w_sides = from_both(GX, nx, w, w)
    w_rims = from_both("gy", ny, *pack_rim(rim_kernel, [RIM] * 2, w, w_sides))
    image0 = old_image(0, start, *sides, *old_rims, coef)
    image1 = old_image(1, start, *sides, *old_rims, coef)

    w_image, spread = image_and_gram(2 * ny, w, *w_sides, *w_rims, coef, start, image0, image1)
    got = lax.all_to_all(spread, ("core", "gy"), 0, 0)
    got = lax.all_to_all(sum_and_spread(got, nz), "z", 0, 0)
    out = finish(cells, got, start, w, image0, image1, w_image)
    return out.reshape(2, 2, 4, LX, LY, NZ)


def solution(mesh):
    nx, ny = mesh.shape["gx"], mesh.shape["gy"]
    fine = Mesh(np.asarray(mesh.devices).reshape(nx // 2, 2, ny), ("z", "core", "gy"))
    in_specs = (P(None, None, None, GX, "gy", None), P(GX, "gy", None))
    out_specs = P(None, None, None, GX, "gy", None)
    return jax.shard_map(
        functools.partial(per_device, nx, ny, nx // 2),
        mesh=fine, in_specs=in_specs, out_specs=out_specs, check_vma=False,
    )
```

```python
import functools

import jax
import jax.numpy as jnp
import numpy as np
from jax import lax
from jax.experimental import pallas as pl
from jax.experimental.pallas import tpu as pltpu
from jax.sharding import Mesh, PartitionSpec as P

LX, LY, NZ = 4, 8, 128
NEAR, FAR = 4, 8
BLOCKS = 7
ROWS = 64
F32 = jnp.float32
BF16 = jnp.bfloat16
HIGHEST = lax.Precision.HIGHEST
VMEM = pl.BlockSpec(memory_space=pltpu.VMEM)


def widths(halo):
    return [LX + 2 * (halo - d) for d in range(1, halo + 1)]


def rim_spots(halo):
    spots, place = [], 0
    for d, width in zip(range(1, halo + 1), widths(halo)):
        for i in range(width):
            spots.append((d, d + i, place))
            place += 1
    return spots


def plane_of(parts, index):
    ref, first = parts[index // LX]
    return ref, index % LX, first


def shifted(parts, rows):
    return [(ref, first + rows) for ref, first in parts]


def fill_rim(parts, halo, up, down, start):
    for d, plane, place in rim_spots(halo):
        ref, x, first = plane_of(parts, plane)
        up[start + place] = ref[x, pl.ds(first + (LY - d) * 8, 8), :]
        down[start + place] = ref[x, pl.ds(first + (d - 1) * 8, 8), :]


def fill_flat_rim(parts, halo, up, down, start):
    for d, plane, place in rim_spots(halo):
        ref, x, first = plane_of(parts, plane)
        tile, row = start + place // 8, place % 8
        up[tile, pl.ds(row, 1), :] = ref[x, pl.ds(first + LY - d, 1), :]
        down[tile, pl.ds(row, 1), :] = ref[x, pl.ds(first + d - 1, 1), :]


BLOCK = LY * 8
OLD_RIM = sum(widths(NEAR))
FAR_RIM = sum(widths(FAR))


def recent_parts(far_low, low, own, high, far_high):
    return [(far_low, 0), (low, 2 * BLOCK), (own, 2 * BLOCK), (high, 2 * BLOCK), (far_high, 0)]


def rim_kernel(own, low, high, far_low, far_high, up, down, old_up, old_down):
    parts = [(low, 0), (own, 0), (high, 0)]
    wide = recent_parts(far_low, low, own, high, far_high)
    for group in range(2):
        fill_rim(shifted(parts, group * BLOCK), NEAR, old_up, old_down, group * OLD_RIM)
    fill_flat_rim(shifted(wide, BLOCK), FAR, old_up, old_down, 2 * OLD_RIM)
    fill_rim(wide, FAR, up, down, 0)


def pack_rims(*args):
    sizes = [FAR_RIM] * 2 + [2 * OLD_RIM + FAR_RIM // 8] * 2
    shapes = tuple(jax.ShapeDtypeStruct((size, 8, NZ), F32) for size in sizes)
    return pl.pallas_call(
        rim_kernel,
        out_shape=shapes,
        in_specs=[VMEM] * 5,
        out_specs=(VMEM,) * 4,
        compiler_params=pltpu.CompilerParams(vmem_limit_bytes=1 << 20),
        name="pack_rims",
    )(*args)


def fill_block(parts, halo, from_low, from_high, start, wide):
    wide[...] = jnp.zeros(wide.shape, F32)
    for index in range(LX + 2 * halo):
        ref, x, first = plane_of(parts, index)
        wide[index, halo:halo + LY] = ref[x, pl.ds(first, BLOCK), :].reshape(LY, 8, NZ)
    for d, plane, place in rim_spots(halo):
        wide[plane, halo - d] = from_low[start + place]
        wide[plane, halo + LY - 1 + d] = from_high[start + place]


def fill_flat(parts, halo, from_low, from_high, start, wide):
    wide[...] = jnp.zeros(wide.shape, F32)
    for index in range(LX + 2 * halo):
        ref, x, first = plane_of(parts, index)
        wide[index, halo:halo + LY] = ref[x, pl.ds(first, LY), :]
    for d, plane, place in rim_spots(halo):
        tile, row = start + place // 8, place % 8
        wide[plane, pl.ds(halo - d, 1), :] = from_low[tile, pl.ds(row, 1), :]
        wide[plane, pl.ds(halo + LY - 1 + d, 1), :] = from_high[tile, pl.ds(row, 1), :]


def fill_tables(coef, skip, table_re, table_im, diag_re, diag_im):
    value = coef[...]
    real = 6.0 - value
    imag = 0.5 * value
    scale = jnp.where(value > 0.0, 0.8 / (real * real + imag * imag), 0.0)
    diag_re[...] = real * scale
    diag_im[...] = imag * scale
    sign = jnp.where(lax.broadcasted_iota(jnp.int32, (8, NZ), 0) < 4, 1.0, -1.0)
    size_x, size_y = table_re.shape[:2]

    def body(x, carry):
        for y in range(size_y):
            spot = pl.ds(y + skip, 1)
            table_re[x, y] = jnp.broadcast_to(diag_re[x + skip, spot, :], (8, NZ))
            table_im[x, y] = jnp.broadcast_to(diag_im[x + skip, spot, :], (8, NZ)) * sign
        return carry

    lax.fori_loop(0, size_x, body, 0)


def depth_sum(value):
    lane = lax.broadcasted_iota(jnp.int32, value.shape, 1)
    above = jnp.where(lane == 0, 0.0, pltpu.roll(value, 1, 1))
    below = jnp.where(lane == NZ - 1, 0.0, pltpu.roll(value, NZ - 1, 1))
    return above + below


def smooth(block, coef, skip, reach, table_re, table_im, first, second, store):
    size_x, size_y = block.shape[:2]

    def solve(value, x, y):
        return table_re[x, y] * value + table_im[x, y] * pltpu.roll(value, 4, 0)

    def sections(k):
        low, high = k, size_y - k
        if reach == 0:
            return [((k, size_x - k), (low, high))]
        return [((k, 4), (low + 5, high - 5)), ((4, size_x - 4), (low, high)),
                ((size_x - 4, size_x - k), (low + 5, high - 5))]

    def planes(k, body):
        for (begin, end), (low, high) in sections(k):
            if begin < end:
                lax.fori_loop(begin, end, functools.partial(body, low, high), 0)

    def start(low, high, x, carry):
        for y in range(low, high):
            first[x, y] = solve(block[x, y], x, y)
        return carry

    def around(ref, x, low, high):
        line = [ref[x, y] for y in range(low - 1, high + 1)]
        for y in range(low, high):
            mid = line[y - low + 1]
            total = ref[x - 1, y] + ref[x + 1, y] + line[y - low] + line[y - low + 2]
            yield y, mid, total + depth_sum(mid)

    if reach:
        first[...] = jnp.zeros(first.shape, F32)
        second[...] = jnp.zeros(second.shape, F32)
    planes(0, start)
    here, there = first, second
    for k in range(1, 4):
        def sweep(low, high, x, carry, here=here, there=there):
            for y, mid, total in around(here, x, low, high):
                there[x, y] = 0.2 * mid + solve(block[x, y] + total, x, y)
            return carry

        planes(k, sweep)
        here, there = there, here

    def image(x, carry):
        for y, mid, total in around(here, x, 4, size_y - 4):
            diag = 6.0 - coef[x + skip, pl.ds(y + skip, 1), :]
            store(x - 4, y - 4, diag * mid - total)
        return carry

    lax.fori_loop(4, size_x - 4, image, 0)


def wide_shape(halo):
    return (LX + 2 * halo, LY + 2 * halo)


FLAT = pltpu.VMEM((*wide_shape(FAR), NZ), F32)


def smooth_scratch(halo):
    return [pltpu.VMEM((*wide_shape(halo), 8, NZ), F32)] * 5 + [FLAT] * 2


def old_kernel(own, low, high, far_low, far_high, from_low, from_high, out, coef, block, first, second,
               table_re, table_im, diag_re, diag_im):
    wide = recent_parts(far_low, low, own, high, far_high)
    fill_flat(shifted(wide, BLOCK), FAR, from_low, from_high, 2 * OLD_RIM, coef)
    fill_tables(coef, FAR - NEAR, table_re, table_im, diag_re, diag_im)
    for group in range(2):
        parts = [(low, group * BLOCK), (own, group * BLOCK), (high, group * BLOCK)]
        fill_block(parts, NEAR, from_low, from_high, group * OLD_RIM, block)

        def store(x, y, value, group=group):
            out[x, pl.ds(group * BLOCK + y * 8, 8), :] = value

        smooth(block, coef, FAR - NEAR, 0, table_re, table_im, first, second, store)


def old_images(*args):
    return pl.pallas_call(
        old_kernel,
        out_shape=(jax.ShapeDtypeStruct((LX, 2 * BLOCK, NZ), F32),
                   jax.ShapeDtypeStruct((*wide_shape(FAR), NZ), F32)),
        in_specs=[VMEM] * 7,
        out_specs=(VMEM, VMEM),
        scratch_shapes=smooth_scratch(NEAR),
        compiler_params=pltpu.CompilerParams(vmem_limit_bytes=16 << 20),
        cost_estimate=pl.CostEstimate(flops=12_000_000, bytes_accessed=24_000_000, transcendentals=0),
        name="old_images",
    )(*args)


def first_kernel(own, low, high, far_low, far_high, from_low, from_high, coef, out, block, first, second,
                 table_re, table_im, diag_re, diag_im):
    fill_tables(coef, 0, table_re, table_im, diag_re, diag_im)
    fill_block(recent_parts(far_low, low, own, high, far_high), FAR, from_low, from_high, 0, block)

    def store(x, y, value):
        out[x, y] = value

    smooth(block, coef, 0, NEAR, table_re, table_im, first, second, store)


def first_image(*args):
    return pl.pallas_call(
        first_kernel,
        out_shape=jax.ShapeDtypeStruct((*wide_shape(NEAR), 8, NZ), F32),
        in_specs=[VMEM] * 8,
        out_specs=VMEM,
        scratch_shapes=smooth_scratch(FAR),
        compiler_params=pltpu.CompilerParams(vmem_limit_bytes=24 << 20),
        name="first_image",
    )(*args)


def split3(value):
    high = value.astype(BF16)
    rest = value - high.astype(F32)
    middle = rest.astype(BF16)
    low = (rest - middle.astype(F32)).astype(BF16)
    return high, middle, low


def basis_plane(start, w, old_image, w_image, x):
    refs = [(start, 0), (start, LY), (start, 2 * LY), (w, None), (old_image, 0), (old_image, LY), (w_image, 0)]
    rows = []
    for ref, first in refs:
        if first is None:
            tiles = [ref[x + NEAR, NEAR + y] for y in range(LY)]
        else:
            tiles = [ref[x, pl.ds((first + y) * 8, 8), :] for y in range(LY)]
        rows.append(jnp.concatenate(tiles, axis=1))
    rows.append(jnp.zeros((8, LY * NZ), F32))
    return jnp.concatenate(rows, axis=0)


def lane_roll(value, amount):
    return pltpu.roll(value, amount % NZ, 1)


SLOTS = [(0, 0), (0, 56), (1, 0), (1, 40), (1, 72), (1, 96), (0, 104)]


def pack_gram(gram):
    lane = lax.broadcasted_iota(jnp.int32, (8, NZ), 1)
    row = lax.broadcasted_iota(jnp.int32, (8, NZ), 0)
    packed = jnp.zeros((8, NZ), F32)
    for b in range(BLOCKS):
        rows = gram[8 * b:8 * b + 8]
        turned = jnp.where(lane % 8 < 4, lane_roll(rows, -4), -lane_roll(rows, 4))
        both = rows + pltpu.roll(turned, 4, 0)
        half, start = SLOTS[b]
        moved = lane_roll(both, start - 8 * b)
        if half:
            moved = pltpu.roll(moved, 4, 0)
        keep = (lane >= start) & (lane < start + 8 * (BLOCKS - b)) & (row // 4 == half)
        packed = packed + jnp.where(keep, moved, 0.0)
    return packed


def unpack_gram(packed):
    lane = lax.broadcasted_iota(jnp.int32, (8, NZ), 1)
    row = lax.broadcasted_iota(jnp.int32, (8, NZ), 0)
    rows = []
    for b in range(BLOCKS):
        half, start = SLOTS[b]
        moved = lane_roll(packed, 8 * b - start)
        if half:
            moved = pltpu.roll(moved, 4, 0)
        keep = (lane >= 8 * b) & (lane < 8 * BLOCKS) & (row < 4)
        moved = jnp.where(keep, moved, 0.0)
        turned = jnp.where(lane % 8 < 4, -lane_roll(moved, -4), lane_roll(moved, 4))
        rows.append(moved + pltpu.roll(turned, 4, 0))
    rows.append(jnp.zeros((NZ - 8 * BLOCKS, NZ), F32))
    upper = jnp.concatenate(rows, axis=0)
    tall = lax.broadcasted_iota(jnp.int32, (NZ, NZ), 0)
    wide = lax.broadcasted_iota(jnp.int32, (NZ, NZ), 1)
    return jnp.where(tall // 8 <= wide // 8, upper, upper.T)


def gram_kernel(peers, w, coef, start, old_image, w_image, out,
                first, second, table_re, table_im, diag_re, diag_im):
    fill_tables(coef, FAR - NEAR, table_re, table_im, diag_re, diag_im)

    def store(x, y, value):
        w_image[x, pl.ds(y * 8, 8), :] = value

    smooth(w, coef, FAR - NEAR, 0, table_re, table_im, first, second, store)

    def plane(x, total):
        stacked = jnp.concatenate(split3(basis_plane(start, w, old_image, w_image, x)), axis=0)
        return total + lax.dot_general(stacked, stacked, (((1,), (1,)), ((), ())), preferred_element_type=F32)

    total = lax.fori_loop(0, LX, plane, jnp.zeros((3 * ROWS, 3 * ROWS), F32))
    tall = total[0:ROWS] + total[ROWS:2 * ROWS] + total[2 * ROWS:3 * ROWS]
    gram = tall[:, 0:ROWS] + tall[:, ROWS:2 * ROWS] + tall[:, 2 * ROWS:3 * ROWS]
    gram = jnp.concatenate([gram, jnp.zeros((ROWS, NZ - ROWS), F32)], axis=1)
    packed = pack_gram(gram)
    for peer in range(peers):
        out[peer] = packed


def image_and_gram(peers, *args):
    return pl.pallas_call(
        functools.partial(gram_kernel, peers),
        out_shape=(jax.ShapeDtypeStruct((LX, LY * 8, NZ), F32),
                   jax.ShapeDtypeStruct((peers, 8, NZ), F32)),
        in_specs=[VMEM] * 4,
        out_specs=(VMEM, VMEM),
        scratch_shapes=smooth_scratch(NEAR)[1:],
        compiler_params=pltpu.CompilerParams(vmem_limit_bytes=32 << 20),
        name="image_and_gram",
    )(*args)


def sum_kernel(parts, out):
    total = jnp.sum(parts[...], axis=0)
    for peer in range(out.shape[0]):
        out[peer] = total


def sum_and_spread(parts, peers):
    return pl.pallas_call(
        sum_kernel,
        out_shape=jax.ShapeDtypeStruct((peers, 8, NZ), F32),
        in_specs=[VMEM],
        out_specs=VMEM,
        compiler_params=pltpu.CompilerParams(vmem_limit_bytes=1 << 20),
        name="sum_and_spread",
    )(parts)


def mul(left, right):
    return lax.dot_general(left, right, (((1,), (0,)), ((), ())), precision=HIGHEST, preferred_element_type=F32)


def mul_t(left, right):
    return lax.dot_general(left, right, (((1,), (1,)), ((), ())), precision=HIGHEST, preferred_element_type=F32)


def inverse_factor(gram):
    lane = lax.broadcasted_iota(jnp.int32, (8, NZ), 1)
    row = lax.broadcasted_iota(jnp.int32, (8, NZ), 0)
    work = jnp.where(lane < 8, gram, jnp.where(lane == row + 8, 1.0, 0.0))
    rank = 2 * (row % 4) + row // 4
    for step in range(8):
        k = (step % 2) * 4 + step // 2
        line = work[k:k + 1, :]
        pivot = line[:, k:k + 1]
        column = work[:, k:k + 1]
        root = 1.0 / jnp.sqrt(pivot)
        line = line * root
        factor = column * root
        work = jnp.where(rank > step, work - factor * line, jnp.where(rank == step, line, work))
    return jnp.where(lane < 8, lane_roll(work, -8), 0.0)


def coefficients(gram):
    lane = lax.broadcasted_iota(jnp.int32, (8, NZ), 1)
    row = lax.broadcasted_iota(jnp.int32, (8, NZ), 0)
    tall = lax.broadcasted_iota(jnp.int32, (NZ, NZ), 0)
    wide = lax.broadcasted_iota(jnp.int32, (NZ, NZ), 1)

    def normalise(rows):
        small = mul_t(mul(rows, gram), rows_in(rows))
        return mul(inverse_factor(small)[:, 0:8], rows)

    def rows_in(rows):
        return jnp.concatenate([rows, jnp.zeros((NZ - 8, NZ), F32)], axis=0)

    once = jnp.where(lane < 24, gram[24:32], 0.0)
    again = jnp.where(lane < 24, mul(once, gram), 0.0)
    fresh = jnp.where(lane == row + 24, 1.0, 0.0)
    new = normalise(fresh - (2.0 * once - again))
    image = (jnp.where((lane >= 32) & (lane < 48), lane_roll(new, 32), 0.0)
             + jnp.where((lane >= 24) & (lane < 32), lane_roll(new, 8), 0.0)
             + jnp.where((lane >= 48) & (lane < 56), lane_roll(new, 24), 0.0))
    window = jnp.where((tall < 16) & (wide == tall + 8), 1.0, 0.0)
    window = jnp.concatenate([window[0:16], new, window[24:]], axis=0)

    def project(rows):
        return mul(mul_t(mul(rows, gram), window), window)

    once = project(image)
    again = project(once)
    newest = normalise(image - (2.0 * once - again))
    return new, newest


def final_kernel(cells, parts, start, w, old_image, w_image, out):
    gram = unpack_gram(jnp.sum(parts[...], axis=0) * (1.0 / cells))
    new, newest = coefficients(gram)
    mapping = jnp.concatenate([new, newest], axis=0)[:, 0:ROWS]
    pieces = [jnp.concatenate([piece] * 3, axis=1) for piece in split3(mapping)]
    stacked_map = jnp.concatenate(pieces, axis=0)

    def plane(x, carry):
        stacked = jnp.concatenate(split3(basis_plane(start, w, old_image, w_image, x)), axis=0)
        full = lax.dot_general(stacked_map, stacked, (((1,), (0,)), ((), ())), preferred_element_type=F32)
        result = full[32:48] + full[16:32] + full[0:16]
        for k in range(2):
            tiles = jnp.stack([result[8 * k:8 * k + 8, y * NZ:(y + 1) * NZ] for y in range(LY)])
            out[k, :, x] = jnp.swapaxes(tiles, 0, 1)
        return carry

    lax.fori_loop(0, LX, plane, 0)


def finish(cells, *args):
    return pl.pallas_call(
        functools.partial(final_kernel, cells),
        out_shape=jax.ShapeDtypeStruct((2, 8, LX, LY, NZ), F32),
        in_specs=[VMEM] * 5,
        out_specs=VMEM,
        compiler_params=pltpu.CompilerParams(vmem_limit_bytes=32 << 20),
        name="finish",
    )(*args)


GX = ("z", "core")


def from_both(axis, count, to_higher, to_lower, step=1):
    return (
        lax.ppermute(to_higher, axis, [(i, i + step) for i in range(count - step)]),
        lax.ppermute(to_lower, axis, [(i + step, i) for i in range(count - step)]),
    )


def per_device(nx, ny, nz, prior, coefficient):
    cells = coefficient.size * nx * ny
    by_cell = prior.transpose(3, 0, 4, 1, 2, 5).reshape(LX, 3 * LY * 8, NZ)
    start = jnp.concatenate([by_cell, coefficient], axis=1)
    far = start[:, 2 * BLOCK:]
    sides = from_both(GX, nx, start, start) + from_both(GX, nx, far, far, 2)
    up, down, old_up, old_down = pack_rims(start, *sides)
    old_rims = from_both("gy", ny, old_up, old_down)
    rims = from_both("gy", ny, up, down)
    old_image, coef = old_images(start, *sides, *old_rims)
    w = first_image(start, *sides, *rims, coef)

    w_image, spread = image_and_gram(2 * ny, w, coef, start, old_image)
    got = lax.all_to_all(spread, ("core", "gy"), 0, 0)
    got = lax.all_to_all(sum_and_spread(got, nz), "z", 0, 0)
    out = finish(cells, got, start, w, old_image, w_image)
    return out.reshape(2, 2, 4, LX, LY, NZ)


def solution(mesh):
    nx, ny = mesh.shape["gx"], mesh.shape["gy"]
    fine = Mesh(np.asarray(mesh.devices).reshape(nx // 2, 2, ny), ("z", "core", "gy"))
    in_specs = (P(None, None, None, GX, "gy", None), P(GX, "gy", None))
    out_specs = P(None, None, None, GX, "gy", None)
    return jax.shard_map(
        functools.partial(per_device, nx, ny, nx // 2),
        mesh=fine, in_specs=in_specs, out_specs=out_specs, check_vma=False,
    )
```

```python
import functools

import jax
import jax.numpy as jnp
import numpy as np
from jax import lax
from jax.experimental import pallas as pl
from jax.experimental.pallas import tpu as pltpu
from jax.sharding import Mesh, PartitionSpec as P

LX, LY, NZ = 4, 8, 128
NEAR, FAR = 4, 8
BLOCKS = 7
ROWS = 64
F32 = jnp.float32
BF16 = jnp.bfloat16
HIGHEST = lax.Precision.HIGHEST
VMEM = pl.BlockSpec(memory_space=pltpu.VMEM)


def widths(halo):
    return [LX + 2 * (halo - d) for d in range(1, halo + 1)]


def rim_spots(halo):
    spots, place = [], 0
    for d, width in zip(range(1, halo + 1), widths(halo)):
        for i in range(width):
            spots.append((d, d + i, place))
            place += 1
    return spots


def plane_of(parts, index):
    ref, first = parts[index // LX]
    return ref, index % LX, first


def shifted(parts, rows):
    return [(ref, first + rows) for ref, first in parts]


def fill_rim(parts, halo, up, down, start, begin=0, end=None):
    for d, plane, place in rim_spots(halo)[begin:end]:
        ref, x, first = plane_of(parts, plane)
        up[start + place] = ref[x, pl.ds(first + (LY - d) * 8, 8), :]
        down[start + place] = ref[x, pl.ds(first + (d - 1) * 8, 8), :]


def fill_flat_rim(parts, halo, up, down, start):
    for d, plane, place in rim_spots(halo):
        ref, x, first = plane_of(parts, plane)
        tile, row = start + place // 8, place % 8
        up[tile, pl.ds(row, 1), :] = ref[x, pl.ds(first + LY - d, 1), :]
        down[tile, pl.ds(row, 1), :] = ref[x, pl.ds(first + d - 1, 1), :]


BLOCK = LY * 8
OLD_RIM = sum(widths(NEAR))
FAR_RIM = sum(widths(FAR))
SPLIT = sum(widths(FAR)[:5])
EARLY = 2 * OLD_RIM + FAR_RIM // 8


def recent_parts(far_low, low, own, high, far_high):
    return [(far_low, 0), (low, 2 * BLOCK), (own, 2 * BLOCK), (high, 2 * BLOCK), (far_high, 0)]


def rim_kernel(own, low, high, far_low, far_high, up, down, old_up, old_down):
    parts = [(low, 0), (own, 0), (high, 0)]
    wide = recent_parts(far_low, low, own, high, far_high)
    for group in range(2):
        fill_rim(shifted(parts, group * BLOCK), NEAR, old_up, old_down, group * OLD_RIM)
    fill_flat_rim(shifted(wide, BLOCK), FAR, old_up, old_down, 2 * OLD_RIM)
    fill_rim(wide, FAR, up, down, 0, 0, SPLIT)
    fill_rim(wide, FAR, old_up, old_down, EARLY - SPLIT, SPLIT)


def pack_rims(*args):
    sizes = [SPLIT] * 2 + [EARLY + FAR_RIM - SPLIT] * 2
    shapes = tuple(jax.ShapeDtypeStruct((size, 8, NZ), F32) for size in sizes)
    return pl.pallas_call(
        rim_kernel,
        out_shape=shapes,
        in_specs=[VMEM] * 5,
        out_specs=(VMEM,) * 4,
        compiler_params=pltpu.CompilerParams(vmem_limit_bytes=1 << 20),
        name="pack_rims",
    )(*args)


def fill_block(parts, halo, find_rim, wide):
    wide[...] = jnp.zeros(wide.shape, F32)
    for index in range(LX + 2 * halo):
        ref, x, first = plane_of(parts, index)
        wide[index, halo:halo + LY] = ref[x, pl.ds(first, BLOCK), :].reshape(LY, 8, NZ)
    for d, plane, place in rim_spots(halo):
        from_low, from_high, spot = find_rim(place)
        wide[plane, halo - d] = from_low[spot]
        wide[plane, halo + LY - 1 + d] = from_high[spot]


def fill_flat(parts, halo, from_low, from_high, start, wide):
    wide[...] = jnp.zeros(wide.shape, F32)
    for index in range(LX + 2 * halo):
        ref, x, first = plane_of(parts, index)
        wide[index, halo:halo + LY] = ref[x, pl.ds(first, LY), :]
    for d, plane, place in rim_spots(halo):
        tile, row = start + place // 8, place % 8
        wide[plane, pl.ds(halo - d, 1), :] = from_low[tile, pl.ds(row, 1), :]
        wide[plane, pl.ds(halo + LY - 1 + d, 1), :] = from_high[tile, pl.ds(row, 1), :]


def fill_tables(coef, skip, table_re, table_im, diag_re, diag_im):
    value = coef[...]
    real = 6.0 - value
    imag = 0.5 * value
    scale = jnp.where(value > 0.0, 0.8 / (real * real + imag * imag), 0.0)
    diag_re[...] = real * scale
    diag_im[...] = imag * scale
    sign = jnp.where(lax.broadcasted_iota(jnp.int32, (8, NZ), 0) < 4, 1.0, -1.0)
    size_x, size_y = table_re.shape[:2]

    def body(x, carry):
        for y in range(size_y):
            spot = pl.ds(y + skip, 1)
            table_re[x, y] = jnp.broadcast_to(diag_re[x + skip, spot, :], (8, NZ))
            table_im[x, y] = jnp.broadcast_to(diag_im[x + skip, spot, :], (8, NZ)) * sign
        return carry

    lax.fori_loop(0, size_x, body, 0)


def depth_sum(value):
    lane = lax.broadcasted_iota(jnp.int32, value.shape, 1)
    above = jnp.where(lane == 0, 0.0, pltpu.roll(value, 1, 1))
    below = jnp.where(lane == NZ - 1, 0.0, pltpu.roll(value, NZ - 1, 1))
    return above + below


def smooth(block, coef, skip, reach, table_re, table_im, first, second, store):
    size_x, size_y = block.shape[:2]

    def solve(value, x, y):
        return table_re[x, y] * value + table_im[x, y] * pltpu.roll(value, 4, 0)

    def sections(k):
        low, high = k, size_y - k
        if reach == 0:
            return [((k, size_x - k), (low, high))]
        return [((k, 4), (low + 5, high - 5)), ((4, size_x - 4), (low, high)),
                ((size_x - 4, size_x - k), (low + 5, high - 5))]

    def planes(k, body):
        for (begin, end), (low, high) in sections(k):
            if begin < end:
                lax.fori_loop(begin, end, functools.partial(body, low, high), 0)

    def start(low, high, x, carry):
        for y in range(low, high):
            first[x, y] = solve(block[x, y], x, y)
        return carry

    def around(ref, x, low, high):
        line = [ref[x, y] for y in range(low - 1, high + 1)]
        for y in range(low, high):
            mid = line[y - low + 1]
            total = ref[x - 1, y] + ref[x + 1, y] + line[y - low] + line[y - low + 2]
            yield y, mid, total + depth_sum(mid)

    if reach:
        first[...] = jnp.zeros(first.shape, F32)
        second[...] = jnp.zeros(second.shape, F32)
    planes(0, start)
    here, there = first, second
    for k in range(1, 4):
        def sweep(low, high, x, carry, here=here, there=there):
            for y, mid, total in around(here, x, low, high):
                there[x, y] = 0.2 * mid + solve(block[x, y] + total, x, y)
            return carry

        planes(k, sweep)
        here, there = there, here

    def image(x, carry):
        for y, mid, total in around(here, x, 4, size_y - 4):
            diag = 6.0 - coef[x + skip, pl.ds(y + skip, 1), :]
            store(x - 4, y - 4, diag * mid - total)
        return carry

    lax.fori_loop(4, size_x - 4, image, 0)


def wide_shape(halo):
    return (LX + 2 * halo, LY + 2 * halo)


FLAT = pltpu.VMEM((*wide_shape(FAR), NZ), F32)


def smooth_scratch(halo):
    return [pltpu.VMEM((*wide_shape(halo), 8, NZ), F32)] * 5 + [FLAT] * 2


def old_kernel(own, low, high, far_low, far_high, from_low, from_high, out, coef, block, first, second,
               table_re, table_im, diag_re, diag_im):
    wide = recent_parts(far_low, low, own, high, far_high)
    fill_flat(shifted(wide, BLOCK), FAR, from_low, from_high, 2 * OLD_RIM, coef)
    fill_tables(coef, FAR - NEAR, table_re, table_im, diag_re, diag_im)
    for group in range(2):
        parts = [(low, group * BLOCK), (own, group * BLOCK), (high, group * BLOCK)]
        fill_block(parts, NEAR, lambda place, group=group: (from_low, from_high, group * OLD_RIM + place), block)

        def store(x, y, value, group=group):
            out[x, pl.ds(group * BLOCK + y * 8, 8), :] = value

        smooth(block, coef, FAR - NEAR, 0, table_re, table_im, first, second, store)


def old_images(*args):
    return pl.pallas_call(
        old_kernel,
        out_shape=(jax.ShapeDtypeStruct((LX, 2 * BLOCK, NZ), F32),
                   jax.ShapeDtypeStruct((*wide_shape(FAR), NZ), F32)),
        in_specs=[VMEM] * 7,
        out_specs=(VMEM, VMEM),
        scratch_shapes=smooth_scratch(NEAR),
        compiler_params=pltpu.CompilerParams(vmem_limit_bytes=16 << 20),
        cost_estimate=pl.CostEstimate(flops=12_000_000, bytes_accessed=24_000_000, transcendentals=0),
        name="old_images",
    )(*args)


def first_kernel(coef, own, low, high, far_low, far_high, from_low, from_high, early_low, early_high, out, block, first, second,
                 table_re, table_im, diag_re, diag_im):
    fill_tables(coef, 0, table_re, table_im, diag_re, diag_im)

    def find_rim(place):
        if place < SPLIT:
            return from_low, from_high, place
        return early_low, early_high, EARLY + place - SPLIT

    fill_block(recent_parts(far_low, low, own, high, far_high), FAR, find_rim, block)

    def store(x, y, value):
        out[x, y] = value

    smooth(block, coef, 0, NEAR, table_re, table_im, first, second, store)


def first_image(*args):
    return pl.pallas_call(
        first_kernel,
        out_shape=jax.ShapeDtypeStruct((*wide_shape(NEAR), 8, NZ), F32),
        in_specs=[VMEM] * 10,
        out_specs=VMEM,
        scratch_shapes=smooth_scratch(FAR),
        compiler_params=pltpu.CompilerParams(vmem_limit_bytes=24 << 20),
        name="first_image",
    )(*args)


def split3(value):
    high = value.astype(BF16)
    rest = value - high.astype(F32)
    middle = rest.astype(BF16)
    low = (rest - middle.astype(F32)).astype(BF16)
    return high, middle, low


def basis_plane(start, w, old_image, w_image, x):
    refs = [(start, 0), (start, LY), (start, 2 * LY), (w, None), (old_image, 0), (old_image, LY), (w_image, 0)]
    rows = []
    for ref, first in refs:
        if first is None:
            tiles = [ref[x + NEAR, NEAR + y] for y in range(LY)]
        else:
            tiles = [ref[x, pl.ds((first + y) * 8, 8), :] for y in range(LY)]
        rows.append(jnp.concatenate(tiles, axis=1))
    rows.append(jnp.zeros((8, LY * NZ), F32))
    return jnp.concatenate(rows, axis=0)


def lane_roll(value, amount):
    return pltpu.roll(value, amount % NZ, 1)


SLOTS = [(0, 0), (0, 56), (1, 0), (1, 40), (1, 72), (1, 96), (0, 104)]


def pack_gram(gram):
    lane = lax.broadcasted_iota(jnp.int32, (8, NZ), 1)
    row = lax.broadcasted_iota(jnp.int32, (8, NZ), 0)
    packed = jnp.zeros((8, NZ), F32)
    for b in range(BLOCKS):
        rows = gram[8 * b:8 * b + 8]
        turned = jnp.where(lane % 8 < 4, lane_roll(rows, -4), -lane_roll(rows, 4))
        both = rows + pltpu.roll(turned, 4, 0)
        half, start = SLOTS[b]
        moved = lane_roll(both, start - 8 * b)
        if half:
            moved = pltpu.roll(moved, 4, 0)
        keep = (lane >= start) & (lane < start + 8 * (BLOCKS - b)) & (row // 4 == half)
        packed = packed + jnp.where(keep, moved, 0.0)
    return packed


def unpack_gram(packed):
    lane = lax.broadcasted_iota(jnp.int32, (8, NZ), 1)
    row = lax.broadcasted_iota(jnp.int32, (8, NZ), 0)
    rows = []
    for b in range(BLOCKS):
        half, start = SLOTS[b]
        moved = lane_roll(packed, 8 * b - start)
        if half:
            moved = pltpu.roll(moved, 4, 0)
        keep = (lane >= 8 * b) & (lane < 8 * BLOCKS) & (row < 4)
        moved = jnp.where(keep, moved, 0.0)
        turned = jnp.where(lane % 8 < 4, -lane_roll(moved, -4), lane_roll(moved, 4))
        rows.append(moved + pltpu.roll(turned, 4, 0))
    rows.append(jnp.zeros((NZ - 8 * BLOCKS, NZ), F32))
    upper = jnp.concatenate(rows, axis=0)
    tall = lax.broadcasted_iota(jnp.int32, (NZ, NZ), 0)
    wide = lax.broadcasted_iota(jnp.int32, (NZ, NZ), 1)
    return jnp.where(tall // 8 <= wide // 8, upper, upper.T)


def gram_kernel(peers, w, coef, start, old_image, w_image, out,
                first, second, table_re, table_im, diag_re, diag_im):
    fill_tables(coef, FAR - NEAR, table_re, table_im, diag_re, diag_im)

    def store(x, y, value):
        w_image[x, pl.ds(y * 8, 8), :] = value

    smooth(w, coef, FAR - NEAR, 0, table_re, table_im, first, second, store)

    def plane(x, total):
        stacked = jnp.concatenate(split3(basis_plane(start, w, old_image, w_image, x)), axis=0)
        return total + lax.dot_general(stacked, stacked, (((1,), (1,)), ((), ())), preferred_element_type=F32)

    total = lax.fori_loop(0, LX, plane, jnp.zeros((3 * ROWS, 3 * ROWS), F32))
    tall = total[0:ROWS] + total[ROWS:2 * ROWS] + total[2 * ROWS:3 * ROWS]
    gram = tall[:, 0:ROWS] + tall[:, ROWS:2 * ROWS] + tall[:, 2 * ROWS:3 * ROWS]
    gram = jnp.concatenate([gram, jnp.zeros((ROWS, NZ - ROWS), F32)], axis=1)
    packed = pack_gram(gram)
    for peer in range(peers):
        out[peer] = packed


def image_and_gram(peers, *args):
    return pl.pallas_call(
        functools.partial(gram_kernel, peers),
        out_shape=(jax.ShapeDtypeStruct((LX, LY * 8, NZ), F32),
                   jax.ShapeDtypeStruct((peers, 8, NZ), F32)),
        in_specs=[VMEM] * 4,
        out_specs=(VMEM, VMEM),
        scratch_shapes=smooth_scratch(NEAR)[1:],
        compiler_params=pltpu.CompilerParams(vmem_limit_bytes=32 << 20),
        name="image_and_gram",
    )(*args)


def sum_kernel(parts, out):
    total = jnp.sum(parts[...], axis=0)
    for peer in range(out.shape[0]):
        out[peer] = total


def sum_and_spread(parts, peers):
    return pl.pallas_call(
        sum_kernel,
        out_shape=jax.ShapeDtypeStruct((peers, 8, NZ), F32),
        in_specs=[VMEM],
        out_specs=VMEM,
        compiler_params=pltpu.CompilerParams(vmem_limit_bytes=1 << 20),
        name="sum_and_spread",
    )(parts)


def mul(left, right):
    return lax.dot_general(left, right, (((1,), (0,)), ((), ())), precision=HIGHEST, preferred_element_type=F32)


def mul_t(left, right):
    return lax.dot_general(left, right, (((1,), (1,)), ((), ())), precision=HIGHEST, preferred_element_type=F32)


def inverse_factor(gram):
    lane = lax.broadcasted_iota(jnp.int32, (8, NZ), 1)
    row = lax.broadcasted_iota(jnp.int32, (8, NZ), 0)
    work = jnp.where(lane < 8, gram, jnp.where(lane == row + 8, 1.0, 0.0))
    rank = 2 * (row % 4) + row // 4
    for step in range(8):
        k = (step % 2) * 4 + step // 2
        line = work[k:k + 1, :]
        pivot = line[:, k:k + 1]
        column = work[:, k:k + 1]
        root = 1.0 / jnp.sqrt(pivot)
        line = line * root
        factor = column * root
        work = jnp.where(rank > step, work - factor * line, jnp.where(rank == step, line, work))
    return jnp.where(lane < 8, lane_roll(work, -8), 0.0)


def coefficients(gram):
    lane = lax.broadcasted_iota(jnp.int32, (8, NZ), 1)
    row = lax.broadcasted_iota(jnp.int32, (8, NZ), 0)
    tall = lax.broadcasted_iota(jnp.int32, (NZ, NZ), 0)
    wide = lax.broadcasted_iota(jnp.int32, (NZ, NZ), 1)

    def normalise(rows):
        small = mul_t(mul(rows, gram), rows_in(rows))
        return mul(inverse_factor(small)[:, 0:8], rows)

    def rows_in(rows):
        return jnp.concatenate([rows, jnp.zeros((NZ - 8, NZ), F32)], axis=0)

    once = jnp.where(lane < 24, gram[24:32], 0.0)
    again = jnp.where(lane < 24, mul(once, gram), 0.0)
    fresh = jnp.where(lane == row + 24, 1.0, 0.0)
    new = normalise(fresh - (2.0 * once - again))
    image = (jnp.where((lane >= 32) & (lane < 48), lane_roll(new, 32), 0.0)
             + jnp.where((lane >= 24) & (lane < 32), lane_roll(new, 8), 0.0)
             + jnp.where((lane >= 48) & (lane < 56), lane_roll(new, 24), 0.0))
    window = jnp.where((tall < 16) & (wide == tall + 8), 1.0, 0.0)
    window = jnp.concatenate([window[0:16], new, window[24:]], axis=0)

    def project(rows):
        return mul(mul_t(mul(rows, gram), window), window)

    once = project(image)
    again = project(once)
    newest = normalise(image - (2.0 * once - again))
    return new, newest


def final_kernel(cells, parts, start, w, old_image, w_image, out):
    gram = unpack_gram(jnp.sum(parts[...], axis=0) * (1.0 / cells))
    new, newest = coefficients(gram)
    mapping = jnp.concatenate([new, newest], axis=0)[:, 0:ROWS]
    pieces = [jnp.concatenate([piece] * 3, axis=1) for piece in split3(mapping)]
    stacked_map = jnp.concatenate(pieces, axis=0)

    def plane(x, carry):
        stacked = jnp.concatenate(split3(basis_plane(start, w, old_image, w_image, x)), axis=0)
        full = lax.dot_general(stacked_map, stacked, (((1,), (0,)), ((), ())), preferred_element_type=F32)
        result = full[32:48] + full[16:32] + full[0:16]
        for k in range(2):
            tiles = jnp.stack([result[8 * k:8 * k + 8, y * NZ:(y + 1) * NZ] for y in range(LY)])
            out[k, :, x] = jnp.swapaxes(tiles, 0, 1)
        return carry

    lax.fori_loop(0, LX, plane, 0)


def finish(cells, *args):
    return pl.pallas_call(
        functools.partial(final_kernel, cells),
        out_shape=jax.ShapeDtypeStruct((2, 8, LX, LY, NZ), F32),
        in_specs=[VMEM] * 5,
        out_specs=VMEM,
        compiler_params=pltpu.CompilerParams(vmem_limit_bytes=32 << 20),
        name="finish",
    )(*args)


GX = ("z", "core")


def from_both(axis, count, to_higher, to_lower, step=1):
    return (
        lax.ppermute(to_higher, axis, [(i, i + step) for i in range(count - step)]),
        lax.ppermute(to_lower, axis, [(i + step, i) for i in range(count - step)]),
    )


def per_device(nx, ny, nz, prior, coefficient):
    cells = coefficient.size * nx * ny
    by_cell = prior.transpose(3, 0, 4, 1, 2, 5).reshape(LX, 3 * LY * 8, NZ)
    start = jnp.concatenate([by_cell, coefficient], axis=1)
    far = start[:, 2 * BLOCK:]
    sides = from_both(GX, nx, start, start) + from_both(GX, nx, far, far, 2)
    up, down, old_up, old_down = pack_rims(start, *sides)
    rims = from_both("gy", ny, up, down)
    old_rims = from_both("gy", ny, old_up, old_down)
    old_image, coef = old_images(start, *sides, *old_rims)
    w = first_image(coef, start, *sides, *rims, *old_rims)

    w_image, spread = image_and_gram(2 * ny, w, coef, start, old_image)
    got = lax.all_to_all(spread, ("core", "gy"), 0, 0)
    got = lax.all_to_all(sum_and_spread(got, nz), "z", 0, 0)
    out = finish(cells, got, start, w, old_image, w_image)
    return out.reshape(2, 2, 4, LX, LY, NZ)


def solution(mesh):
    nx, ny = mesh.shape["gx"], mesh.shape["gy"]
    fine = Mesh(np.asarray(mesh.devices).reshape(nx // 2, 2, ny), ("z", "core", "gy"))
    in_specs = (P(None, None, None, GX, "gy", None), P(GX, "gy", None))
    out_specs = P(None, None, None, GX, "gy", None)
    return jax.shard_map(
        functools.partial(per_device, nx, ny, nx // 2),
        mesh=fine, in_specs=in_specs, out_specs=out_specs, check_vma=False,
    )
```

```python
import functools

import jax
import jax.numpy as jnp
import numpy as np
from jax import lax
from jax.experimental import pallas as pl
from jax.experimental.pallas import tpu as pltpu
from jax.sharding import Mesh, PartitionSpec as P

LX, LY, NZ = 4, 8, 128
NEAR, FAR = 4, 8
BLOCKS = 7
ROWS = 64
F32 = jnp.float32
BF16 = jnp.bfloat16
HIGHEST = lax.Precision.HIGHEST
VMEM = pl.BlockSpec(memory_space=pltpu.VMEM)


BLOCK = LY * 8
HALF = NEAR * 8


def spans(halo, begin, end):
    found, place = [], 0
    for d in range(begin + 1, end + 1):
        found.append((d, halo - d, place))
        place += LY + 2 * (halo - d)
    return found, place


OLD_SPANS, OLD_SIZE = spans(NEAR, 0, LX)
SIDE_SPANS, SIDE_SIZE = spans(FAR, 0, LX)
FAR_SPANS, FAR_SIZE = spans(FAR, LX, 2 * LX)
SIDE_TILES = 2 * OLD_SIZE + SIDE_SIZE + -(-SIDE_SIZE // 8)
FAR_TILES = FAR_SIZE + -(-FAR_SIZE // 8)


def pack_columns(out, start, found, to_higher, rows, reach):
    (below, low_row), (own, own_row), (above, high_row) = rows
    for d, more, place in found:
        x = LX - 1 - (d - 1) % LX if to_higher else (d - 1) % LX
        spot = start + place
        size = more * 8
        if more:
            out[pl.ds(spot, more)] = below[x, pl.ds(low_row + reach * 8 - size, size), :].reshape(more, 8, NZ)
            out[pl.ds(spot + more + LY, more)] = above[x, pl.ds(high_row, size), :].reshape(more, 8, NZ)
        out[pl.ds(spot + more, LY)] = own[x, pl.ds(own_row, BLOCK), :].reshape(LY, 8, NZ)


def pack_coefficient(out, start, found, to_higher, below, own, above):
    for d, more, place in found:
        x = LX - 1 - (d - 1) % LX if to_higher else (d - 1) % LX
        for y in range(-more, LY + more):
            if y < 0:
                ref, row = below, 2 * HALF + BLOCK + LY + y
            elif y < LY:
                ref, row = own, 3 * BLOCK + y
            else:
                ref, row = above, 2 * HALF + BLOCK + y - LY
            spot = place + more + y
            out[start + spot // 8, pl.ds(spot % 8, 1), :] = ref[x, pl.ds(row, 1), :]


def column_kernel(own, below, above, *outs):
    for out, to_higher, found, size in (
        (outs[0], True, SIDE_SPANS, SIDE_SIZE),
        (outs[1], False, SIDE_SPANS, SIDE_SIZE),
        (outs[2], True, FAR_SPANS, FAR_SIZE),
        (outs[3], False, FAR_SPANS, FAR_SIZE),
    ):
        start = 0
        if found is SIDE_SPANS:
            for group in range(2):
                rows = [(below, group * HALF), (own, group * BLOCK), (above, group * HALF)]
                pack_columns(out, start, OLD_SPANS, to_higher, rows, NEAR)
                start += OLD_SIZE
        rows = [(below, 2 * HALF), (own, 2 * BLOCK), (above, 2 * HALF)]
        pack_columns(out, start, found, to_higher, rows, FAR)
        if size % 8:
            out[out.shape[0] - 1] = jnp.zeros((8, NZ), F32)
        pack_coefficient(out, start + size, found, to_higher, below, own, above)


def pack_all(*args):
    shapes = tuple(jax.ShapeDtypeStruct((size, 8, NZ), F32) for size in [SIDE_TILES] * 2 + [FAR_TILES] * 2)
    return pl.pallas_call(
        column_kernel,
        out_shape=shapes,
        in_specs=[VMEM] * 3,
        out_specs=(VMEM,) * 4,
        compiler_params=pltpu.CompilerParams(vmem_limit_bytes=1 << 20),
        name="pack_all",
    )(*args)


def fill_block(wide, halo, rows, reach, sides):
    (below, low_row), (own, own_row), (above, high_row) = rows
    wide[...] = jnp.zeros(wide.shape, F32)
    for x in range(LX):
        size = halo * 8
        wide[halo + x, 0:halo] = below[x, pl.ds(low_row + reach * 8 - size, size), :].reshape(halo, 8, NZ)
        wide[halo + x, halo:halo + LY] = own[x, pl.ds(own_row, BLOCK), :].reshape(LY, 8, NZ)
        wide[halo + x, halo + LY:] = above[x, pl.ds(high_row, size), :].reshape(halo, 8, NZ)
    for low, high, start, found in sides:
        for d, more, place in found:
            count = LY + 2 * more
            begin = halo - more
            wide[halo - d, begin:begin + count] = low[pl.ds(start + place, count)]
            wide[halo + LX - 1 + d, begin:begin + count] = high[pl.ds(start + place, count)]


def fill_flat(wide, below, own, above, sides):
    wide[...] = jnp.zeros(wide.shape, F32)
    for x in range(LX):
        wide[FAR + x, 0:FAR] = below[x, pl.ds(2 * HALF + BLOCK, LY), :]
        wide[FAR + x, FAR:FAR + LY] = own[x, pl.ds(3 * BLOCK, LY), :]
        wide[FAR + x, FAR + LY:] = above[x, pl.ds(2 * HALF + BLOCK, LY), :]
    for low, high, start, found in sides:
        for d, more, place in found:
            for i in range(LY + 2 * more):
                tile, row = start + (place + i) // 8, (place + i) % 8
                y = FAR - more + i
                wide[FAR - d, pl.ds(y, 1), :] = low[tile, pl.ds(row, 1), :]
                wide[FAR + LX - 1 + d, pl.ds(y, 1), :] = high[tile, pl.ds(row, 1), :]


def fill_tables(coef, skip, table_re, table_im, diag_re, diag_im):
    value = coef[...]
    real = 6.0 - value
    imag = 0.5 * value
    scale = jnp.where(value > 0.0, 0.8 / (real * real + imag * imag), 0.0)
    diag_re[...] = real * scale
    diag_im[...] = imag * scale
    sign = jnp.where(lax.broadcasted_iota(jnp.int32, (8, NZ), 0) < 4, 1.0, -1.0)
    size_x, size_y = table_re.shape[:2]

    def body(x, carry):
        for y in range(size_y):
            spot = pl.ds(y + skip, 1)
            table_re[x, y] = jnp.broadcast_to(diag_re[x + skip, spot, :], (8, NZ))
            table_im[x, y] = jnp.broadcast_to(diag_im[x + skip, spot, :], (8, NZ)) * sign
        return carry

    lax.fori_loop(0, size_x, body, 0)


def depth_sum(value):
    lane = lax.broadcasted_iota(jnp.int32, value.shape, 1)
    above = jnp.where(lane == 0, 0.0, pltpu.roll(value, 1, 1))
    below = jnp.where(lane == NZ - 1, 0.0, pltpu.roll(value, NZ - 1, 1))
    return above + below


def smooth(block, coef, skip, reach, table_re, table_im, first, second, store):
    size_x, size_y = block.shape[:2]

    def solve(value, x, y):
        return table_re[x, y] * value + table_im[x, y] * pltpu.roll(value, 4, 0)

    def sections(k):
        low, high = k, size_y - k
        if reach == 0:
            return [((k, size_x - k), (low, high))]
        return [((k, 4), (low + 5, high - 5)), ((4, size_x - 4), (low, high)),
                ((size_x - 4, size_x - k), (low + 5, high - 5))]

    def planes(k, body):
        for (begin, end), (low, high) in sections(k):
            if begin < end:
                lax.fori_loop(begin, end, functools.partial(body, low, high), 0)

    def start(low, high, x, carry):
        for y in range(low, high):
            first[x, y] = solve(block[x, y], x, y)
        return carry

    def around(ref, x, low, high):
        line = [ref[x, y] for y in range(low - 1, high + 1)]
        for y in range(low, high):
            mid = line[y - low + 1]
            total = ref[x - 1, y] + ref[x + 1, y] + line[y - low] + line[y - low + 2]
            yield y, mid, total + depth_sum(mid)

    if reach:
        first[...] = jnp.zeros(first.shape, F32)
        second[...] = jnp.zeros(second.shape, F32)
    planes(0, start)
    here, there = first, second
    for k in range(1, 4):
        def sweep(low, high, x, carry, here=here, there=there):
            for y, mid, total in around(here, x, low, high):
                there[x, y] = 0.2 * mid + solve(block[x, y] + total, x, y)
            return carry

        planes(k, sweep)
        here, there = there, here

    def image(x, carry):
        for y, mid, total in around(here, x, 4, size_y - 4):
            diag = 6.0 - coef[x + skip, pl.ds(y + skip, 1), :]
            store(x - 4, y - 4, diag * mid - total)
        return carry

    lax.fori_loop(4, size_x - 4, image, 0)


def wide_shape(halo):
    return (LX + 2 * halo, LY + 2 * halo)


FLAT = pltpu.VMEM((*wide_shape(FAR), NZ), F32)


def smooth_scratch(halo):
    return [pltpu.VMEM((*wide_shape(halo), 8, NZ), F32)] * 5 + [FLAT] * 2


def side_coefficient(low, high):
    return (low, high, 2 * OLD_SIZE + SIDE_SIZE, SIDE_SPANS)


def old_kernel(own, below, above, low, high, out, block, first, second,
               table_re, table_im, diag_re, diag_im, coef):
    fill_flat(coef, below, own, above, [side_coefficient(low, high)])
    fill_tables(coef, FAR - NEAR, table_re, table_im, diag_re, diag_im)
    for group in range(2):
        rows = [(below, group * HALF), (own, group * BLOCK), (above, group * HALF)]
        fill_block(block, NEAR, rows, NEAR, [(low, high, group * OLD_SIZE, OLD_SPANS)])

        def store(x, y, value, group=group):
            out[x, pl.ds(group * BLOCK + y * 8, 8), :] = value

        smooth(block, coef, FAR - NEAR, 0, table_re, table_im, first, second, store)


def old_images(*args):
    return pl.pallas_call(
        old_kernel,
        out_shape=jax.ShapeDtypeStruct((LX, 2 * BLOCK, NZ), F32),
        in_specs=[VMEM] * 5,
        out_specs=VMEM,
        scratch_shapes=smooth_scratch(NEAR) + [FLAT],
        compiler_params=pltpu.CompilerParams(vmem_limit_bytes=16 << 20),
        cost_estimate=pl.CostEstimate(flops=12_000_000, bytes_accessed=24_000_000, transcendentals=0),
        name="old_images",
    )(*args)


def first_kernel(own, below, above, low, high, far_low, far_high, after, out, coef, block, first, second,
                 table_re, table_im, diag_re, diag_im):
    del after
    fill_flat(coef, below, own, above, [side_coefficient(low, high), (far_low, far_high, FAR_SIZE, FAR_SPANS)])
    fill_tables(coef, 0, table_re, table_im, diag_re, diag_im)
    rows = [(below, 2 * HALF), (own, 2 * BLOCK), (above, 2 * HALF)]
    fill_block(block, FAR, rows, FAR,
               [(low, high, 2 * OLD_SIZE, SIDE_SPANS), (far_low, far_high, 0, FAR_SPANS)])

    def store(x, y, value):
        out[x, y] = value

    smooth(block, coef, 0, NEAR, table_re, table_im, first, second, store)


def first_image(*args):
    return pl.pallas_call(
        first_kernel,
        out_shape=(jax.ShapeDtypeStruct((*wide_shape(NEAR), 8, NZ), F32),
                   jax.ShapeDtypeStruct((*wide_shape(FAR), NZ), F32)),
        in_specs=[VMEM] * 7 + [pl.BlockSpec(memory_space=pl.ANY)],
        out_specs=(VMEM, VMEM),
        scratch_shapes=smooth_scratch(FAR),
        compiler_params=pltpu.CompilerParams(vmem_limit_bytes=24 << 20),
        name="first_image",
    )(*args)


def split3(value):
    high = value.astype(BF16)
    rest = value - high.astype(F32)
    middle = rest.astype(BF16)
    low = (rest - middle.astype(F32)).astype(BF16)
    return high, middle, low


def basis_plane(start, w, old_image, w_image, x):
    refs = [(start, 0), (start, LY), (start, 2 * LY), (w, None), (old_image, 0), (old_image, LY), (w_image, 0)]
    rows = []
    for ref, first in refs:
        if first is None:
            tiles = [ref[x + NEAR, NEAR + y] for y in range(LY)]
        else:
            tiles = [ref[x, pl.ds((first + y) * 8, 8), :] for y in range(LY)]
        rows.append(jnp.concatenate(tiles, axis=1))
    rows.append(jnp.zeros((8, LY * NZ), F32))
    return jnp.concatenate(rows, axis=0)


def lane_roll(value, amount):
    return pltpu.roll(value, amount % NZ, 1)


SLOTS = [(0, 0), (0, 56), (1, 0), (1, 40), (1, 72), (1, 96), (0, 104)]


def pack_gram(gram):
    lane = lax.broadcasted_iota(jnp.int32, (8, NZ), 1)
    row = lax.broadcasted_iota(jnp.int32, (8, NZ), 0)
    packed = jnp.zeros((8, NZ), F32)
    for b in range(BLOCKS):
        rows = gram[8 * b:8 * b + 8]
        turned = jnp.where(lane % 8 < 4, lane_roll(rows, -4), -lane_roll(rows, 4))
        both = rows + pltpu.roll(turned, 4, 0)
        half, start = SLOTS[b]
        moved = lane_roll(both, start - 8 * b)
        if half:
            moved = pltpu.roll(moved, 4, 0)
        keep = (lane >= start) & (lane < start + 8 * (BLOCKS - b)) & (row // 4 == half)
        packed = packed + jnp.where(keep, moved, 0.0)
    return packed


def unpack_gram(packed):
    lane = lax.broadcasted_iota(jnp.int32, (8, NZ), 1)
    row = lax.broadcasted_iota(jnp.int32, (8, NZ), 0)
    rows = []
    for b in range(BLOCKS):
        half, start = SLOTS[b]
        moved = lane_roll(packed, 8 * b - start)
        if half:
            moved = pltpu.roll(moved, 4, 0)
        keep = (lane >= 8 * b) & (lane < 8 * BLOCKS) & (row < 4)
        moved = jnp.where(keep, moved, 0.0)
        turned = jnp.where(lane % 8 < 4, -lane_roll(moved, -4), lane_roll(moved, 4))
        rows.append(moved + pltpu.roll(turned, 4, 0))
    rows.append(jnp.zeros((NZ - 8 * BLOCKS, NZ), F32))
    upper = jnp.concatenate(rows, axis=0)
    tall = lax.broadcasted_iota(jnp.int32, (NZ, NZ), 0)
    wide = lax.broadcasted_iota(jnp.int32, (NZ, NZ), 1)
    return jnp.where(tall // 8 <= wide // 8, upper, upper.T)


def gram_kernel(peers, w, coef, start, old_image, w_image, out,
                first, second, table_re, table_im, diag_re, diag_im):
    fill_tables(coef, FAR - NEAR, table_re, table_im, diag_re, diag_im)

    def store(x, y, value):
        w_image[x, pl.ds(y * 8, 8), :] = value

    smooth(w, coef, FAR - NEAR, 0, table_re, table_im, first, second, store)

    def plane(x, total):
        stacked = jnp.concatenate(split3(basis_plane(start, w, old_image, w_image, x)), axis=0)
        return total + lax.dot_general(stacked, stacked, (((1,), (1,)), ((), ())), preferred_element_type=F32)

    total = lax.fori_loop(0, LX, plane, jnp.zeros((3 * ROWS, 3 * ROWS), F32))
    tall = total[0:ROWS] + total[ROWS:2 * ROWS] + total[2 * ROWS:3 * ROWS]
    gram = tall[:, 0:ROWS] + tall[:, ROWS:2 * ROWS] + tall[:, 2 * ROWS:3 * ROWS]
    gram = jnp.concatenate([gram, jnp.zeros((ROWS, NZ - ROWS), F32)], axis=1)
    packed = pack_gram(gram)
    for peer in range(peers):
        out[peer] = packed


def image_and_gram(peers, *args):
    return pl.pallas_call(
        functools.partial(gram_kernel, peers),
        out_shape=(jax.ShapeDtypeStruct((LX, LY * 8, NZ), F32),
                   jax.ShapeDtypeStruct((peers, 8, NZ), F32)),
        in_specs=[VMEM] * 4,
        out_specs=(VMEM, VMEM),
        scratch_shapes=smooth_scratch(NEAR)[1:],
        compiler_params=pltpu.CompilerParams(vmem_limit_bytes=32 << 20),
        name="image_and_gram",
    )(*args)


def sum_kernel(parts, out):
    total = jnp.sum(parts[...], axis=0)
    for peer in range(out.shape[0]):
        out[peer] = total


def sum_and_spread(parts, peers):
    return pl.pallas_call(
        sum_kernel,
        out_shape=jax.ShapeDtypeStruct((peers, 8, NZ), F32),
        in_specs=[VMEM],
        out_specs=VMEM,
        compiler_params=pltpu.CompilerParams(vmem_limit_bytes=1 << 20),
        name="sum_and_spread",
    )(parts)


def mul(left, right):
    return lax.dot_general(left, right, (((1,), (0,)), ((), ())), precision=HIGHEST, preferred_element_type=F32)


def mul_t(left, right):
    return lax.dot_general(left, right, (((1,), (1,)), ((), ())), precision=HIGHEST, preferred_element_type=F32)


def inverse_factor(gram):
    lane = lax.broadcasted_iota(jnp.int32, (8, NZ), 1)
    row = lax.broadcasted_iota(jnp.int32, (8, NZ), 0)
    work = jnp.where(lane < 8, gram, jnp.where(lane == row + 8, 1.0, 0.0))
    rank = 2 * (row % 4) + row // 4
    for step in range(8):
        k = (step % 2) * 4 + step // 2
        line = work[k:k + 1, :]
        pivot = line[:, k:k + 1]
        column = work[:, k:k + 1]
        root = 1.0 / jnp.sqrt(pivot)
        line = line * root
        factor = column * root
        work = jnp.where(rank > step, work - factor * line, jnp.where(rank == step, line, work))
    return jnp.where(lane < 8, lane_roll(work, -8), 0.0)


def coefficients(gram):
    lane = lax.broadcasted_iota(jnp.int32, (8, NZ), 1)
    row = lax.broadcasted_iota(jnp.int32, (8, NZ), 0)
    tall = lax.broadcasted_iota(jnp.int32, (NZ, NZ), 0)
    wide = lax.broadcasted_iota(jnp.int32, (NZ, NZ), 1)

    def normalise(rows):
        small = mul_t(mul(rows, gram), rows_in(rows))
        return mul(inverse_factor(small)[:, 0:8], rows)

    def rows_in(rows):
        return jnp.concatenate([rows, jnp.zeros((NZ - 8, NZ), F32)], axis=0)

    once = jnp.where(lane < 24, gram[24:32], 0.0)
    again = jnp.where(lane < 24, mul(once, gram), 0.0)
    fresh = jnp.where(lane == row + 24, 1.0, 0.0)
    new = normalise(fresh - (2.0 * once - again))
    image = (jnp.where((lane >= 32) & (lane < 48), lane_roll(new, 32), 0.0)
             + jnp.where((lane >= 24) & (lane < 32), lane_roll(new, 8), 0.0)
             + jnp.where((lane >= 48) & (lane < 56), lane_roll(new, 24), 0.0))
    window = jnp.where((tall < 16) & (wide == tall + 8), 1.0, 0.0)
    window = jnp.concatenate([window[0:16], new, window[24:]], axis=0)

    def project(rows):
        return mul(mul_t(mul(rows, gram), window), window)

    once = project(image)
    again = project(once)
    newest = normalise(image - (2.0 * once - again))
    return new, newest


def final_kernel(cells, parts, start, w, old_image, w_image, out):
    gram = unpack_gram(jnp.sum(parts[...], axis=0) * (1.0 / cells))
    new, newest = coefficients(gram)
    mapping = jnp.concatenate([new, newest], axis=0)[:, 0:ROWS]
    pieces = [jnp.concatenate([piece] * 3, axis=1) for piece in split3(mapping)]
    stacked_map = jnp.concatenate(pieces, axis=0)

    def plane(x, carry):
        stacked = jnp.concatenate(split3(basis_plane(start, w, old_image, w_image, x)), axis=0)
        full = lax.dot_general(stacked_map, stacked, (((1,), (0,)), ((), ())), preferred_element_type=F32)
        result = full[32:48] + full[16:32] + full[0:16]
        for k in range(2):
            tiles = jnp.stack([result[8 * k:8 * k + 8, y * NZ:(y + 1) * NZ] for y in range(LY)])
            out[k, :, x] = jnp.swapaxes(tiles, 0, 1)
        return carry

    lax.fori_loop(0, LX, plane, 0)


def finish(cells, *args):
    return pl.pallas_call(
        functools.partial(final_kernel, cells),
        out_shape=jax.ShapeDtypeStruct((2, 8, LX, LY, NZ), F32),
        in_specs=[VMEM] * 5,
        out_specs=VMEM,
        compiler_params=pltpu.CompilerParams(vmem_limit_bytes=32 << 20),
        name="finish",
    )(*args)


GX = ("z", "core")


def from_both(axis, count, to_higher, to_lower, step=1):
    return (
        lax.ppermute(to_higher, axis, [(i, i + step) for i in range(count - step)]),
        lax.ppermute(to_lower, axis, [(i + step, i) for i in range(count - step)]),
    )


def per_device(nx, ny, nz, prior, coefficient):
    cells = coefficient.size * nx * ny
    by_cell = prior.transpose(3, 0, 4, 1, 2, 5).reshape(LX, 3 * LY * 8, NZ)
    start = jnp.concatenate([by_cell, coefficient], axis=1)
    up = jnp.concatenate([start[:, HALF:BLOCK], start[:, BLOCK + HALF:]], axis=1)
    down = jnp.concatenate([start[:, :HALF], start[:, BLOCK:BLOCK + HALF], start[:, 2 * BLOCK:]], axis=1)
    rims = from_both("gy", ny, up, down)
    right, left, far_right, far_left = pack_all(start, *rims)
    sides = from_both(GX, nx, right, left)
    far_sides = from_both(GX, nx, far_right, far_left, 2)
    old_image = old_images(start, *rims, *sides)
    w, coef = first_image(start, *rims, *sides, *far_sides, old_image)

    w_image, spread = image_and_gram(2 * ny, w, coef, start, old_image)
    got = lax.all_to_all(spread, ("core", "gy"), 0, 0)
    got = lax.all_to_all(sum_and_spread(got, nz), "z", 0, 0)
    out = finish(cells, got, start, w, old_image, w_image)
    return out.reshape(2, 2, 4, LX, LY, NZ)


def solution(mesh):
    nx, ny = mesh.shape["gx"], mesh.shape["gy"]
    fine = Mesh(np.asarray(mesh.devices).reshape(nx // 2, 2, ny), ("z", "core", "gy"))
    in_specs = (P(None, None, None, GX, "gy", None), P(GX, "gy", None))
    out_specs = P(None, None, None, GX, "gy", None)
    return jax.shard_map(
        functools.partial(per_device, nx, ny, nx // 2),
        mesh=fine, in_specs=in_specs, out_specs=out_specs, check_vma=False,
    )
```

```python
import functools

import jax
import jax.numpy as jnp
import numpy as np
from jax import lax
from jax.experimental import pallas as pl
from jax.experimental.pallas import tpu as pltpu
from jax.sharding import Mesh, PartitionSpec as P

LX, LY, NZ = 4, 8, 128
NEAR, FAR = 4, 8
BLOCKS = 7
ROWS = 64
F32 = jnp.float32
BF16 = jnp.bfloat16
HIGHEST = lax.Precision.HIGHEST
VMEM = pl.BlockSpec(memory_space=pltpu.VMEM)


BLOCK = LY * 8
HALF = NEAR * 8


def spans(halo, begin, end):
    found, place = [], 0
    for d in range(begin + 1, end + 1):
        found.append((d, halo - d, place))
        place += LY + 2 * (halo - d)
    return found, place


NEAR_SPANS, NEAR_SIZE = spans(NEAR, 0, LX)
SIDE_SPANS, SIDE_SIZE = spans(FAR, 0, LX)
FLAT_TILES = -(-SIDE_SIZE // 8)
SPLIT = NEAR_SPANS[-1][2]
FIRST_TILES = SIDE_SIZE + FLAT_TILES + NEAR_SIZE - SPLIT
SECOND_TILES = SPLIT + NEAR_SIZE


def pack_columns(out, start, found, to_higher, rows, reach):
    (below, low_row), (own, own_row), (above, high_row) = rows
    for d, more, place in found:
        x = LX - 1 - (d - 1) % LX if to_higher else (d - 1) % LX
        spot = start + place
        size = more * 8
        if more:
            out[pl.ds(spot, more)] = below[x, pl.ds(low_row + reach * 8 - size, size), :].reshape(more, 8, NZ)
            out[pl.ds(spot + more + LY, more)] = above[x, pl.ds(high_row, size), :].reshape(more, 8, NZ)
        out[pl.ds(spot + more, LY)] = own[x, pl.ds(own_row, BLOCK), :].reshape(LY, 8, NZ)


def pack_coefficient(out, start, found, to_higher, below, own, above):
    for d, more, place in found:
        x = LX - 1 - (d - 1) % LX if to_higher else (d - 1) % LX
        for y in range(-more, LY + more):
            if y < 0:
                ref, row = below, 2 * HALF + BLOCK + LY + y
            elif y < LY:
                ref, row = own, 3 * BLOCK + y
            else:
                ref, row = above, 2 * HALF + BLOCK + y - LY
            spot = place + more + y
            out[start + spot // 8, pl.ds(spot % 8, 1), :] = ref[x, pl.ds(row, 1), :]


def column_kernel(own, below, above, right, left, old_right, old_left):
    for first, second, to_higher in ((right, old_right, True), (left, old_left, False)):
        rows = [(below, 2 * HALF), (own, 2 * BLOCK), (above, 2 * HALF)]
        pack_columns(first, 0, SIDE_SPANS, to_higher, rows, FAR)
        if SIDE_SIZE % 8:
            first[SIDE_SIZE + FLAT_TILES - 1] = jnp.zeros((8, NZ), F32)
        pack_coefficient(first, SIDE_SIZE, SIDE_SPANS, to_higher, below, own, above)
        rows = [(below, 0), (own, 0), (above, 0)]
        pack_columns(second, 0, NEAR_SPANS[:-1], to_higher, rows, NEAR)
        pack_columns(first, SIDE_SIZE + FLAT_TILES - SPLIT, NEAR_SPANS[-1:], to_higher, rows, NEAR)
        rows = [(below, HALF), (own, BLOCK), (above, HALF)]
        pack_columns(second, SPLIT, NEAR_SPANS, to_higher, rows, NEAR)


def pack_all(*args):
    shapes = tuple(jax.ShapeDtypeStruct((size, 8, NZ), F32) for size in [FIRST_TILES] * 2 + [SECOND_TILES] * 2)
    return pl.pallas_call(
        column_kernel,
        out_shape=shapes,
        in_specs=[VMEM] * 3,
        out_specs=(VMEM,) * 4,
        compiler_params=pltpu.CompilerParams(vmem_limit_bytes=1 << 20),
        name="pack_all",
    )(*args)


def fill_sides(wide, halo, sides):
    for low, high, start, found in sides:
        for d, more, place in found:
            count = LY + 2 * more
            begin = halo - more
            wide[NEAR - d, begin:begin + count] = low[pl.ds(start + place, count)]
            wide[NEAR + LX - 1 + d, begin:begin + count] = high[pl.ds(start + place, count)]


def fill_block(wide, halo, rows, reach, sides):
    (below, low_row), (own, own_row), (above, high_row) = rows
    wide[...] = jnp.zeros(wide.shape, F32)
    for x in range(LX):
        size = halo * 8
        wide[NEAR + x, 0:halo] = below[x, pl.ds(low_row + reach * 8 - size, size), :].reshape(halo, 8, NZ)
        wide[NEAR + x, halo:halo + LY] = own[x, pl.ds(own_row, BLOCK), :].reshape(LY, 8, NZ)
        wide[NEAR + x, halo + LY:] = above[x, pl.ds(high_row, size), :].reshape(halo, 8, NZ)
    fill_sides(wide, halo, sides)


def fill_flat(wide, below, own, above, low, high):
    wide[...] = jnp.zeros(wide.shape, F32)
    for x in range(LX):
        wide[NEAR + x, 0:FAR] = below[x, pl.ds(2 * HALF + BLOCK, LY), :]
        wide[NEAR + x, FAR:FAR + LY] = own[x, pl.ds(3 * BLOCK, LY), :]
        wide[NEAR + x, FAR + LY:] = above[x, pl.ds(2 * HALF + BLOCK, LY), :]
    for d, more, place in SIDE_SPANS:
        for i in range(LY + 2 * more):
            tile, row = SIDE_SIZE + (place + i) // 8, (place + i) % 8
            y = FAR - more + i
            wide[NEAR - d, pl.ds(y, 1), :] = low[tile, pl.ds(row, 1), :]
            wide[NEAR + LX - 1 + d, pl.ds(y, 1), :] = high[tile, pl.ds(row, 1), :]


def fill_tables(coef, skip, table_re, table_im, diag_re, diag_im):
    value = coef[...]
    real = 6.0 - value
    imag = 0.5 * value
    scale = jnp.where(value > 0.0, 0.8 / (real * real + imag * imag), 0.0)
    diag_re[...] = real * scale
    diag_im[...] = imag * scale
    sign = jnp.where(lax.broadcasted_iota(jnp.int32, (8, NZ), 0) < 4, 1.0, -1.0)
    size_x, size_y = table_re.shape[:2]

    def body(x, carry):
        for y in range(size_y):
            spot = pl.ds(y + skip, 1)
            table_re[x, y] = jnp.broadcast_to(diag_re[x, spot, :], (8, NZ))
            table_im[x, y] = jnp.broadcast_to(diag_im[x, spot, :], (8, NZ)) * sign
        return carry

    lax.fori_loop(0, size_x, body, 0)


def depth_sum(value):
    lane = lax.broadcasted_iota(jnp.int32, value.shape, 1)
    above = jnp.where(lane == 0, 0.0, pltpu.roll(value, 1, 1))
    below = jnp.where(lane == NZ - 1, 0.0, pltpu.roll(value, NZ - 1, 1))
    return above + below


def smooth(block, coef, skip, table_re, table_im, first, second, store):
    size_x, size_y = block.shape[:2]

    def solve(value, x, y):
        return table_re[x, y] * value + table_im[x, y] * pltpu.roll(value, 4, 0)

    def planes(k, body):
        lax.fori_loop(k, size_x - k, functools.partial(body, k, size_y - k), 0)

    def start(low, high, x, carry):
        for y in range(low, high):
            first[x, y] = solve(block[x, y], x, y)
        return carry

    def around(ref, x, low, high):
        line = [ref[x, y] for y in range(low - 1, high + 1)]
        for y in range(low, high):
            mid = line[y - low + 1]
            total = ref[x - 1, y] + ref[x + 1, y] + line[y - low] + line[y - low + 2]
            yield y, mid, total + depth_sum(mid)

    planes(0, start)
    here, there = first, second
    for k in range(1, 4):
        def sweep(low, high, x, carry, here=here, there=there):
            for y, mid, total in around(here, x, low, high):
                there[x, y] = 0.2 * mid + solve(block[x, y] + total, x, y)
            return carry

        planes(k, sweep)
        here, there = there, here

    def image(x, carry):
        for y, mid, total in around(here, x, 4, size_y - 4):
            diag = 6.0 - coef[x, pl.ds(y + skip, 1), :]
            store(x - 4, y - 4, diag * mid - total)
        return carry

    lax.fori_loop(4, size_x - 4, image, 0)


def wide_shape(halo):
    return (LX + 2 * NEAR, LY + 2 * halo)


FLAT = pltpu.VMEM((*wide_shape(FAR), NZ), F32)


def smooth_scratch(halo):
    return [pltpu.VMEM((*wide_shape(halo), 8, NZ), F32)] * 5 + [FLAT] * 2


def first_kernel(own, below, above, low, high, w, coef, out_right, out_left, block, first, second,
                 table_re, table_im, diag_re, diag_im):
    fill_flat(coef, below, own, above, low, high)
    fill_tables(coef, 0, table_re, table_im, diag_re, diag_im)
    rows = [(below, 2 * HALF), (own, 2 * BLOCK), (above, 2 * HALF)]
    fill_block(block, FAR, rows, FAR, [(low, high, 0, SIDE_SPANS)])

    def store(x, y, value):
        w[x, y] = value

    smooth(block, coef, 0, table_re, table_im, first, second, store)
    for d, more, place in NEAR_SPANS:
        count = LY + 2 * more
        out_right[pl.ds(place, count)] = w[LX - d, pl.ds(NEAR - more, count)]
        out_left[pl.ds(place, count)] = w[d - 1, pl.ds(NEAR - more, count)]


def first_image(*args):
    side = jax.ShapeDtypeStruct((NEAR_SIZE, 8, NZ), F32)
    return pl.pallas_call(
        first_kernel,
        out_shape=(jax.ShapeDtypeStruct((LX, LY + 2 * NEAR, 8, NZ), F32),
                   jax.ShapeDtypeStruct((*wide_shape(FAR), NZ), F32), side, side),
        in_specs=[VMEM] * 5,
        out_specs=(VMEM,) * 4,
        scratch_shapes=smooth_scratch(FAR),
        compiler_params=pltpu.CompilerParams(vmem_limit_bytes=16 << 20),
        cost_estimate=pl.CostEstimate(flops=12_000_000, bytes_accessed=18_000_000, transcendentals=0),
        name="first_image",
    )(*args)


def old_kernel(coef, own, below, above, low, high, first_low, first_high, out, block, first, second,
               table_re, table_im, diag_re, diag_im):
    fill_tables(coef, FAR - NEAR, table_re, table_im, diag_re, diag_im)
    for group in range(2):
        rows = [(below, group * HALF), (own, group * BLOCK), (above, group * HALF)]
        if group == 0:
            sides = [(low, high, 0, NEAR_SPANS[:-1]),
                     (first_low, first_high, SIDE_SIZE + FLAT_TILES - SPLIT, NEAR_SPANS[-1:])]
        else:
            sides = [(low, high, SPLIT, NEAR_SPANS)]
        fill_block(block, NEAR, rows, NEAR, sides)

        def store(x, y, value, group=group):
            out[x, pl.ds(group * BLOCK + y * 8, 8), :] = value

        smooth(block, coef, FAR - NEAR, table_re, table_im, first, second, store)


def old_images(*args):
    return pl.pallas_call(
        old_kernel,
        out_shape=jax.ShapeDtypeStruct((LX, 2 * BLOCK, NZ), F32),
        in_specs=[VMEM] * 8,
        out_specs=VMEM,
        scratch_shapes=smooth_scratch(NEAR),
        compiler_params=pltpu.CompilerParams(vmem_limit_bytes=16 << 20),
        cost_estimate=pl.CostEstimate(flops=12_000_000, bytes_accessed=24_000_000, transcendentals=0),
        name="old_images",
    )(*args)


def split3(value):
    high = value.astype(BF16)
    rest = value - high.astype(F32)
    middle = rest.astype(BF16)
    low = (rest - middle.astype(F32)).astype(BF16)
    return high, middle, low


def basis_plane(start, w, old_image, w_image, x):
    refs = [(start, 0), (start, LY), (start, 2 * LY), (w, None), (old_image, 0), (old_image, LY), (w_image, 0)]
    rows = []
    for ref, first in refs:
        if first is None:
            tiles = [ref[x, NEAR + y] for y in range(LY)]
        else:
            tiles = [ref[x, pl.ds((first + y) * 8, 8), :] for y in range(LY)]
        rows.append(jnp.concatenate(tiles, axis=1))
    rows.append(jnp.zeros((8, LY * NZ), F32))
    return jnp.concatenate(rows, axis=0)


def lane_roll(value, amount):
    return pltpu.roll(value, amount % NZ, 1)


SLOTS = [(0, 0), (0, 56), (1, 0), (1, 40), (1, 72), (1, 96), (0, 104)]


def pack_gram(gram):
    lane = lax.broadcasted_iota(jnp.int32, (8, NZ), 1)
    row = lax.broadcasted_iota(jnp.int32, (8, NZ), 0)
    packed = jnp.zeros((8, NZ), F32)
    for b in range(BLOCKS):
        rows = gram[8 * b:8 * b + 8]
        turned = jnp.where(lane % 8 < 4, lane_roll(rows, -4), -lane_roll(rows, 4))
        both = rows + pltpu.roll(turned, 4, 0)
        half, start = SLOTS[b]
        moved = lane_roll(both, start - 8 * b)
        if half:
            moved = pltpu.roll(moved, 4, 0)
        keep = (lane >= start) & (lane < start + 8 * (BLOCKS - b)) & (row // 4 == half)
        packed = packed + jnp.where(keep, moved, 0.0)
    return packed


def unpack_gram(packed):
    lane = lax.broadcasted_iota(jnp.int32, (8, NZ), 1)
    row = lax.broadcasted_iota(jnp.int32, (8, NZ), 0)
    rows = []
    for b in range(BLOCKS):
        half, start = SLOTS[b]
        moved = lane_roll(packed, 8 * b - start)
        if half:
            moved = pltpu.roll(moved, 4, 0)
        keep = (lane >= 8 * b) & (lane < 8 * BLOCKS) & (row < 4)
        moved = jnp.where(keep, moved, 0.0)
        turned = jnp.where(lane % 8 < 4, -lane_roll(moved, -4), lane_roll(moved, 4))
        rows.append(moved + pltpu.roll(turned, 4, 0))
    rows.append(jnp.zeros((NZ - 8 * BLOCKS, NZ), F32))
    upper = jnp.concatenate(rows, axis=0)
    tall = lax.broadcasted_iota(jnp.int32, (NZ, NZ), 0)
    wide = lax.broadcasted_iota(jnp.int32, (NZ, NZ), 1)
    return jnp.where(tall // 8 <= wide // 8, upper, upper.T)


def gram_kernel(peers, w, coef, low, high, start, old_image, w_image, out,
                block, first, second, table_re, table_im, diag_re, diag_im):
    fill_tables(coef, FAR - NEAR, table_re, table_im, diag_re, diag_im)
    block[...] = jnp.zeros(block.shape, F32)
    for x in range(LX):
        block[NEAR + x] = w[x]
    fill_sides(block, NEAR, [(low, high, 0, NEAR_SPANS)])

    def store(x, y, value):
        w_image[x, pl.ds(y * 8, 8), :] = value

    smooth(block, coef, FAR - NEAR, table_re, table_im, first, second, store)

    def plane(x, total):
        stacked = jnp.concatenate(split3(basis_plane(start, w, old_image, w_image, x)), axis=0)
        return total + lax.dot_general(stacked, stacked, (((1,), (1,)), ((), ())), preferred_element_type=F32)

    total = lax.fori_loop(0, LX, plane, jnp.zeros((3 * ROWS, 3 * ROWS), F32))
    tall = total[0:ROWS] + total[ROWS:2 * ROWS] + total[2 * ROWS:3 * ROWS]
    gram = tall[:, 0:ROWS] + tall[:, ROWS:2 * ROWS] + tall[:, 2 * ROWS:3 * ROWS]
    gram = jnp.concatenate([gram, jnp.zeros((ROWS, NZ - ROWS), F32)], axis=1)
    packed = pack_gram(gram)
    for peer in range(peers):
        out[peer] = packed


def image_and_gram(peers, *args):
    return pl.pallas_call(
        functools.partial(gram_kernel, peers),
        out_shape=(jax.ShapeDtypeStruct((LX, LY * 8, NZ), F32),
                   jax.ShapeDtypeStruct((peers, 8, NZ), F32)),
        in_specs=[VMEM] * 6,
        out_specs=(VMEM, VMEM),
        scratch_shapes=smooth_scratch(NEAR),
        compiler_params=pltpu.CompilerParams(vmem_limit_bytes=32 << 20),
        name="image_and_gram",
    )(*args)


def sum_kernel(parts, out):
    total = jnp.sum(parts[...], axis=0)
    for peer in range(out.shape[0]):
        out[peer] = total


def sum_and_spread(parts, peers):
    return pl.pallas_call(
        sum_kernel,
        out_shape=jax.ShapeDtypeStruct((peers, 8, NZ), F32),
        in_specs=[VMEM],
        out_specs=VMEM,
        compiler_params=pltpu.CompilerParams(vmem_limit_bytes=1 << 20),
        name="sum_and_spread",
    )(parts)


def mul(left, right):
    return lax.dot_general(left, right, (((1,), (0,)), ((), ())), precision=HIGHEST, preferred_element_type=F32)


def mul_t(left, right):
    return lax.dot_general(left, right, (((1,), (1,)), ((), ())), precision=HIGHEST, preferred_element_type=F32)


def inverse_factor(gram):
    lane = lax.broadcasted_iota(jnp.int32, (8, NZ), 1)
    row = lax.broadcasted_iota(jnp.int32, (8, NZ), 0)
    work = jnp.where(lane < 8, gram, jnp.where(lane == row + 8, 1.0, 0.0))
    rank = 2 * (row % 4) + row // 4
    for step in range(8):
        k = (step % 2) * 4 + step // 2
        line = work[k:k + 1, :]
        pivot = line[:, k:k + 1]
        column = work[:, k:k + 1]
        root = 1.0 / jnp.sqrt(pivot)
        line = line * root
        factor = column * root
        work = jnp.where(rank > step, work - factor * line, jnp.where(rank == step, line, work))
    return jnp.where(lane < 8, lane_roll(work, -8), 0.0)


def coefficients(gram):
    lane = lax.broadcasted_iota(jnp.int32, (8, NZ), 1)
    row = lax.broadcasted_iota(jnp.int32, (8, NZ), 0)
    tall = lax.broadcasted_iota(jnp.int32, (NZ, NZ), 0)
    wide = lax.broadcasted_iota(jnp.int32, (NZ, NZ), 1)

    def normalise(rows):
        small = mul_t(mul(rows, gram), rows_in(rows))
        return mul(inverse_factor(small)[:, 0:8], rows)

    def rows_in(rows):
        return jnp.concatenate([rows, jnp.zeros((NZ - 8, NZ), F32)], axis=0)

    once = jnp.where(lane < 24, gram[24:32], 0.0)
    again = jnp.where(lane < 24, mul(once, gram), 0.0)
    fresh = jnp.where(lane == row + 24, 1.0, 0.0)
    new = normalise(fresh - (2.0 * once - again))
    image = (jnp.where((lane >= 32) & (lane < 48), lane_roll(new, 32), 0.0)
             + jnp.where((lane >= 24) & (lane < 32), lane_roll(new, 8), 0.0)
             + jnp.where((lane >= 48) & (lane < 56), lane_roll(new, 24), 0.0))
    window = jnp.where((tall < 16) & (wide == tall + 8), 1.0, 0.0)
    window = jnp.concatenate([window[0:16], new, window[24:]], axis=0)

    def project(rows):
        return mul(mul_t(mul(rows, gram), window), window)

    once = project(image)
    again = project(once)
    newest = normalise(image - (2.0 * once - again))
    return new, newest


def final_kernel(cells, parts, start, w, old_image, w_image, out):
    gram = unpack_gram(jnp.sum(parts[...], axis=0) * (1.0 / cells))
    new, newest = coefficients(gram)
    mapping = jnp.concatenate([new, newest], axis=0)[:, 0:ROWS]
    pieces = [jnp.concatenate([piece] * 3, axis=1) for piece in split3(mapping)]
    stacked_map = jnp.concatenate(pieces, axis=0)

    def plane(x, carry):
        stacked = jnp.concatenate(split3(basis_plane(start, w, old_image, w_image, x)), axis=0)
        full = lax.dot_general(stacked_map, stacked, (((1,), (0,)), ((), ())), preferred_element_type=F32)
        result = full[32:48] + full[16:32] + full[0:16]
        for k in range(2):
            tiles = jnp.stack([result[8 * k:8 * k + 8, y * NZ:(y + 1) * NZ] for y in range(LY)])
            out[k, :, x] = jnp.swapaxes(tiles, 0, 1)
        return carry

    lax.fori_loop(0, LX, plane, 0)


def finish(cells, *args):
    return pl.pallas_call(
        functools.partial(final_kernel, cells),
        out_shape=jax.ShapeDtypeStruct((2, 8, LX, LY, NZ), F32),
        in_specs=[VMEM] * 5,
        out_specs=VMEM,
        compiler_params=pltpu.CompilerParams(vmem_limit_bytes=32 << 20),
        name="finish",
    )(*args)


GX = ("z", "core")


def from_both(axis, count, to_higher, to_lower, step=1):
    return (
        lax.ppermute(to_higher, axis, [(i, i + step) for i in range(count - step)]),
        lax.ppermute(to_lower, axis, [(i + step, i) for i in range(count - step)]),
    )


def per_device(nx, ny, nz, prior, coefficient):
    cells = coefficient.size * nx * ny
    by_cell = prior.transpose(3, 0, 4, 1, 2, 5).reshape(LX, 3 * LY * 8, NZ)
    start = jnp.concatenate([by_cell, coefficient], axis=1)
    up = jnp.concatenate([start[:, HALF:BLOCK], start[:, BLOCK + HALF:]], axis=1)
    down = jnp.concatenate([start[:, :HALF], start[:, BLOCK:BLOCK + HALF], start[:, 2 * BLOCK:]], axis=1)
    rims = from_both("gy", ny, up, down)
    right, left, old_right, old_left = pack_all(start, *rims)
    sides = from_both(GX, nx, right, left)
    old_sides = from_both(GX, nx, old_right, old_left)
    w, coef, w_right, w_left = first_image(start, *rims, *sides)
    w_sides = from_both(GX, nx, w_right, w_left)
    old_image = old_images(coef, start, *rims, *old_sides, *sides)

    w_image, spread = image_and_gram(2 * ny, w, coef, *w_sides, start, old_image)
    got = lax.all_to_all(spread, ("core", "gy"), 0, 0)
    got = lax.all_to_all(sum_and_spread(got, nz), "z", 0, 0)
    out = finish(cells, got, start, w, old_image, w_image)
    return out.reshape(2, 2, 4, LX, LY, NZ)


def solution(mesh):
    nx, ny = mesh.shape["gx"], mesh.shape["gy"]
    fine = Mesh(np.asarray(mesh.devices).reshape(nx // 2, 2, ny), ("z", "core", "gy"))
    in_specs = (P(None, None, None, GX, "gy", None), P(GX, "gy", None))
    out_specs = P(None, None, None, GX, "gy", None)
    return jax.shard_map(
        functools.partial(per_device, nx, ny, nx // 2),
        mesh=fine, in_specs=in_specs, out_specs=out_specs, check_vma=False,
    )
```

```python
import functools

import jax
import jax.numpy as jnp
import numpy as np
from jax import lax
from jax.experimental import pallas as pl
from jax.experimental.pallas import tpu as pltpu
from jax.sharding import Mesh, PartitionSpec as P

LX, LY, NZ = 4, 8, 128
NEAR, FAR = 4, 8
BLOCKS = 7
ROWS = 64
F32 = jnp.float32
BF16 = jnp.bfloat16
HIGHEST = lax.Precision.HIGHEST
VMEM = pl.BlockSpec(memory_space=pltpu.VMEM)


BLOCK = LY * 8
HALF = NEAR * 8


def spans(halo, begin, end):
    found, place = [], 0
    for d in range(begin + 1, end + 1):
        found.append((d, halo - d, place))
        place += LY + 2 * (halo - d)
    return found, place


NEAR_SPANS, NEAR_SIZE = spans(NEAR, 0, LX)
SIDE_SPANS, SIDE_SIZE = spans(FAR, 0, LX)
FLAT_TILES = -(-SIDE_SIZE // 8)
SPLIT = NEAR_SPANS[-1][2]
FIRST_TILES = SIDE_SIZE + FLAT_TILES + NEAR_SIZE - SPLIT
SECOND_TILES = SPLIT + NEAR_SIZE


def pack_columns(out, start, found, to_higher, rows, reach):
    (below, low_row), (own, own_row), (above, high_row) = rows
    for d, more, place in found:
        x = LX - 1 - (d - 1) % LX if to_higher else (d - 1) % LX
        spot = start + place
        size = more * 8
        if more:
            out[pl.ds(spot, more)] = below[x, pl.ds(low_row + reach * 8 - size, size), :].reshape(more, 8, NZ)
            out[pl.ds(spot + more + LY, more)] = above[x, pl.ds(high_row, size), :].reshape(more, 8, NZ)
        out[pl.ds(spot + more, LY)] = own[x, pl.ds(own_row, BLOCK), :].reshape(LY, 8, NZ)


def pack_coefficient(out, start, found, to_higher, below, own, above):
    for d, more, place in found:
        x = LX - 1 - (d - 1) % LX if to_higher else (d - 1) % LX
        for y in range(-more, LY + more):
            if y < 0:
                ref, row = below, 2 * HALF + BLOCK + LY + y
            elif y < LY:
                ref, row = own, 3 * BLOCK + y
            else:
                ref, row = above, 2 * HALF + BLOCK + y - LY
            spot = place + more + y
            out[start + spot // 8, pl.ds(spot % 8, 1), :] = ref[x, pl.ds(row, 1), :]


def column_kernel(own, below, above, right, left, old_right, old_left):
    for first, second, to_higher in ((right, old_right, True), (left, old_left, False)):
        rows = [(below, 2 * HALF), (own, 2 * BLOCK), (above, 2 * HALF)]
        pack_columns(first, 0, SIDE_SPANS, to_higher, rows, FAR)
        if SIDE_SIZE % 8:
            first[SIDE_SIZE + FLAT_TILES - 1] = jnp.zeros((8, NZ), F32)
        pack_coefficient(first, SIDE_SIZE, SIDE_SPANS, to_higher, below, own, above)
        rows = [(below, 0), (own, 0), (above, 0)]
        pack_columns(second, 0, NEAR_SPANS[:-1], to_higher, rows, NEAR)
        pack_columns(first, SIDE_SIZE + FLAT_TILES - SPLIT, NEAR_SPANS[-1:], to_higher, rows, NEAR)
        rows = [(below, HALF), (own, BLOCK), (above, HALF)]
        pack_columns(second, SPLIT, NEAR_SPANS, to_higher, rows, NEAR)


def pack_all(*args):
    shapes = tuple(jax.ShapeDtypeStruct((size, 8, NZ), F32) for size in [FIRST_TILES] * 2 + [SECOND_TILES] * 2)
    return pl.pallas_call(
        column_kernel,
        out_shape=shapes,
        in_specs=[VMEM] * 3,
        out_specs=(VMEM,) * 4,
        compiler_params=pltpu.CompilerParams(vmem_limit_bytes=1 << 20),
        name="pack_all",
    )(*args)


def fill_sides(wide, halo, sides):
    for low, high, start, found in sides:
        for d, more, place in found:
            count = LY + 2 * more
            begin = halo - more
            wide[NEAR - d, begin:begin + count] = low[pl.ds(start + place, count)]
            wide[NEAR + LX - 1 + d, begin:begin + count] = high[pl.ds(start + place, count)]


def fill_block(wide, halo, rows, reach, sides):
    (below, low_row), (own, own_row), (above, high_row) = rows
    wide[...] = jnp.zeros(wide.shape, F32)
    for x in range(LX):
        size = halo * 8
        wide[NEAR + x, 0:halo] = below[x, pl.ds(low_row + reach * 8 - size, size), :].reshape(halo, 8, NZ)
        wide[NEAR + x, halo:halo + LY] = own[x, pl.ds(own_row, BLOCK), :].reshape(LY, 8, NZ)
        wide[NEAR + x, halo + LY:] = above[x, pl.ds(high_row, size), :].reshape(halo, 8, NZ)
    fill_sides(wide, halo, sides)


def fill_flat(wide, below, own, above, low, high):
    wide[...] = jnp.zeros(wide.shape, F32)
    for x in range(LX):
        wide[NEAR + x, 0:FAR] = below[x, pl.ds(2 * HALF + BLOCK, LY), :]
        wide[NEAR + x, FAR:FAR + LY] = own[x, pl.ds(3 * BLOCK, LY), :]
        wide[NEAR + x, FAR + LY:] = above[x, pl.ds(2 * HALF + BLOCK, LY), :]
    for d, more, place in SIDE_SPANS:
        for i in range(LY + 2 * more):
            tile, row = SIDE_SIZE + (place + i) // 8, (place + i) % 8
            y = FAR - more + i
            wide[NEAR - d, pl.ds(y, 1), :] = low[tile, pl.ds(row, 1), :]
            wide[NEAR + LX - 1 + d, pl.ds(y, 1), :] = high[tile, pl.ds(row, 1), :]


def fill_tables(coef, skip, table_re, table_im, diag_re, diag_im):
    value = coef[...]
    real = 6.0 - value
    imag = 0.5 * value
    scale = jnp.where(value > 0.0, 0.8 / (real * real + imag * imag), 0.0)
    diag_re[...] = real * scale
    diag_im[...] = imag * scale
    sign = jnp.where(lax.broadcasted_iota(jnp.int32, (8, NZ), 0) < 4, 1.0, -1.0)
    size_x, size_y = table_re.shape[:2]

    def body(x, carry):
        for y in range(size_y):
            spot = pl.ds(y + skip, 1)
            table_re[x, y] = jnp.broadcast_to(diag_re[x, spot, :], (8, NZ))
            table_im[x, y] = jnp.broadcast_to(diag_im[x, spot, :], (8, NZ)) * sign
        return carry

    lax.fori_loop(0, size_x, body, 0, unroll=True)


def depth_sum(value):
    lane = lax.broadcasted_iota(jnp.int32, value.shape, 1)
    above = jnp.where(lane == 0, 0.0, pltpu.roll(value, 1, 1))
    below = jnp.where(lane == NZ - 1, 0.0, pltpu.roll(value, NZ - 1, 1))
    return above + below


def smooth(block, coef, skip, table_re, table_im, first, second, store):
    size_x, size_y = block.shape[:2]

    def solve(value, x, y):
        return table_re[x, y] * value + table_im[x, y] * pltpu.roll(value, 4, 0)

    def planes(k, body):
        lax.fori_loop(k, size_x - k, functools.partial(body, k, size_y - k), 0, unroll=True)

    def start(low, high, x, carry):
        for y in range(low, high):
            first[x, y] = solve(block[x, y], x, y)
        return carry

    def around(ref, x, low, high):
        line = [ref[x, y] for y in range(low - 1, high + 1)]
        for y in range(low, high):
            mid = line[y - low + 1]
            total = ref[x - 1, y] + ref[x + 1, y] + line[y - low] + line[y - low + 2]
            yield y, mid, total + depth_sum(mid)

    planes(0, start)
    here, there = first, second
    for k in range(1, 4):
        def sweep(low, high, x, carry, here=here, there=there):
            for y, mid, total in around(here, x, low, high):
                there[x, y] = 0.2 * mid + solve(block[x, y] + total, x, y)
            return carry

        planes(k, sweep)
        here, there = there, here

    def image(x, carry):
        for y, mid, total in around(here, x, 4, size_y - 4):
            diag = 6.0 - coef[x, pl.ds(y + skip, 1), :]
            store(x - 4, y - 4, diag * mid - total)
        return carry

    lax.fori_loop(4, size_x - 4, image, 0, unroll=True)


def wide_shape(halo):
    return (LX + 2 * NEAR, LY + 2 * halo)


FLAT = pltpu.VMEM((*wide_shape(FAR), NZ), F32)


def smooth_scratch(halo):
    return [pltpu.VMEM((*wide_shape(halo), 8, NZ), F32)] * 5 + [FLAT] * 2


def first_kernel(own, below, above, low, high, w, coef, out_right, out_left, block, first, second,
                 table_re, table_im, diag_re, diag_im):
    fill_flat(coef, below, own, above, low, high)
    fill_tables(coef, 0, table_re, table_im, diag_re, diag_im)
    rows = [(below, 2 * HALF), (own, 2 * BLOCK), (above, 2 * HALF)]
    fill_block(block, FAR, rows, FAR, [(low, high, 0, SIDE_SPANS)])

    def store(x, y, value):
        w[x, y] = value

    smooth(block, coef, 0, table_re, table_im, first, second, store)
    for d, more, place in NEAR_SPANS:
        count = LY + 2 * more
        out_right[pl.ds(place, count)] = w[LX - d, pl.ds(NEAR - more, count)]
        out_left[pl.ds(place, count)] = w[d - 1, pl.ds(NEAR - more, count)]


def first_image(*args):
    side = jax.ShapeDtypeStruct((NEAR_SIZE, 8, NZ), F32)
    return pl.pallas_call(
        first_kernel,
        out_shape=(jax.ShapeDtypeStruct((LX, LY + 2 * NEAR, 8, NZ), F32),
                   jax.ShapeDtypeStruct((*wide_shape(FAR), NZ), F32), side, side),
        in_specs=[VMEM] * 5,
        out_specs=(VMEM,) * 4,
        scratch_shapes=smooth_scratch(FAR),
        compiler_params=pltpu.CompilerParams(vmem_limit_bytes=16 << 20),
        cost_estimate=pl.CostEstimate(flops=12_000_000, bytes_accessed=18_000_000, transcendentals=0),
        name="first_image",
    )(*args)


def old_kernel(coef, own, below, above, low, high, first_low, first_high, out, block, first, second,
               table_re, table_im, diag_re, diag_im):
    fill_tables(coef, FAR - NEAR, table_re, table_im, diag_re, diag_im)
    for group in range(2):
        rows = [(below, group * HALF), (own, group * BLOCK), (above, group * HALF)]
        if group == 0:
            sides = [(low, high, 0, NEAR_SPANS[:-1]),
                     (first_low, first_high, SIDE_SIZE + FLAT_TILES - SPLIT, NEAR_SPANS[-1:])]
        else:
            sides = [(low, high, SPLIT, NEAR_SPANS)]
        fill_block(block, NEAR, rows, NEAR, sides)

        def store(x, y, value, group=group):
            out[x, pl.ds(group * BLOCK + y * 8, 8), :] = value

        smooth(block, coef, FAR - NEAR, table_re, table_im, first, second, store)


def old_images(*args):
    return pl.pallas_call(
        old_kernel,
        out_shape=jax.ShapeDtypeStruct((LX, 2 * BLOCK, NZ), F32),
        in_specs=[VMEM] * 8,
        out_specs=VMEM,
        scratch_shapes=smooth_scratch(NEAR),
        compiler_params=pltpu.CompilerParams(vmem_limit_bytes=16 << 20),
        cost_estimate=pl.CostEstimate(flops=12_000_000, bytes_accessed=24_000_000, transcendentals=0),
        name="old_images",
    )(*args)


def split3(value):
    high = value.astype(BF16)
    rest = value - high.astype(F32)
    middle = rest.astype(BF16)
    low = (rest - middle.astype(F32)).astype(BF16)
    return high, middle, low


def basis_plane(start, w, old_image, w_image, x):
    refs = [(start, 0), (start, LY), (start, 2 * LY), (w, None), (old_image, 0), (old_image, LY), (w_image, 0)]
    rows = []
    for ref, first in refs:
        if first is None:
            tiles = [ref[x, NEAR + y] for y in range(LY)]
        else:
            tiles = [ref[x, pl.ds((first + y) * 8, 8), :] for y in range(LY)]
        rows.append(jnp.concatenate(tiles, axis=1))
    rows.append(jnp.zeros((8, LY * NZ), F32))
    return jnp.concatenate(rows, axis=0)


def lane_roll(value, amount):
    return pltpu.roll(value, amount % NZ, 1)


SLOTS = [(0, 0), (0, 56), (1, 0), (1, 40), (1, 72), (1, 96), (0, 104)]


def pack_gram(gram):
    lane = lax.broadcasted_iota(jnp.int32, (8, NZ), 1)
    row = lax.broadcasted_iota(jnp.int32, (8, NZ), 0)
    packed = jnp.zeros((8, NZ), F32)
    for b in range(BLOCKS):
        rows = gram[8 * b:8 * b + 8]
        turned = jnp.where(lane % 8 < 4, lane_roll(rows, -4), -lane_roll(rows, 4))
        both = rows + pltpu.roll(turned, 4, 0)
        half, start = SLOTS[b]
        moved = lane_roll(both, start - 8 * b)
        if half:
            moved = pltpu.roll(moved, 4, 0)
        keep = (lane >= start) & (lane < start + 8 * (BLOCKS - b)) & (row // 4 == half)
        packed = packed + jnp.where(keep, moved, 0.0)
    return packed


def unpack_gram(packed):
    lane = lax.broadcasted_iota(jnp.int32, (8, NZ), 1)
    row = lax.broadcasted_iota(jnp.int32, (8, NZ), 0)
    rows = []
    for b in range(BLOCKS):
        half, start = SLOTS[b]
        moved = lane_roll(packed, 8 * b - start)
        if half:
            moved = pltpu.roll(moved, 4, 0)
        keep = (lane >= 8 * b) & (lane < 8 * BLOCKS) & (row < 4)
        moved = jnp.where(keep, moved, 0.0)
        turned = jnp.where(lane % 8 < 4, -lane_roll(moved, -4), lane_roll(moved, 4))
        rows.append(moved + pltpu.roll(turned, 4, 0))
    rows.append(jnp.zeros((NZ - 8 * BLOCKS, NZ), F32))
    upper = jnp.concatenate(rows, axis=0)
    tall = lax.broadcasted_iota(jnp.int32, (NZ, NZ), 0)
    wide = lax.broadcasted_iota(jnp.int32, (NZ, NZ), 1)
    return jnp.where(tall // 8 <= wide // 8, upper, upper.T)


def gram_kernel(peers, w, coef, low, high, start, old_image, w_image, out,
                block, first, second, table_re, table_im, diag_re, diag_im):
    fill_tables(coef, FAR - NEAR, table_re, table_im, diag_re, diag_im)
    block[...] = jnp.zeros(block.shape, F32)
    for x in range(LX):
        block[NEAR + x] = w[x]
    fill_sides(block, NEAR, [(low, high, 0, NEAR_SPANS)])

    def store(x, y, value):
        w_image[x, pl.ds(y * 8, 8), :] = value

    smooth(block, coef, FAR - NEAR, table_re, table_im, first, second, store)

    def plane(x, total):
        stacked = jnp.concatenate(split3(basis_plane(start, w, old_image, w_image, x)), axis=0)
        return total + lax.dot_general(stacked, stacked, (((1,), (1,)), ((), ())), preferred_element_type=F32)

    total = lax.fori_loop(0, LX, plane, jnp.zeros((3 * ROWS, 3 * ROWS), F32), unroll=True)
    tall = total[0:ROWS] + total[ROWS:2 * ROWS] + total[2 * ROWS:3 * ROWS]
    gram = tall[:, 0:ROWS] + tall[:, ROWS:2 * ROWS] + tall[:, 2 * ROWS:3 * ROWS]
    gram = jnp.concatenate([gram, jnp.zeros((ROWS, NZ - ROWS), F32)], axis=1)
    packed = pack_gram(gram)
    for peer in range(peers):
        out[peer] = packed


def image_and_gram(peers, *args):
    return pl.pallas_call(
        functools.partial(gram_kernel, peers),
        out_shape=(jax.ShapeDtypeStruct((LX, LY * 8, NZ), F32),
                   jax.ShapeDtypeStruct((peers, 8, NZ), F32)),
        in_specs=[VMEM] * 6,
        out_specs=(VMEM, VMEM),
        scratch_shapes=smooth_scratch(NEAR),
        compiler_params=pltpu.CompilerParams(vmem_limit_bytes=32 << 20),
        name="image_and_gram",
    )(*args)


def sum_kernel(parts, out):
    total = jnp.sum(parts[...], axis=0)
    for peer in range(out.shape[0]):
        out[peer] = total


def sum_and_spread(parts, peers):
    return pl.pallas_call(
        sum_kernel,
        out_shape=jax.ShapeDtypeStruct((peers, 8, NZ), F32),
        in_specs=[VMEM],
        out_specs=VMEM,
        compiler_params=pltpu.CompilerParams(vmem_limit_bytes=1 << 20),
        name="sum_and_spread",
    )(parts)


def mul(left, right):
    return lax.dot_general(left, right, (((1,), (0,)), ((), ())), precision=HIGHEST, preferred_element_type=F32)


def mul_t(left, right):
    return lax.dot_general(left, right, (((1,), (1,)), ((), ())), precision=HIGHEST, preferred_element_type=F32)


def inverse_factor(gram):
    lane = lax.broadcasted_iota(jnp.int32, (8, NZ), 1)
    row = lax.broadcasted_iota(jnp.int32, (8, NZ), 0)
    work = jnp.where(lane < 8, gram, jnp.where(lane == row + 8, 1.0, 0.0))
    rank = 2 * (row % 4) + row // 4
    for step in range(8):
        k = (step % 2) * 4 + step // 2
        line = work[k:k + 1, :]
        pivot = line[:, k:k + 1]
        column = work[:, k:k + 1]
        root = 1.0 / jnp.sqrt(pivot)
        line = line * root
        factor = column * root
        work = jnp.where(rank > step, work - factor * line, jnp.where(rank == step, line, work))
    return jnp.where(lane < 8, lane_roll(work, -8), 0.0)


def coefficients(gram):
    lane = lax.broadcasted_iota(jnp.int32, (8, NZ), 1)
    row = lax.broadcasted_iota(jnp.int32, (8, NZ), 0)
    tall = lax.broadcasted_iota(jnp.int32, (NZ, NZ), 0)
    wide = lax.broadcasted_iota(jnp.int32, (NZ, NZ), 1)

    def normalise(rows):
        small = mul_t(mul(rows, gram), rows_in(rows))
        return mul(inverse_factor(small)[:, 0:8], rows)

    def rows_in(rows):
        return jnp.concatenate([rows, jnp.zeros((NZ - 8, NZ), F32)], axis=0)

    once = jnp.where(lane < 24, gram[24:32], 0.0)
    again = jnp.where(lane < 24, mul(once, gram), 0.0)
    fresh = jnp.where(lane == row + 24, 1.0, 0.0)
    new = normalise(fresh - (2.0 * once - again))
    image = (jnp.where((lane >= 32) & (lane < 48), lane_roll(new, 32), 0.0)
             + jnp.where((lane >= 24) & (lane < 32), lane_roll(new, 8), 0.0)
             + jnp.where((lane >= 48) & (lane < 56), lane_roll(new, 24), 0.0))
    window = jnp.where((tall < 16) & (wide == tall + 8), 1.0, 0.0)
    window = jnp.concatenate([window[0:16], new, window[24:]], axis=0)

    def project(rows):
        return mul(mul_t(mul(rows, gram), window), window)

    once = project(image)
    again = project(once)
    newest = normalise(image - (2.0 * once - again))
    return new, newest


def final_kernel(cells, parts, start, w, old_image, w_image, out):
    gram = unpack_gram(jnp.sum(parts[...], axis=0) * (1.0 / cells))
    new, newest = coefficients(gram)
    mapping = jnp.concatenate([new, newest], axis=0)[:, 0:ROWS]
    pieces = [jnp.concatenate([piece] * 3, axis=1) for piece in split3(mapping)]
    stacked_map = jnp.concatenate(pieces, axis=0)

    def plane(x, carry):
        stacked = jnp.concatenate(split3(basis_plane(start, w, old_image, w_image, x)), axis=0)
        full = lax.dot_general(stacked_map, stacked, (((1,), (0,)), ((), ())), preferred_element_type=F32)
        result = full[32:48] + full[16:32] + full[0:16]
        for k in range(2):
            tiles = jnp.stack([result[8 * k:8 * k + 8, y * NZ:(y + 1) * NZ] for y in range(LY)])
            out[k, :, x] = jnp.swapaxes(tiles, 0, 1)
        return carry

    lax.fori_loop(0, LX, plane, 0, unroll=True)


def finish(cells, *args):
    return pl.pallas_call(
        functools.partial(final_kernel, cells),
        out_shape=jax.ShapeDtypeStruct((2, 8, LX, LY, NZ), F32),
        in_specs=[VMEM] * 5,
        out_specs=VMEM,
        compiler_params=pltpu.CompilerParams(vmem_limit_bytes=32 << 20),
        name="finish",
    )(*args)


GX = ("z", "core")


def from_both(axis, count, to_higher, to_lower, step=1):
    return (
        lax.ppermute(to_higher, axis, [(i, i + step) for i in range(count - step)]),
        lax.ppermute(to_lower, axis, [(i + step, i) for i in range(count - step)]),
    )


def per_device(nx, ny, nz, prior, coefficient):
    cells = coefficient.size * nx * ny
    by_cell = prior.transpose(3, 0, 4, 1, 2, 5).reshape(LX, 3 * LY * 8, NZ)
    start = jnp.concatenate([by_cell, coefficient], axis=1)
    up = jnp.concatenate([start[:, HALF:BLOCK], start[:, BLOCK + HALF:]], axis=1)
    down = jnp.concatenate([start[:, :HALF], start[:, BLOCK:BLOCK + HALF], start[:, 2 * BLOCK:]], axis=1)
    rims = from_both("gy", ny, up, down)
    right, left, old_right, old_left = pack_all(start, *rims)
    sides = from_both(GX, nx, right, left)
    old_sides = from_both(GX, nx, old_right, old_left)
    w, coef, w_right, w_left = first_image(start, *rims, *sides)
    w_sides = from_both(GX, nx, w_right, w_left)
    old_image = old_images(coef, start, *rims, *old_sides, *sides)

    w_image, spread = image_and_gram(2 * ny, w, coef, *w_sides, start, old_image)
    got = lax.all_to_all(spread, ("core", "gy"), 0, 0)
    got = lax.all_to_all(sum_and_spread(got, nz), "z", 0, 0)
    out = finish(cells, got, start, w, old_image, w_image)
    return out.reshape(2, 2, 4, LX, LY, NZ)


def solution(mesh):
    nx, ny = mesh.shape["gx"], mesh.shape["gy"]
    fine = Mesh(np.asarray(mesh.devices).reshape(nx // 2, 2, ny), ("z", "core", "gy"))
    in_specs = (P(None, None, None, GX, "gy", None), P(GX, "gy", None))
    out_specs = P(None, None, None, GX, "gy", None)
    return jax.shard_map(
        functools.partial(per_device, nx, ny, nx // 2),
        mesh=fine, in_specs=in_specs, out_specs=out_specs, check_vma=False,
    )
```

```python
import functools

import jax
import jax.numpy as jnp
import numpy as np
from jax import lax
from jax.experimental import pallas as pl
from jax.experimental.pallas import tpu as pltpu
from jax.sharding import Mesh, PartitionSpec as P

LX, LY, NZ = 4, 8, 128
NEAR, FAR = 4, 8
BLOCKS = 7
ROWS = 64
F32 = jnp.float32
BF16 = jnp.bfloat16
VMEM = pl.BlockSpec(memory_space=pltpu.VMEM)


BLOCK = LY * 8
HALF = NEAR * 8


def spans(halo, begin, end):
    found, place = [], 0
    for d in range(begin + 1, end + 1):
        found.append((d, halo - d, place))
        place += LY + 2 * (halo - d)
    return found, place


NEAR_SPANS, NEAR_SIZE = spans(NEAR, 0, LX)
SIDE_SPANS, SIDE_SIZE = spans(FAR, 0, LX)
FLAT_TILES = -(-SIDE_SIZE // 8)
SPLIT = NEAR_SPANS[-1][2]
FIRST_TILES = SIDE_SIZE + FLAT_TILES + NEAR_SIZE - SPLIT
SECOND_TILES = SPLIT + NEAR_SIZE


def pack_columns(out, start, found, to_higher, rows, reach):
    (below, low_row), (own, own_row), (above, high_row) = rows
    for d, more, place in found:
        x = LX - 1 - (d - 1) % LX if to_higher else (d - 1) % LX
        spot = start + place
        size = more * 8
        if more:
            out[pl.ds(spot, more)] = below[x, pl.ds(low_row + reach * 8 - size, size), :].reshape(more, 8, NZ)
            out[pl.ds(spot + more + LY, more)] = above[x, pl.ds(high_row, size), :].reshape(more, 8, NZ)
        out[pl.ds(spot + more, LY)] = own[x, pl.ds(own_row, BLOCK), :].reshape(LY, 8, NZ)


def pack_coefficient(out, start, found, to_higher, below, own, above):
    for d, more, place in found:
        x = LX - 1 - (d - 1) % LX if to_higher else (d - 1) % LX
        for y in range(-more, LY + more):
            if y < 0:
                ref, row = below, 2 * HALF + BLOCK + LY + y
            elif y < LY:
                ref, row = own, 3 * BLOCK + y
            else:
                ref, row = above, 2 * HALF + BLOCK + y - LY
            spot = place + more + y
            out[start + spot // 8, pl.ds(spot % 8, 1), :] = ref[x, pl.ds(row, 1), :]


def column_kernel(own, below, above, right, left, old_right, old_left):
    for first, second, to_higher in ((right, old_right, True), (left, old_left, False)):
        rows = [(below, 2 * HALF), (own, 2 * BLOCK), (above, 2 * HALF)]
        pack_columns(first, 0, SIDE_SPANS, to_higher, rows, FAR)
        if SIDE_SIZE % 8:
            first[SIDE_SIZE + FLAT_TILES - 1] = jnp.zeros((8, NZ), F32)
        pack_coefficient(first, SIDE_SIZE, SIDE_SPANS, to_higher, below, own, above)
        rows = [(below, 0), (own, 0), (above, 0)]
        pack_columns(second, 0, NEAR_SPANS[:-1], to_higher, rows, NEAR)
        pack_columns(first, SIDE_SIZE + FLAT_TILES - SPLIT, NEAR_SPANS[-1:], to_higher, rows, NEAR)
        rows = [(below, HALF), (own, BLOCK), (above, HALF)]
        pack_columns(second, SPLIT, NEAR_SPANS, to_higher, rows, NEAR)


def pack_all(*args):
    shapes = tuple(jax.ShapeDtypeStruct((size, 8, NZ), F32) for size in [FIRST_TILES] * 2 + [SECOND_TILES] * 2)
    return pl.pallas_call(
        column_kernel,
        out_shape=shapes,
        in_specs=[VMEM] * 3,
        out_specs=(VMEM,) * 4,
        compiler_params=pltpu.CompilerParams(vmem_limit_bytes=1 << 20),
        name="pack_all",
    )(*args)


def fill_sides(wide, halo, sides):
    for low, high, start, found in sides:
        for d, more, place in found:
            count = LY + 2 * more
            begin = halo - more
            wide[NEAR - d, begin:begin + count] = low[pl.ds(start + place, count)]
            wide[NEAR + LX - 1 + d, begin:begin + count] = high[pl.ds(start + place, count)]


def fill_block(wide, halo, rows, reach, sides):
    (below, low_row), (own, own_row), (above, high_row) = rows
    wide[...] = jnp.zeros(wide.shape, F32)
    for x in range(LX):
        size = halo * 8
        wide[NEAR + x, 0:halo] = below[x, pl.ds(low_row + reach * 8 - size, size), :].reshape(halo, 8, NZ)
        wide[NEAR + x, halo:halo + LY] = own[x, pl.ds(own_row, BLOCK), :].reshape(LY, 8, NZ)
        wide[NEAR + x, halo + LY:] = above[x, pl.ds(high_row, size), :].reshape(halo, 8, NZ)
    fill_sides(wide, halo, sides)


def fill_flat(wide, below, own, above, low, high):
    wide[...] = jnp.zeros(wide.shape, F32)
    for x in range(LX):
        wide[NEAR + x, 0:FAR] = below[x, pl.ds(2 * HALF + BLOCK, LY), :]
        wide[NEAR + x, FAR:FAR + LY] = own[x, pl.ds(3 * BLOCK, LY), :]
        wide[NEAR + x, FAR + LY:] = above[x, pl.ds(2 * HALF + BLOCK, LY), :]
    for d, more, place in SIDE_SPANS:
        for i in range(LY + 2 * more):
            tile, row = SIDE_SIZE + (place + i) // 8, (place + i) % 8
            y = FAR - more + i
            wide[NEAR - d, pl.ds(y, 1), :] = low[tile, pl.ds(row, 1), :]
            wide[NEAR + LX - 1 + d, pl.ds(y, 1), :] = high[tile, pl.ds(row, 1), :]


def fill_tables(coef, skip, table_re, table_im, diag_re, diag_im):
    value = coef[...]
    real = 6.0 - value
    imag = 0.5 * value
    scale = jnp.where(value > 0.0, 0.8 / (real * real + imag * imag), 0.0)
    diag_re[...] = real * scale
    diag_im[...] = imag * scale
    sign = jnp.where(lax.broadcasted_iota(jnp.int32, (8, NZ), 0) < 4, 1.0, -1.0)
    size_x, size_y = table_re.shape[:2]

    def body(x, carry):
        for y in range(size_y):
            spot = pl.ds(y + skip, 1)
            table_re[x, y] = jnp.broadcast_to(diag_re[x, spot, :], (8, NZ))
            table_im[x, y] = jnp.broadcast_to(diag_im[x, spot, :], (8, NZ)) * sign
        return carry

    lax.fori_loop(0, size_x, body, 0, unroll=True)


def depth_sum(value):
    lane = lax.broadcasted_iota(jnp.int32, value.shape, 1)
    above = jnp.where(lane == 0, 0.0, pltpu.roll(value, 1, 1))
    below = jnp.where(lane == NZ - 1, 0.0, pltpu.roll(value, NZ - 1, 1))
    return above + below


def smooth(block, coef, skip, table_re, table_im, first, second, store):
    size_x, size_y = block.shape[:2]

    def solve(value, x, y):
        return table_re[x, y] * value + table_im[x, y] * pltpu.roll(value, 4, 0)

    def planes(k, body):
        lax.fori_loop(k, size_x - k, functools.partial(body, k, size_y - k), 0, unroll=True)

    def start(low, high, x, carry):
        for y in range(low, high):
            first[x, y] = solve(block[x, y], x, y)
        return carry

    def around(ref, x, low, high):
        line = [ref[x, y] for y in range(low - 1, high + 1)]
        for y in range(low, high):
            mid = line[y - low + 1]
            total = ref[x - 1, y] + ref[x + 1, y] + line[y - low] + line[y - low + 2]
            yield y, mid, total + depth_sum(mid)

    planes(0, start)
    here, there = first, second
    for k in range(1, 4):
        def sweep(low, high, x, carry, here=here, there=there):
            for y, mid, total in around(here, x, low, high):
                there[x, y] = 0.2 * mid + solve(block[x, y] + total, x, y)
            return carry

        planes(k, sweep)
        here, there = there, here

    def image(x, carry):
        for y, mid, total in around(here, x, 4, size_y - 4):
            diag = 6.0 - coef[x, pl.ds(y + skip, 1), :]
            store(x - 4, y - 4, diag * mid - total)
        return carry

    lax.fori_loop(4, size_x - 4, image, 0, unroll=True)


def wide_shape(halo):
    return (LX + 2 * NEAR, LY + 2 * halo)


FLAT = pltpu.VMEM((*wide_shape(FAR), NZ), F32)


def smooth_scratch(halo):
    return [pltpu.VMEM((*wide_shape(halo), 8, NZ), F32)] * 5 + [FLAT] * 2


def first_kernel(own, below, above, low, high, w, coef, out_right, out_left, block, first, second,
                 table_re, table_im, diag_re, diag_im):
    fill_flat(coef, below, own, above, low, high)
    fill_tables(coef, 0, table_re, table_im, diag_re, diag_im)
    rows = [(below, 2 * HALF), (own, 2 * BLOCK), (above, 2 * HALF)]
    fill_block(block, FAR, rows, FAR, [(low, high, 0, SIDE_SPANS)])

    def store(x, y, value):
        w[x, y] = value

    smooth(block, coef, 0, table_re, table_im, first, second, store)
    for d, more, place in NEAR_SPANS:
        count = LY + 2 * more
        out_right[pl.ds(place, count)] = w[LX - d, pl.ds(NEAR - more, count)]
        out_left[pl.ds(place, count)] = w[d - 1, pl.ds(NEAR - more, count)]


def first_image(*args):
    side = jax.ShapeDtypeStruct((NEAR_SIZE, 8, NZ), F32)
    return pl.pallas_call(
        first_kernel,
        out_shape=(jax.ShapeDtypeStruct((LX, LY + 2 * NEAR, 8, NZ), F32),
                   jax.ShapeDtypeStruct((*wide_shape(FAR), NZ), F32), side, side),
        in_specs=[VMEM] * 5,
        out_specs=(VMEM,) * 4,
        scratch_shapes=smooth_scratch(FAR),
        compiler_params=pltpu.CompilerParams(vmem_limit_bytes=16 << 20),
        cost_estimate=pl.CostEstimate(flops=12_000_000, bytes_accessed=18_000_000, transcendentals=0),
        name="first_image",
    )(*args)


def old_kernel(coef, own, below, above, low, high, first_low, first_high, out, block, first, second,
               table_re, table_im, diag_re, diag_im):
    fill_tables(coef, FAR - NEAR, table_re, table_im, diag_re, diag_im)
    for group in range(2):
        rows = [(below, group * HALF), (own, group * BLOCK), (above, group * HALF)]
        if group == 0:
            sides = [(low, high, 0, NEAR_SPANS[:-1]),
                     (first_low, first_high, SIDE_SIZE + FLAT_TILES - SPLIT, NEAR_SPANS[-1:])]
        else:
            sides = [(low, high, SPLIT, NEAR_SPANS)]
        fill_block(block, NEAR, rows, NEAR, sides)

        def store(x, y, value, group=group):
            out[x, pl.ds(group * BLOCK + y * 8, 8), :] = value

        smooth(block, coef, FAR - NEAR, table_re, table_im, first, second, store)


def old_images(*args):
    return pl.pallas_call(
        old_kernel,
        out_shape=jax.ShapeDtypeStruct((LX, 2 * BLOCK, NZ), F32),
        in_specs=[VMEM] * 8,
        out_specs=VMEM,
        scratch_shapes=smooth_scratch(NEAR),
        compiler_params=pltpu.CompilerParams(vmem_limit_bytes=16 << 20),
        cost_estimate=pl.CostEstimate(flops=12_000_000, bytes_accessed=24_000_000, transcendentals=0),
        name="old_images",
    )(*args)


def split3(value):
    high = value.astype(BF16)
    rest = value - high.astype(F32)
    middle = rest.astype(BF16)
    low = (rest - middle.astype(F32)).astype(BF16)
    return high, middle, low


def basis_plane(start, w, old_image, w_image, x):
    refs = [(start, 0), (start, LY), (start, 2 * LY), (w, None), (old_image, 0), (old_image, LY), (w_image, 0)]
    rows = []
    for ref, first in refs:
        if first is None:
            tiles = [ref[x, NEAR + y] for y in range(LY)]
        else:
            tiles = [ref[x, pl.ds((first + y) * 8, 8), :] for y in range(LY)]
        rows.append(jnp.concatenate(tiles, axis=1))
    rows.append(jnp.zeros((8, LY * NZ), F32))
    return jnp.concatenate(rows, axis=0)


def lane_roll(value, amount):
    return pltpu.roll(value, amount % NZ, 1)


SLOTS = [(0, 0), (0, 56), (1, 0), (1, 40), (1, 72), (1, 96), (0, 104)]


def pack_gram(gram):
    lane = lax.broadcasted_iota(jnp.int32, (8, NZ), 1)
    row = lax.broadcasted_iota(jnp.int32, (8, NZ), 0)
    packed = jnp.zeros((8, NZ), F32)
    for b in range(BLOCKS):
        rows = gram[8 * b:8 * b + 8]
        turned = jnp.where(lane % 8 < 4, lane_roll(rows, -4), -lane_roll(rows, 4))
        both = rows + pltpu.roll(turned, 4, 0)
        half, start = SLOTS[b]
        moved = lane_roll(both, start - 8 * b)
        if half:
            moved = pltpu.roll(moved, 4, 0)
        keep = (lane >= start) & (lane < start + 8 * (BLOCKS - b)) & (row // 4 == half)
        packed = packed + jnp.where(keep, moved, 0.0)
    return packed


def unpack_gram(packed):
    lane = lax.broadcasted_iota(jnp.int32, (8, NZ), 1)
    row = lax.broadcasted_iota(jnp.int32, (8, NZ), 0)
    rows = []
    for b in range(BLOCKS):
        half, start = SLOTS[b]
        moved = lane_roll(packed, 8 * b - start)
        if half:
            moved = pltpu.roll(moved, 4, 0)
        keep = (lane >= 8 * b) & (lane < 8 * BLOCKS) & (row < 4)
        moved = jnp.where(keep, moved, 0.0)
        turned = jnp.where(lane % 8 < 4, -lane_roll(moved, -4), lane_roll(moved, 4))
        rows.append(moved + pltpu.roll(turned, 4, 0))
    rows.append(jnp.zeros((NZ - 8 * BLOCKS, NZ), F32))
    upper = jnp.concatenate(rows, axis=0)
    tall = lax.broadcasted_iota(jnp.int32, (NZ, NZ), 0)
    wide = lax.broadcasted_iota(jnp.int32, (NZ, NZ), 1)
    return jnp.where(tall // 8 <= wide // 8, upper, upper.T)


def gram_kernel(peers, w, coef, low, high, start, old_image, w_image, out,
                block, first, second, table_re, table_im, diag_re, diag_im):
    fill_tables(coef, FAR - NEAR, table_re, table_im, diag_re, diag_im)
    block[...] = jnp.zeros(block.shape, F32)
    for x in range(LX):
        block[NEAR + x] = w[x]
    fill_sides(block, NEAR, [(low, high, 0, NEAR_SPANS)])

    def store(x, y, value):
        w_image[x, pl.ds(y * 8, 8), :] = value

    smooth(block, coef, FAR - NEAR, table_re, table_im, first, second, store)

    def plane(x, total):
        stacked = jnp.concatenate(split3(basis_plane(start, w, old_image, w_image, x)), axis=0)
        return total + lax.dot_general(stacked, stacked, (((1,), (1,)), ((), ())), preferred_element_type=F32)

    total = lax.fori_loop(0, LX, plane, jnp.zeros((3 * ROWS, 3 * ROWS), F32), unroll=True)
    tall = total[0:ROWS] + total[ROWS:2 * ROWS] + total[2 * ROWS:3 * ROWS]
    gram = tall[:, 0:ROWS] + tall[:, ROWS:2 * ROWS] + tall[:, 2 * ROWS:3 * ROWS]
    gram = jnp.concatenate([gram, jnp.zeros((ROWS, NZ - ROWS), F32)], axis=1)
    packed = pack_gram(gram)
    for peer in range(peers):
        out[peer] = packed


def image_and_gram(peers, *args):
    return pl.pallas_call(
        functools.partial(gram_kernel, peers),
        out_shape=(jax.ShapeDtypeStruct((LX, LY * 8, NZ), F32),
                   jax.ShapeDtypeStruct((peers, 8, NZ), F32)),
        in_specs=[VMEM] * 6,
        out_specs=(VMEM, VMEM),
        scratch_shapes=smooth_scratch(NEAR),
        compiler_params=pltpu.CompilerParams(vmem_limit_bytes=32 << 20),
        name="image_and_gram",
    )(*args)


def sum_kernel(parts, out):
    total = jnp.sum(parts[...], axis=0)
    for peer in range(out.shape[0]):
        out[peer] = total


def sum_and_spread(parts, peers):
    return pl.pallas_call(
        sum_kernel,
        out_shape=jax.ShapeDtypeStruct((peers, 8, NZ), F32),
        in_specs=[VMEM],
        out_specs=VMEM,
        compiler_params=pltpu.CompilerParams(vmem_limit_bytes=1 << 20),
        name="sum_and_spread",
    )(parts)


def exact(left, right, dims):
    parts = [part.astype(F32) for part in split3(left)]
    stacked = jnp.concatenate([*parts, jnp.zeros((8, NZ), F32)], axis=0).astype(BF16)
    high, middle, low = (
        lax.dot_general(stacked, part, (dims, ((), ())), preferred_element_type=F32) for part in split3(right)
    )
    small = low[0:8] + middle[8:16] + high[16:24]
    return small + (middle[0:8] + high[8:16]) + high[0:8]


def mul(left, right):
    return exact(left, right, ((1,), (0,)))


def mul_t(left, right):
    return exact(left, right, ((1,), (1,)))


def inverse_factor(gram):
    lane = lax.broadcasted_iota(jnp.int32, (8, NZ), 1)
    row = lax.broadcasted_iota(jnp.int32, (8, NZ), 0)
    work = jnp.where(lane < 8, gram, jnp.where(lane == row + 8, 1.0, 0.0))
    pivots = jnp.ones((8, NZ), F32)
    for s in range(4):
        pivot = jnp.broadcast_to(work[s:s + 1, s:s + 1], (8, NZ))
        pivots = jnp.where(row % 4 == s, pivot, pivots)
        if s < 3:
            change = work[:, s:s + 1] * work[s:s + 1, :] + work[:, 4 + s:5 + s] * work[4 + s:5 + s, :]
            work = jnp.where(row % 4 > s, work - change / pivot, work)
    return jnp.where(lane < 8, lane_roll(work, -8), 0.0) / jnp.sqrt(pivots)


def at_row(rows, start):
    parts = [rows, jnp.zeros((NZ - 8 - start, NZ), F32)]
    if start:
        parts.insert(0, jnp.zeros((start, NZ), F32))
    return jnp.concatenate(parts, axis=0)


def coefficients(gram):
    lane = lax.broadcasted_iota(jnp.int32, (8, NZ), 1)
    row = lax.broadcasted_iota(jnp.int32, (8, NZ), 0)
    new_at = 8 * BLOCKS

    once = jnp.where(lane < 24, gram[24:32], 0.0)
    again = jnp.where(lane < 24, mul(once, gram), 0.0)
    rows = jnp.where(lane == row + 24, 1.0, 0.0) - (2.0 * once - again)
    rows_gram = mul(rows, gram)
    spread = at_row(rows, 0)
    factor = inverse_factor(mul_t(rows_gram, spread))
    new = mul(factor, spread)
    new_gram = mul(factor, at_row(rows_gram, 0))
    new_rows = at_row(new, new_at)
    border = at_row(new_gram + mul_t(new_gram, new_rows), new_at)
    body = jnp.concatenate([gram[0:new_at], new_gram, gram[new_at + 8:]], axis=0)
    image = (jnp.where((lane >= 32) & (lane < 48), lane_roll(new, 32), 0.0)
             + jnp.where((lane >= 24) & (lane < 32), lane_roll(new, 8), 0.0)
             + jnp.where((lane >= 48) & (lane < 56), lane_roll(new, 24), 0.0))
    inside = ((lane >= 8) & (lane < 24)) | ((lane >= new_at) & (lane < new_at + 8))

    def times_gram(value):
        return mul(value, body) + mul_t(value, border)

    once = jnp.where(inside, times_gram(image), 0.0)
    again = jnp.where(inside, times_gram(once), 0.0)
    rows = image - (2.0 * once - again)
    spread = at_row(rows, 0)
    newest = mul(inverse_factor(mul_t(times_gram(rows), spread)), spread)
    on_new = jnp.where((lane >= new_at) & (lane < new_at + 8), newest, 0.0)
    return new, newest - on_new + mul(on_new, new_rows)


def final_kernel(cells, parts, start, w, old_image, w_image, out):
    gram = unpack_gram(jnp.sum(parts[...], axis=0) * (1.0 / cells))
    new, newest = coefficients(gram)
    mapping = jnp.concatenate([new, newest], axis=0)[:, 0:ROWS]
    pieces = [jnp.concatenate([piece] * 3, axis=1) for piece in split3(mapping)]
    stacked_map = jnp.concatenate(pieces, axis=0)

    def plane(x, carry):
        stacked = jnp.concatenate(split3(basis_plane(start, w, old_image, w_image, x)), axis=0)
        full = lax.dot_general(stacked_map, stacked, (((1,), (0,)), ((), ())), preferred_element_type=F32)
        result = full[32:48] + full[16:32] + full[0:16]
        for k in range(2):
            tiles = jnp.stack([result[8 * k:8 * k + 8, y * NZ:(y + 1) * NZ] for y in range(LY)])
            out[k, :, x] = jnp.swapaxes(tiles, 0, 1)
        return carry

    lax.fori_loop(0, LX, plane, 0, unroll=True)


def finish(cells, *args):
    return pl.pallas_call(
        functools.partial(final_kernel, cells),
        out_shape=jax.ShapeDtypeStruct((2, 8, LX, LY, NZ), F32),
        in_specs=[VMEM] * 5,
        out_specs=VMEM,
        compiler_params=pltpu.CompilerParams(vmem_limit_bytes=32 << 20),
        name="finish",
    )(*args)


GX = ("z", "core")


def from_both(axis, count, to_higher, to_lower, step=1):
    return (
        lax.ppermute(to_higher, axis, [(i, i + step) for i in range(count - step)]),
        lax.ppermute(to_lower, axis, [(i + step, i) for i in range(count - step)]),
    )


def per_device(nx, ny, nz, prior, coefficient):
    cells = coefficient.size * nx * ny
    by_cell = prior.transpose(3, 0, 4, 1, 2, 5).reshape(LX, 3 * LY * 8, NZ)
    start = jnp.concatenate([by_cell, coefficient], axis=1)
    up = jnp.concatenate([start[:, HALF:BLOCK], start[:, BLOCK + HALF:]], axis=1)
    down = jnp.concatenate([start[:, :HALF], start[:, BLOCK:BLOCK + HALF], start[:, 2 * BLOCK:]], axis=1)
    rims = from_both("gy", ny, up, down)
    right, left, old_right, old_left = pack_all(start, *rims)
    sides = from_both(GX, nx, right, left)
    old_sides = from_both(GX, nx, old_right, old_left)
    w, coef, w_right, w_left = first_image(start, *rims, *sides)
    w_sides = from_both(GX, nx, w_right, w_left)
    old_image = old_images(coef, start, *rims, *old_sides, *sides)

    w_image, spread = image_and_gram(2 * ny, w, coef, *w_sides, start, old_image)
    got = lax.all_to_all(spread, ("core", "gy"), 0, 0)
    got = lax.all_to_all(sum_and_spread(got, nz), "z", 0, 0)
    out = finish(cells, got, start, w, old_image, w_image)
    return out.reshape(2, 2, 4, LX, LY, NZ)


def solution(mesh):
    nx, ny = mesh.shape["gx"], mesh.shape["gy"]
    fine = Mesh(np.asarray(mesh.devices).reshape(nx // 2, 2, ny), ("z", "core", "gy"))
    in_specs = (P(None, None, None, GX, "gy", None), P(GX, "gy", None))
    out_specs = P(None, None, None, GX, "gy", None)
    return jax.shard_map(
        functools.partial(per_device, nx, ny, nx // 2),
        mesh=fine, in_specs=in_specs, out_specs=out_specs, check_vma=False,
    )
```

```python
import functools

import jax
import jax.numpy as jnp
import numpy as np
from jax import lax
from jax.experimental import pallas as pl
from jax.experimental.pallas import tpu as pltpu
from jax.sharding import Mesh, PartitionSpec as P

LX, LY, NZ = 4, 8, 128
NEAR, FAR = 4, 8
BLOCKS = 7
ROWS = 64
F32 = jnp.float32
BF16 = jnp.bfloat16
VMEM = pl.BlockSpec(memory_space=pltpu.VMEM)


BLOCK = LY * 8
HALF = NEAR * 8


def spans(halo, begin, end):
    found, place = [], 0
    for d in range(begin + 1, end + 1):
        found.append((d, halo - d, place))
        place += LY + 2 * (halo - d)
    return found, place


NEAR_SPANS, NEAR_SIZE = spans(NEAR, 0, LX)
SIDE_SPANS, SIDE_SIZE = spans(FAR, 0, LX)
FLAT_TILES = -(-SIDE_SIZE // 8)
FIRST_TILES = SIDE_SIZE + FLAT_TILES
SECOND_TILES = 3 * NEAR_SIZE


def pack_columns(out, start, found, to_higher, rows, reach):
    (below, low_row), (own, own_row), (above, high_row) = rows
    for d, more, place in found:
        x = LX - 1 - (d - 1) % LX if to_higher else (d - 1) % LX
        spot = start + place
        size = more * 8
        if more:
            out[pl.ds(spot, more)] = below[x, pl.ds(low_row + reach * 8 - size, size), :].reshape(more, 8, NZ)
            out[pl.ds(spot + more + LY, more)] = above[x, pl.ds(high_row, size), :].reshape(more, 8, NZ)
        out[pl.ds(spot + more, LY)] = own[x, pl.ds(own_row, BLOCK), :].reshape(LY, 8, NZ)


def pack_coefficient(out, start, found, to_higher, below, own, above):
    for d, more, place in found:
        x = LX - 1 - (d - 1) % LX if to_higher else (d - 1) % LX
        for y in range(-more, LY + more):
            if y < 0:
                ref, row = below, 2 * HALF + BLOCK + LY + y
            elif y < LY:
                ref, row = own, 3 * BLOCK + y
            else:
                ref, row = above, 2 * HALF + BLOCK + y - LY
            spot = place + more + y
            out[start + spot // 8, pl.ds(spot % 8, 1), :] = ref[x, pl.ds(row, 1), :]


def column_kernel(own, below, above, right, left):
    for out, to_higher in ((right, True), (left, False)):
        rows = [(below, 2 * HALF), (own, 2 * BLOCK), (above, 2 * HALF)]
        pack_columns(out, 0, SIDE_SPANS, to_higher, rows, FAR)
        if SIDE_SIZE % 8:
            out[SIDE_SIZE + FLAT_TILES - 1] = jnp.zeros((8, NZ), F32)
        pack_coefficient(out, SIDE_SIZE, SIDE_SPANS, to_higher, below, own, above)


def pack_recent(*args):
    shape = jax.ShapeDtypeStruct((FIRST_TILES, 8, NZ), F32)
    return pl.pallas_call(
        column_kernel,
        out_shape=(shape, shape),
        in_specs=[VMEM] * 3,
        out_specs=(VMEM, VMEM),
        compiler_params=pltpu.CompilerParams(vmem_limit_bytes=1 << 20),
        name="pack_recent",
    )(*args)


def old_rows(below, own, above, group):
    return [(below, group * HALF), (own, group * BLOCK), (above, group * HALF)]


def fill_sides(wide, halo, sides):
    for low, high, start, found in sides:
        for d, more, place in found:
            count = LY + 2 * more
            begin = halo - more
            wide[NEAR - d, begin:begin + count] = low[pl.ds(start + place, count)]
            wide[NEAR + LX - 1 + d, begin:begin + count] = high[pl.ds(start + place, count)]


def fill_block(wide, halo, rows, reach, sides):
    (below, low_row), (own, own_row), (above, high_row) = rows
    wide[...] = jnp.zeros(wide.shape, F32)
    for x in range(LX):
        size = halo * 8
        wide[NEAR + x, 0:halo] = below[x, pl.ds(low_row + reach * 8 - size, size), :].reshape(halo, 8, NZ)
        wide[NEAR + x, halo:halo + LY] = own[x, pl.ds(own_row, BLOCK), :].reshape(LY, 8, NZ)
        wide[NEAR + x, halo + LY:] = above[x, pl.ds(high_row, size), :].reshape(halo, 8, NZ)
    fill_sides(wide, halo, sides)


def fill_flat(wide, below, own, above, low, high):
    wide[...] = jnp.zeros(wide.shape, F32)
    for x in range(LX):
        wide[NEAR + x, 0:FAR] = below[x, pl.ds(2 * HALF + BLOCK, LY), :]
        wide[NEAR + x, FAR:FAR + LY] = own[x, pl.ds(3 * BLOCK, LY), :]
        wide[NEAR + x, FAR + LY:] = above[x, pl.ds(2 * HALF + BLOCK, LY), :]
    for d, more, place in SIDE_SPANS:
        for i in range(LY + 2 * more):
            tile, row = SIDE_SIZE + (place + i) // 8, (place + i) % 8
            y = FAR - more + i
            wide[NEAR - d, pl.ds(y, 1), :] = low[tile, pl.ds(row, 1), :]
            wide[NEAR + LX - 1 + d, pl.ds(y, 1), :] = high[tile, pl.ds(row, 1), :]


def fill_tables(coef, skip, table_re, table_im, diag_re, diag_im):
    value = coef[...]
    real = 6.0 - value
    imag = 0.5 * value
    scale = jnp.where(value > 0.0, 0.8 / (real * real + imag * imag), 0.0)
    diag_re[...] = real * scale
    diag_im[...] = imag * scale
    sign = jnp.where(lax.broadcasted_iota(jnp.int32, (8, NZ), 0) < 4, 1.0, -1.0)
    size_x, size_y = table_re.shape[:2]

    def body(x, carry):
        for y in range(size_y):
            spot = pl.ds(y + skip, 1)
            table_re[x, y] = jnp.broadcast_to(diag_re[x, spot, :], (8, NZ))
            table_im[x, y] = jnp.broadcast_to(diag_im[x, spot, :], (8, NZ)) * sign
        return carry

    lax.fori_loop(0, size_x, body, 0, unroll=True)


def depth_sum(value):
    lane = lax.broadcasted_iota(jnp.int32, value.shape, 1)
    above = jnp.where(lane == 0, 0.0, pltpu.roll(value, 1, 1))
    below = jnp.where(lane == NZ - 1, 0.0, pltpu.roll(value, NZ - 1, 1))
    return above + below


def smooth(block, coef, skip, table_re, table_im, first, second, store):
    size_x, size_y = block.shape[:2]

    def solve(value, x, y):
        return table_re[x, y] * value + table_im[x, y] * pltpu.roll(value, 4, 0)

    def planes(k, body):
        lax.fori_loop(k, size_x - k, functools.partial(body, k, size_y - k), 0, unroll=True)

    def start(low, high, x, carry):
        for y in range(low, high):
            first[x, y] = solve(block[x, y], x, y)
        return carry

    def around(ref, x, low, high):
        line = [ref[x, y] for y in range(low - 1, high + 1)]
        for y in range(low, high):
            mid = line[y - low + 1]
            total = ref[x - 1, y] + ref[x + 1, y] + line[y - low] + line[y - low + 2]
            yield y, mid, total + depth_sum(mid)

    planes(0, start)
    here, there = first, second
    for k in range(1, 4):
        def sweep(low, high, x, carry, here=here, there=there):
            for y, mid, total in around(here, x, low, high):
                there[x, y] = 0.2 * mid + solve(block[x, y] + total, x, y)
            return carry

        planes(k, sweep)
        here, there = there, here

    def image(x, carry):
        for y, mid, total in around(here, x, 4, size_y - 4):
            diag = 6.0 - coef[x, pl.ds(y + skip, 1), :]
            store(x - 4, y - 4, diag * mid - total)
        return carry

    lax.fori_loop(4, size_x - 4, image, 0, unroll=True)


def wide_shape(halo):
    return (LX + 2 * NEAR, LY + 2 * halo)


FLAT = pltpu.VMEM((*wide_shape(FAR), NZ), F32)


def smooth_scratch(halo):
    return [pltpu.VMEM((*wide_shape(halo), 8, NZ), F32)] * 5 + [FLAT] * 2


def first_kernel(own, below, above, low, high, w, coef, out_right, out_left, block, first, second,
                 table_re, table_im, diag_re, diag_im):
    fill_flat(coef, below, own, above, low, high)
    fill_tables(coef, 0, table_re, table_im, diag_re, diag_im)
    rows = [(below, 2 * HALF), (own, 2 * BLOCK), (above, 2 * HALF)]
    fill_block(block, FAR, rows, FAR, [(low, high, 0, SIDE_SPANS)])

    def store(x, y, value):
        w[x, y] = value

    smooth(block, coef, 0, table_re, table_im, first, second, store)
    for group in range(2):
        rows = old_rows(below, own, above, group)
        pack_columns(out_right, group * NEAR_SIZE, NEAR_SPANS, True, rows, NEAR)
        pack_columns(out_left, group * NEAR_SIZE, NEAR_SPANS, False, rows, NEAR)
    for d, more, place in NEAR_SPANS:
        count, spot = LY + 2 * more, 2 * NEAR_SIZE + place
        out_right[pl.ds(spot, count)] = w[LX - d, pl.ds(NEAR - more, count)]
        out_left[pl.ds(spot, count)] = w[d - 1, pl.ds(NEAR - more, count)]


def first_image(*args):
    side = jax.ShapeDtypeStruct((SECOND_TILES, 8, NZ), F32)
    return pl.pallas_call(
        first_kernel,
        out_shape=(jax.ShapeDtypeStruct((LX, LY + 2 * NEAR, 8, NZ), F32),
                   jax.ShapeDtypeStruct((*wide_shape(FAR), NZ), F32), side, side),
        in_specs=[VMEM] * 5,
        out_specs=(VMEM,) * 4,
        scratch_shapes=smooth_scratch(FAR),
        compiler_params=pltpu.CompilerParams(vmem_limit_bytes=16 << 20),
        cost_estimate=pl.CostEstimate(flops=12_000_000, bytes_accessed=18_000_000, transcendentals=0),
        name="first_image",
    )(*args)


def split3(value):
    high = value.astype(BF16)
    rest = value - high.astype(F32)
    middle = rest.astype(BF16)
    low = (rest - middle.astype(F32)).astype(BF16)
    return high, middle, low


def basis_plane(start, w, old_image, w_image, x):
    refs = [(start, 0), (start, LY), (start, 2 * LY), (w, None), (old_image, 0), (old_image, LY), (w_image, 0)]
    rows = []
    for ref, first in refs:
        if first is None:
            tiles = [ref[x, NEAR + y] for y in range(LY)]
        else:
            tiles = [ref[x, pl.ds((first + y) * 8, 8), :] for y in range(LY)]
        rows.append(jnp.concatenate(tiles, axis=1))
    rows.append(jnp.zeros((8, LY * NZ), F32))
    return jnp.concatenate(rows, axis=0)


def lane_roll(value, amount):
    return pltpu.roll(value, amount % NZ, 1)


SLOTS = [(0, 0), (0, 56), (1, 0), (1, 40), (1, 72), (1, 96), (0, 104)]


def pack_gram(gram):
    lane = lax.broadcasted_iota(jnp.int32, (8, NZ), 1)
    row = lax.broadcasted_iota(jnp.int32, (8, NZ), 0)
    packed = jnp.zeros((8, NZ), F32)
    for b in range(BLOCKS):
        rows = gram[8 * b:8 * b + 8]
        turned = jnp.where(lane % 8 < 4, lane_roll(rows, -4), -lane_roll(rows, 4))
        both = rows + pltpu.roll(turned, 4, 0)
        half, start = SLOTS[b]
        moved = lane_roll(both, start - 8 * b)
        if half:
            moved = pltpu.roll(moved, 4, 0)
        keep = (lane >= start) & (lane < start + 8 * (BLOCKS - b)) & (row // 4 == half)
        packed = packed + jnp.where(keep, moved, 0.0)
    return packed


def unpack_gram(packed):
    lane = lax.broadcasted_iota(jnp.int32, (8, NZ), 1)
    row = lax.broadcasted_iota(jnp.int32, (8, NZ), 0)
    rows = []
    for b in range(BLOCKS):
        half, start = SLOTS[b]
        moved = lane_roll(packed, 8 * b - start)
        if half:
            moved = pltpu.roll(moved, 4, 0)
        keep = (lane >= 8 * b) & (lane < 8 * BLOCKS) & (row < 4)
        moved = jnp.where(keep, moved, 0.0)
        turned = jnp.where(lane % 8 < 4, -lane_roll(moved, -4), lane_roll(moved, 4))
        rows.append(moved + pltpu.roll(turned, 4, 0))
    rows.append(jnp.zeros((NZ - 8 * BLOCKS, NZ), F32))
    upper = jnp.concatenate(rows, axis=0)
    tall = lax.broadcasted_iota(jnp.int32, (NZ, NZ), 0)
    wide = lax.broadcasted_iota(jnp.int32, (NZ, NZ), 1)
    return jnp.where(tall // 8 <= wide // 8, upper, upper.T)


def gram_kernel(peers, w, coef, low, high, start, below, above, old_image, w_image, out,
                block, first, second, table_re, table_im, diag_re, diag_im):
    fill_tables(coef, FAR - NEAR, table_re, table_im, diag_re, diag_im)
    for group in range(2):
        rows = old_rows(below, start, above, group)
        fill_block(block, NEAR, rows, NEAR, [(low, high, group * NEAR_SIZE, NEAR_SPANS)])

        def store_old(x, y, value, group=group):
            old_image[x, pl.ds(group * BLOCK + y * 8, 8), :] = value

        smooth(block, coef, FAR - NEAR, table_re, table_im, first, second, store_old)
    block[...] = jnp.zeros(block.shape, F32)
    for x in range(LX):
        block[NEAR + x] = w[x]
    fill_sides(block, NEAR, [(low, high, 2 * NEAR_SIZE, NEAR_SPANS)])

    def store(x, y, value):
        w_image[x, pl.ds(y * 8, 8), :] = value

    smooth(block, coef, FAR - NEAR, table_re, table_im, first, second, store)

    def plane(x, total):
        stacked = jnp.concatenate(split3(basis_plane(start, w, old_image, w_image, x)), axis=0)
        return total + lax.dot_general(stacked, stacked, (((1,), (1,)), ((), ())), preferred_element_type=F32)

    total = lax.fori_loop(0, LX, plane, jnp.zeros((3 * ROWS, 3 * ROWS), F32), unroll=True)
    tall = total[0:ROWS] + total[ROWS:2 * ROWS] + total[2 * ROWS:3 * ROWS]
    gram = tall[:, 0:ROWS] + tall[:, ROWS:2 * ROWS] + tall[:, 2 * ROWS:3 * ROWS]
    gram = jnp.concatenate([gram, jnp.zeros((ROWS, NZ - ROWS), F32)], axis=1)
    packed = pack_gram(gram)
    for peer in range(peers):
        out[peer] = packed


def images_and_gram(peers, *args):
    return pl.pallas_call(
        functools.partial(gram_kernel, peers),
        out_shape=(jax.ShapeDtypeStruct((LX, 2 * BLOCK, NZ), F32),
                   jax.ShapeDtypeStruct((LX, BLOCK, NZ), F32),
                   jax.ShapeDtypeStruct((peers, 8, NZ), F32)),
        in_specs=[VMEM] * 7,
        out_specs=(VMEM,) * 3,
        scratch_shapes=smooth_scratch(NEAR),
        compiler_params=pltpu.CompilerParams(vmem_limit_bytes=24 << 20),
        name="images_and_gram",
    )(*args)


def sum_kernel(parts, out):
    total = jnp.sum(parts[...], axis=0)
    for peer in range(out.shape[0]):
        out[peer] = total


def sum_and_spread(parts, peers):
    return pl.pallas_call(
        sum_kernel,
        out_shape=jax.ShapeDtypeStruct((peers, 8, NZ), F32),
        in_specs=[VMEM],
        out_specs=VMEM,
        compiler_params=pltpu.CompilerParams(vmem_limit_bytes=1 << 20),
        name="sum_and_spread",
    )(parts)


def exact(left, right, dims):
    parts = [part.astype(F32) for part in split3(left)]
    stacked = jnp.concatenate([*parts, jnp.zeros((8, NZ), F32)], axis=0).astype(BF16)
    high, middle, low = (
        lax.dot_general(stacked, part, (dims, ((), ())), preferred_element_type=F32) for part in split3(right)
    )
    small = low[0:8] + middle[8:16] + high[16:24]
    return small + (middle[0:8] + high[8:16]) + high[0:8]


def mul(left, right):
    return exact(left, right, ((1,), (0,)))


def mul_t(left, right):
    return exact(left, right, ((1,), (1,)))


def inverse_factor(gram):
    lane = lax.broadcasted_iota(jnp.int32, (8, NZ), 1)
    row = lax.broadcasted_iota(jnp.int32, (8, NZ), 0)
    work = jnp.where(lane < 8, gram, jnp.where(lane == row + 8, 1.0, 0.0))
    pivots = jnp.ones((8, NZ), F32)
    for s in range(4):
        pivot = jnp.broadcast_to(work[s:s + 1, s:s + 1], (8, NZ))
        pivots = jnp.where(row % 4 == s, pivot, pivots)
        if s < 3:
            change = work[:, s:s + 1] * work[s:s + 1, :] + work[:, 4 + s:5 + s] * work[4 + s:5 + s, :]
            work = jnp.where(row % 4 > s, work - change / pivot, work)
    return jnp.where(lane < 8, lane_roll(work, -8), 0.0) / jnp.sqrt(pivots)


def at_row(rows, start):
    parts = [rows, jnp.zeros((NZ - 8 - start, NZ), F32)]
    if start:
        parts.insert(0, jnp.zeros((start, NZ), F32))
    return jnp.concatenate(parts, axis=0)


def coefficients(gram):
    lane = lax.broadcasted_iota(jnp.int32, (8, NZ), 1)
    row = lax.broadcasted_iota(jnp.int32, (8, NZ), 0)
    new_at = 8 * BLOCKS

    once = jnp.where(lane < 24, gram[24:32], 0.0)
    again = jnp.where(lane < 24, mul(once, gram), 0.0)
    rows = jnp.where(lane == row + 24, 1.0, 0.0) - (2.0 * once - again)
    rows_gram = mul(rows, gram)
    spread = at_row(rows, 0)
    factor = inverse_factor(mul_t(rows_gram, spread))
    new = mul(factor, spread)
    new_gram = mul(factor, at_row(rows_gram, 0))
    new_rows = at_row(new, new_at)
    border = at_row(new_gram + mul_t(new_gram, new_rows), new_at)
    body = jnp.concatenate([gram[0:new_at], new_gram, gram[new_at + 8:]], axis=0)
    image = (jnp.where((lane >= 32) & (lane < 48), lane_roll(new, 32), 0.0)
             + jnp.where((lane >= 24) & (lane < 32), lane_roll(new, 8), 0.0)
             + jnp.where((lane >= 48) & (lane < 56), lane_roll(new, 24), 0.0))
    inside = ((lane >= 8) & (lane < 24)) | ((lane >= new_at) & (lane < new_at + 8))

    def times_gram(value):
        return mul(value, body) + mul_t(value, border)

    once = jnp.where(inside, times_gram(image), 0.0)
    again = jnp.where(inside, times_gram(once), 0.0)
    rows = image - (2.0 * once - again)
    spread = at_row(rows, 0)
    newest = mul(inverse_factor(mul_t(times_gram(rows), spread)), spread)
    on_new = jnp.where((lane >= new_at) & (lane < new_at + 8), newest, 0.0)
    return new, newest - on_new + mul(on_new, new_rows)


def final_kernel(cells, parts, start, w, old_image, w_image, out):
    gram = unpack_gram(jnp.sum(parts[...], axis=0) * (1.0 / cells))
    new, newest = coefficients(gram)
    mapping = jnp.concatenate([new, newest], axis=0)[:, 0:ROWS]
    pieces = [jnp.concatenate([piece] * 3, axis=1) for piece in split3(mapping)]
    stacked_map = jnp.concatenate(pieces, axis=0)

    def plane(x, carry):
        stacked = jnp.concatenate(split3(basis_plane(start, w, old_image, w_image, x)), axis=0)
        full = lax.dot_general(stacked_map, stacked, (((1,), (0,)), ((), ())), preferred_element_type=F32)
        result = full[32:48] + full[16:32] + full[0:16]
        for k in range(2):
            tiles = jnp.stack([result[8 * k:8 * k + 8, y * NZ:(y + 1) * NZ] for y in range(LY)])
            out[k, :, x] = jnp.swapaxes(tiles, 0, 1)
        return carry

    lax.fori_loop(0, LX, plane, 0, unroll=True)


def finish(cells, *args):
    return pl.pallas_call(
        functools.partial(final_kernel, cells),
        out_shape=jax.ShapeDtypeStruct((2, 8, LX, LY, NZ), F32),
        in_specs=[VMEM] * 5,
        out_specs=VMEM,
        compiler_params=pltpu.CompilerParams(vmem_limit_bytes=32 << 20),
        name="finish",
    )(*args)


GX = ("z", "core")


def from_both(axis, count, to_higher, to_lower):
    return (
        lax.ppermute(to_higher, axis, [(i, i + 1) for i in range(count - 1)]),
        lax.ppermute(to_lower, axis, [(i + 1, i) for i in range(count - 1)]),
    )


def per_device(nx, ny, nz, prior, coefficient):
    cells = coefficient.size * nx * ny
    by_cell = prior.transpose(3, 0, 4, 1, 2, 5).reshape(LX, 3 * LY * 8, NZ)
    start = jnp.concatenate([by_cell, coefficient], axis=1)
    up = jnp.concatenate([start[:, HALF:BLOCK], start[:, BLOCK + HALF:]], axis=1)
    down = jnp.concatenate([start[:, :HALF], start[:, BLOCK:BLOCK + HALF], start[:, 2 * BLOCK:]], axis=1)
    rims = from_both("gy", ny, up, down)
    sides = from_both(GX, nx, *pack_recent(start, *rims))
    w, coef, right, left = first_image(start, *rims, *sides)
    sides = from_both(GX, nx, right, left)
    old_image, w_image, spread = images_and_gram(2 * ny, w, coef, *sides, start, *rims)
    got = lax.all_to_all(spread, ("core", "gy"), 0, 0)
    got = lax.all_to_all(sum_and_spread(got, nz), "z", 0, 0)
    out = finish(cells, got, start, w, old_image, w_image)
    return out.reshape(2, 2, 4, LX, LY, NZ)


def solution(mesh):
    nx, ny = mesh.shape["gx"], mesh.shape["gy"]
    fine = Mesh(np.asarray(mesh.devices).reshape(nx // 2, 2, ny), ("z", "core", "gy"))
    in_specs = (P(None, None, None, GX, "gy", None), P(GX, "gy", None))
    out_specs = P(None, None, None, GX, "gy", None)
    return jax.shard_map(
        functools.partial(per_device, nx, ny, nx // 2),
        mesh=fine, in_specs=in_specs, out_specs=out_specs, check_vma=False,
    )
```

```python
import functools

import jax
import jax.numpy as jnp
import numpy as np
from jax import lax
from jax.experimental import pallas as pl
from jax.experimental.pallas import tpu as pltpu
from jax.sharding import Mesh, PartitionSpec as P

LX, LY, NZ = 4, 8, 128
NEAR, FAR = 4, 8
BLOCKS = 7
ROWS = 64
F32 = jnp.float32
BF16 = jnp.bfloat16
VMEM = pl.BlockSpec(memory_space=pltpu.VMEM)


BLOCK = LY * 8
HALF = NEAR * 8


def spans(halo, begin, end):
    found, place = [], 0
    for d in range(begin + 1, end + 1):
        found.append((d, halo - d, place))
        place += LY + 2 * (halo - d)
    return found, place


NEAR_SPANS, NEAR_SIZE = spans(NEAR, 0, LX)
SIDE_SPANS, SIDE_SIZE = spans(FAR, 0, LX)
FLAT_TILES = -(-SIDE_SIZE // 8)
SPLIT = NEAR_SPANS[-1][2]
FIRST_TILES = SIDE_SIZE + FLAT_TILES + NEAR_SIZE - SPLIT
SECOND_TILES = SPLIT + NEAR_SIZE


def sent_plane(inner, d):
    core = lax.axis_index("core")
    far = core if inner else 1 - core
    return (1 - far) * (LX - d) + far * (d - 1)


def halo_plane(inner, d):
    core = lax.axis_index("core")
    far = core if inner else 1 - core
    return (1 - far) * (NEAR + LX - 1 + d) + far * (NEAR - d)


def pack_columns(out, start, found, inner, rows, reach):
    (below, low_row), (own, own_row), (above, high_row) = rows
    for d, more, place in found:
        x = sent_plane(inner, d)
        spot = start + place
        size = more * 8
        if more:
            out[pl.ds(spot, more)] = below[x, pl.ds(low_row + reach * 8 - size, size), :].reshape(more, 8, NZ)
            out[pl.ds(spot + more + LY, more)] = above[x, pl.ds(high_row, size), :].reshape(more, 8, NZ)
        out[pl.ds(spot + more, LY)] = own[x, pl.ds(own_row, BLOCK), :].reshape(LY, 8, NZ)


def pack_coefficient(out, start, found, inner, below, own, above):
    for d, more, place in found:
        x = sent_plane(inner, d)
        for y in range(-more, LY + more):
            if y < 0:
                ref, row = below, 2 * HALF + BLOCK + LY + y
            elif y < LY:
                ref, row = own, 3 * BLOCK + y
            else:
                ref, row = above, 2 * HALF + BLOCK + y - LY
            spot = place + more + y
            out[start + spot // 8, pl.ds(spot % 8, 1), :] = ref[x, pl.ds(row, 1), :]


def column_kernel(own, below, above, outward, inward, old_outward, old_inward):
    for first, second, inner in ((outward, old_outward, False), (inward, old_inward, True)):
        rows = [(below, 2 * HALF), (own, 2 * BLOCK), (above, 2 * HALF)]
        pack_columns(first, 0, SIDE_SPANS, inner, rows, FAR)
        if SIDE_SIZE % 8:
            first[SIDE_SIZE + FLAT_TILES - 1] = jnp.zeros((8, NZ), F32)
        pack_coefficient(first, SIDE_SIZE, SIDE_SPANS, inner, below, own, above)
        rows = [(below, 0), (own, 0), (above, 0)]
        pack_columns(second, 0, NEAR_SPANS[:-1], inner, rows, NEAR)
        pack_columns(first, SIDE_SIZE + FLAT_TILES - SPLIT, NEAR_SPANS[-1:], inner, rows, NEAR)
        rows = [(below, HALF), (own, BLOCK), (above, HALF)]
        pack_columns(second, SPLIT, NEAR_SPANS, inner, rows, NEAR)


def pack_all(*args):
    shapes = tuple(jax.ShapeDtypeStruct((size, 8, NZ), F32) for size in [FIRST_TILES] * 2 + [SECOND_TILES] * 2)
    return pl.pallas_call(
        column_kernel,
        out_shape=shapes,
        in_specs=[VMEM] * 3,
        out_specs=(VMEM,) * 4,
        compiler_params=pltpu.CompilerParams(vmem_limit_bytes=1 << 20),
        name="pack_all",
    )(*args)


def fill_sides(wide, halo, sides):
    for outer, inner, start, found in sides:
        for d, more, place in found:
            count = LY + 2 * more
            begin = halo - more
            wide[halo_plane(False, d), begin:begin + count] = outer[pl.ds(start + place, count)]
            wide[halo_plane(True, d), begin:begin + count] = inner[pl.ds(start + place, count)]


def fill_block(wide, halo, rows, reach, sides):
    (below, low_row), (own, own_row), (above, high_row) = rows
    wide[...] = jnp.zeros(wide.shape, F32)
    for x in range(LX):
        size = halo * 8
        wide[NEAR + x, 0:halo] = below[x, pl.ds(low_row + reach * 8 - size, size), :].reshape(halo, 8, NZ)
        wide[NEAR + x, halo:halo + LY] = own[x, pl.ds(own_row, BLOCK), :].reshape(LY, 8, NZ)
        wide[NEAR + x, halo + LY:] = above[x, pl.ds(high_row, size), :].reshape(halo, 8, NZ)
    fill_sides(wide, halo, sides)


def fill_flat(wide, below, own, above, outer, inner):
    wide[...] = jnp.zeros(wide.shape, F32)
    for x in range(LX):
        wide[NEAR + x, 0:FAR] = below[x, pl.ds(2 * HALF + BLOCK, LY), :]
        wide[NEAR + x, FAR:FAR + LY] = own[x, pl.ds(3 * BLOCK, LY), :]
        wide[NEAR + x, FAR + LY:] = above[x, pl.ds(2 * HALF + BLOCK, LY), :]
    for d, more, place in SIDE_SPANS:
        for i in range(LY + 2 * more):
            tile, row = SIDE_SIZE + (place + i) // 8, (place + i) % 8
            y = FAR - more + i
            wide[halo_plane(False, d), pl.ds(y, 1), :] = outer[tile, pl.ds(row, 1), :]
            wide[halo_plane(True, d), pl.ds(y, 1), :] = inner[tile, pl.ds(row, 1), :]


def fill_tables(coef, skip, table_re, table_im, diag_re, diag_im):
    value = coef[...]
    real = 6.0 - value
    imag = 0.5 * value
    scale = jnp.where(value > 0.0, 0.8 / (real * real + imag * imag), 0.0)
    diag_re[...] = real * scale
    diag_im[...] = imag * scale
    sign = jnp.where(lax.broadcasted_iota(jnp.int32, (8, NZ), 0) < 4, 1.0, -1.0)
    size_x, size_y = table_re.shape[:2]

    def body(x, carry):
        for y in range(size_y):
            spot = pl.ds(y + skip, 1)
            table_re[x, y] = jnp.broadcast_to(diag_re[x, spot, :], (8, NZ))
            table_im[x, y] = jnp.broadcast_to(diag_im[x, spot, :], (8, NZ)) * sign
        return carry

    lax.fori_loop(0, size_x, body, 0, unroll=True)


def depth_sum(value):
    lane = lax.broadcasted_iota(jnp.int32, value.shape, 1)
    above = jnp.where(lane == 0, 0.0, pltpu.roll(value, 1, 1))
    below = jnp.where(lane == NZ - 1, 0.0, pltpu.roll(value, NZ - 1, 1))
    return above + below


def smooth(block, coef, skip, table_re, table_im, first, second, store):
    size_x, size_y = block.shape[:2]

    def solve(value, x, y):
        return table_re[x, y] * value + table_im[x, y] * pltpu.roll(value, 4, 0)

    def planes(k, body):
        lax.fori_loop(k, size_x - k, functools.partial(body, k, size_y - k), 0, unroll=True)

    def start(low, high, x, carry):
        for y in range(low, high):
            first[x, y] = solve(block[x, y], x, y)
        return carry

    def around(ref, x, low, high):
        line = [ref[x, y] for y in range(low - 1, high + 1)]
        for y in range(low, high):
            mid = line[y - low + 1]
            total = ref[x - 1, y] + ref[x + 1, y] + line[y - low] + line[y - low + 2]
            yield y, mid, total + depth_sum(mid)

    planes(0, start)
    here, there = first, second
    for k in range(1, 4):
        def sweep(low, high, x, carry, here=here, there=there):
            for y, mid, total in around(here, x, low, high):
                there[x, y] = 0.2 * mid + solve(block[x, y] + total, x, y)
            return carry

        planes(k, sweep)
        here, there = there, here

    def image(x, carry):
        for y, mid, total in around(here, x, 4, size_y - 4):
            diag = 6.0 - coef[x, pl.ds(y + skip, 1), :]
            store(x - 4, y - 4, diag * mid - total)
        return carry

    lax.fori_loop(4, size_x - 4, image, 0, unroll=True)


def wide_shape(halo):
    return (LX + 2 * NEAR, LY + 2 * halo)


FLAT = pltpu.VMEM((*wide_shape(FAR), NZ), F32)


def smooth_scratch(halo):
    return [pltpu.VMEM((*wide_shape(halo), 8, NZ), F32)] * 5 + [FLAT] * 2


def first_kernel(own, below, above, outer, inner, w, coef, outward, inward, block, first, second,
                 table_re, table_im, diag_re, diag_im):
    fill_flat(coef, below, own, above, outer, inner)
    fill_tables(coef, 0, table_re, table_im, diag_re, diag_im)
    rows = [(below, 2 * HALF), (own, 2 * BLOCK), (above, 2 * HALF)]
    fill_block(block, FAR, rows, FAR, [(outer, inner, 0, SIDE_SPANS)])

    def store(x, y, value):
        w[x, y] = value

    smooth(block, coef, 0, table_re, table_im, first, second, store)
    for d, more, place in NEAR_SPANS:
        count = LY + 2 * more
        outward[pl.ds(place, count)] = w[sent_plane(False, d), pl.ds(NEAR - more, count)]
        inward[pl.ds(place, count)] = w[sent_plane(True, d), pl.ds(NEAR - more, count)]


def first_image(*args):
    side = jax.ShapeDtypeStruct((NEAR_SIZE, 8, NZ), F32)
    return pl.pallas_call(
        first_kernel,
        out_shape=(jax.ShapeDtypeStruct((LX, LY + 2 * NEAR, 8, NZ), F32),
                   jax.ShapeDtypeStruct((*wide_shape(FAR), NZ), F32), side, side),
        in_specs=[VMEM] * 5,
        out_specs=(VMEM,) * 4,
        scratch_shapes=smooth_scratch(FAR),
        compiler_params=pltpu.CompilerParams(vmem_limit_bytes=16 << 20),
        cost_estimate=pl.CostEstimate(flops=12_000_000, bytes_accessed=18_000_000, transcendentals=0),
        name="first_image",
    )(*args)


def old_kernel(coef, own, below, above, outer, inner, first_outer, first_inner, out, block, first, second,
               table_re, table_im, diag_re, diag_im):
    fill_tables(coef, FAR - NEAR, table_re, table_im, diag_re, diag_im)
    for group in range(2):
        rows = [(below, group * HALF), (own, group * BLOCK), (above, group * HALF)]
        if group == 0:
            sides = [(outer, inner, 0, NEAR_SPANS[:-1]),
                     (first_outer, first_inner, SIDE_SIZE + FLAT_TILES - SPLIT, NEAR_SPANS[-1:])]
        else:
            sides = [(outer, inner, SPLIT, NEAR_SPANS)]
        fill_block(block, NEAR, rows, NEAR, sides)

        def store(x, y, value, group=group):
            out[x, pl.ds(group * BLOCK + y * 8, 8), :] = value

        smooth(block, coef, FAR - NEAR, table_re, table_im, first, second, store)


def old_images(*args):
    return pl.pallas_call(
        old_kernel,
        out_shape=jax.ShapeDtypeStruct((LX, 2 * BLOCK, NZ), F32),
        in_specs=[VMEM] * 8,
        out_specs=VMEM,
        scratch_shapes=smooth_scratch(NEAR),
        compiler_params=pltpu.CompilerParams(vmem_limit_bytes=16 << 20),
        cost_estimate=pl.CostEstimate(flops=12_000_000, bytes_accessed=24_000_000, transcendentals=0),
        name="old_images",
    )(*args)


def split3(value):
    high = value.astype(BF16)
    rest = value - high.astype(F32)
    middle = rest.astype(BF16)
    low = (rest - middle.astype(F32)).astype(BF16)
    return high, middle, low


def basis_plane(start, w, old_image, w_image, x):
    refs = [(start, 0), (start, LY), (start, 2 * LY), (w, None), (old_image, 0), (old_image, LY), (w_image, 0)]
    rows = []
    for ref, first in refs:
        if first is None:
            tiles = [ref[x, NEAR + y] for y in range(LY)]
        else:
            tiles = [ref[x, pl.ds((first + y) * 8, 8), :] for y in range(LY)]
        rows.append(jnp.concatenate(tiles, axis=1))
    rows.append(jnp.zeros((8, LY * NZ), F32))
    return jnp.concatenate(rows, axis=0)


def lane_roll(value, amount):
    return pltpu.roll(value, amount % NZ, 1)


SLOTS = [(0, 0), (0, 56), (1, 0), (1, 40), (1, 72), (1, 96), (0, 104)]


def pack_gram(gram):
    lane = lax.broadcasted_iota(jnp.int32, (8, NZ), 1)
    row = lax.broadcasted_iota(jnp.int32, (8, NZ), 0)
    packed = jnp.zeros((8, NZ), F32)
    for b in range(BLOCKS):
        rows = gram[8 * b:8 * b + 8]
        turned = jnp.where(lane % 8 < 4, lane_roll(rows, -4), -lane_roll(rows, 4))
        both = rows + pltpu.roll(turned, 4, 0)
        half, start = SLOTS[b]
        moved = lane_roll(both, start - 8 * b)
        if half:
            moved = pltpu.roll(moved, 4, 0)
        keep = (lane >= start) & (lane < start + 8 * (BLOCKS - b)) & (row // 4 == half)
        packed = packed + jnp.where(keep, moved, 0.0)
    return packed


def unpack_gram(packed):
    lane = lax.broadcasted_iota(jnp.int32, (8, NZ), 1)
    row = lax.broadcasted_iota(jnp.int32, (8, NZ), 0)
    rows = []
    for b in range(BLOCKS):
        half, start = SLOTS[b]
        moved = lane_roll(packed, 8 * b - start)
        if half:
            moved = pltpu.roll(moved, 4, 0)
        keep = (lane >= 8 * b) & (lane < 8 * BLOCKS) & (row < 4)
        moved = jnp.where(keep, moved, 0.0)
        turned = jnp.where(lane % 8 < 4, -lane_roll(moved, -4), lane_roll(moved, 4))
        rows.append(moved + pltpu.roll(turned, 4, 0))
    rows.append(jnp.zeros((NZ - 8 * BLOCKS, NZ), F32))
    upper = jnp.concatenate(rows, axis=0)
    tall = lax.broadcasted_iota(jnp.int32, (NZ, NZ), 0)
    wide = lax.broadcasted_iota(jnp.int32, (NZ, NZ), 1)
    return jnp.where(tall // 8 <= wide // 8, upper, upper.T)


def gram_kernel(peers, w, coef, outer, inner, start, old_image, w_image, out,
                block, first, second, table_re, table_im, diag_re, diag_im):
    fill_tables(coef, FAR - NEAR, table_re, table_im, diag_re, diag_im)
    block[...] = jnp.zeros(block.shape, F32)
    for x in range(LX):
        block[NEAR + x] = w[x]
    fill_sides(block, NEAR, [(outer, inner, 0, NEAR_SPANS)])

    def store(x, y, value):
        w_image[x, pl.ds(y * 8, 8), :] = value

    smooth(block, coef, FAR - NEAR, table_re, table_im, first, second, store)

    def plane(x, total):
        stacked = jnp.concatenate(split3(basis_plane(start, w, old_image, w_image, x)), axis=0)
        return total + lax.dot_general(stacked, stacked, (((1,), (1,)), ((), ())), preferred_element_type=F32)

    total = lax.fori_loop(0, LX, plane, jnp.zeros((3 * ROWS, 3 * ROWS), F32), unroll=True)
    tall = total[0:ROWS] + total[ROWS:2 * ROWS] + total[2 * ROWS:3 * ROWS]
    gram = tall[:, 0:ROWS] + tall[:, ROWS:2 * ROWS] + tall[:, 2 * ROWS:3 * ROWS]
    gram = jnp.concatenate([gram, jnp.zeros((ROWS, NZ - ROWS), F32)], axis=1)
    packed = pack_gram(gram)
    for peer in range(peers):
        out[peer] = packed


def image_and_gram(peers, *args):
    return pl.pallas_call(
        functools.partial(gram_kernel, peers),
        out_shape=(jax.ShapeDtypeStruct((LX, LY * 8, NZ), F32),
                   jax.ShapeDtypeStruct((peers, 8, NZ), F32)),
        in_specs=[VMEM] * 6,
        out_specs=(VMEM, VMEM),
        scratch_shapes=smooth_scratch(NEAR),
        compiler_params=pltpu.CompilerParams(vmem_limit_bytes=32 << 20),
        name="image_and_gram",
    )(*args)


def sum_kernel(parts, out):
    total = jnp.sum(parts[...], axis=0)
    for peer in range(out.shape[0]):
        out[peer] = total


def sum_and_spread(parts, peers):
    return pl.pallas_call(
        sum_kernel,
        out_shape=jax.ShapeDtypeStruct((peers, 8, NZ), F32),
        in_specs=[VMEM],
        out_specs=VMEM,
        compiler_params=pltpu.CompilerParams(vmem_limit_bytes=1 << 20),
        name="sum_and_spread",
    )(parts)


def exact(left, right, dims):
    parts = [part.astype(F32) for part in split3(left)]
    stacked = jnp.concatenate([*parts, jnp.zeros((8, NZ), F32)], axis=0).astype(BF16)
    high, middle, low = (
        lax.dot_general(stacked, part, (dims, ((), ())), preferred_element_type=F32) for part in split3(right)
    )
    small = low[0:8] + middle[8:16] + high[16:24]
    return small + (middle[0:8] + high[8:16]) + high[0:8]


def mul(left, right):
    return exact(left, right, ((1,), (0,)))


def mul_t(left, right):
    return exact(left, right, ((1,), (1,)))


def inverse_factor(gram):
    lane = lax.broadcasted_iota(jnp.int32, (8, NZ), 1)
    row = lax.broadcasted_iota(jnp.int32, (8, NZ), 0)
    work = jnp.where(lane < 8, gram, jnp.where(lane == row + 8, 1.0, 0.0))
    pivots = jnp.ones((8, NZ), F32)
    for s in range(4):
        pivot = jnp.broadcast_to(work[s:s + 1, s:s + 1], (8, NZ))
        pivots = jnp.where(row % 4 == s, pivot, pivots)
        if s < 3:
            change = work[:, s:s + 1] * work[s:s + 1, :] + work[:, 4 + s:5 + s] * work[4 + s:5 + s, :]
            work = jnp.where(row % 4 > s, work - change / pivot, work)
    return jnp.where(lane < 8, lane_roll(work, -8), 0.0) / jnp.sqrt(pivots)


def at_row(rows, start):
    parts = [rows, jnp.zeros((NZ - 8 - start, NZ), F32)]
    if start:
        parts.insert(0, jnp.zeros((start, NZ), F32))
    return jnp.concatenate(parts, axis=0)


def coefficients(gram):
    lane = lax.broadcasted_iota(jnp.int32, (8, NZ), 1)
    row = lax.broadcasted_iota(jnp.int32, (8, NZ), 0)
    new_at = 8 * BLOCKS

    once = jnp.where(lane < 24, gram[24:32], 0.0)
    again = jnp.where(lane < 24, mul(once, gram), 0.0)
    rows = jnp.where(lane == row + 24, 1.0, 0.0) - (2.0 * once - again)
    rows_gram = mul(rows, gram)
    spread = at_row(rows, 0)
    factor = inverse_factor(mul_t(rows_gram, spread))
    new = mul(factor, spread)
    new_gram = mul(factor, at_row(rows_gram, 0))
    new_rows = at_row(new, new_at)
    border = at_row(new_gram + mul_t(new_gram, new_rows), new_at)
    body = jnp.concatenate([gram[0:new_at], new_gram, gram[new_at + 8:]], axis=0)
    image = (jnp.where((lane >= 32) & (lane < 48), lane_roll(new, 32), 0.0)
             + jnp.where((lane >= 24) & (lane < 32), lane_roll(new, 8), 0.0)
             + jnp.where((lane >= 48) & (lane < 56), lane_roll(new, 24), 0.0))
    inside = ((lane >= 8) & (lane < 24)) | ((lane >= new_at) & (lane < new_at + 8))

    def times_gram(value):
        return mul(value, body) + mul_t(value, border)

    once = jnp.where(inside, times_gram(image), 0.0)
    again = jnp.where(inside, times_gram(once), 0.0)
    rows = image - (2.0 * once - again)
    spread = at_row(rows, 0)
    newest = mul(inverse_factor(mul_t(times_gram(rows), spread)), spread)
    on_new = jnp.where((lane >= new_at) & (lane < new_at + 8), newest, 0.0)
    return new, newest - on_new + mul(on_new, new_rows)


def final_kernel(cells, parts, start, w, old_image, w_image, out):
    gram = unpack_gram(jnp.sum(parts[...], axis=0) * (1.0 / cells))
    new, newest = coefficients(gram)
    mapping = jnp.concatenate([new, newest], axis=0)[:, 0:ROWS]
    pieces = [jnp.concatenate([piece] * 3, axis=1) for piece in split3(mapping)]
    stacked_map = jnp.concatenate(pieces, axis=0)

    def plane(x, carry):
        stacked = jnp.concatenate(split3(basis_plane(start, w, old_image, w_image, x)), axis=0)
        full = lax.dot_general(stacked_map, stacked, (((1,), (0,)), ((), ())), preferred_element_type=F32)
        result = full[32:48] + full[16:32] + full[0:16]
        for k in range(2):
            tiles = jnp.stack([result[8 * k:8 * k + 8, y * NZ:(y + 1) * NZ] for y in range(LY)])
            out[k, :, x] = jnp.swapaxes(tiles, 0, 1)
        return carry

    lax.fori_loop(0, LX, plane, 0, unroll=True)


def finish(cells, *args):
    return pl.pallas_call(
        functools.partial(final_kernel, cells),
        out_shape=jax.ShapeDtypeStruct((2, 8, LX, LY, NZ), F32),
        in_specs=[VMEM] * 5,
        out_specs=VMEM,
        compiler_params=pltpu.CompilerParams(vmem_limit_bytes=32 << 20),
        name="finish",
    )(*args)


GX = ("z", "core")


def from_both(axis, count, to_higher, to_lower):
    return (
        lax.ppermute(to_higher, axis, [(i, i + 1) for i in range(count - 1)]),
        lax.ppermute(to_lower, axis, [(i + 1, i) for i in range(count - 1)]),
    )


def exchange(count, outward, inward):
    inner = [(i, i ^ 1) for i in range(count)]
    outer = [(i, i + 1 if i % 2 else i - 1) for i in range(1, count - 1)]
    return lax.ppermute(outward, GX, outer), lax.ppermute(inward, GX, inner)


def per_device(nx, ny, nz, prior, coefficient):
    cells = coefficient.size * nx * ny
    by_cell = prior.transpose(3, 0, 4, 1, 2, 5).reshape(LX, 3 * LY * 8, NZ)
    start = jnp.concatenate([by_cell, coefficient], axis=1)
    up = jnp.concatenate([start[:, HALF:BLOCK], start[:, BLOCK + HALF:]], axis=1)
    down = jnp.concatenate([start[:, :HALF], start[:, BLOCK:BLOCK + HALF], start[:, 2 * BLOCK:]], axis=1)
    rims = from_both("gy", ny, up, down)
    outward, inward, old_outward, old_inward = pack_all(start, *rims)
    sides = exchange(nx, outward, inward)
    old_sides = exchange(nx, old_outward, old_inward)
    w, coef, w_outward, w_inward = first_image(start, *rims, *sides)
    w_sides = exchange(nx, w_outward, w_inward)
    old_image = old_images(coef, start, *rims, *old_sides, *sides)

    w_image, spread = image_and_gram(2 * ny, w, coef, *w_sides, start, old_image)
    got = lax.all_to_all(spread, ("core", "gy"), 0, 0)
    got = lax.all_to_all(sum_and_spread(got, nz), "z", 0, 0)
    out = finish(cells, got, start, w, old_image, w_image)
    return out.reshape(2, 2, 4, LX, LY, NZ)


def solution(mesh):
    nx, ny = mesh.shape["gx"], mesh.shape["gy"]
    fine = Mesh(np.asarray(mesh.devices).reshape(nx // 2, 2, ny), ("z", "core", "gy"))
    in_specs = (P(None, None, None, GX, "gy", None), P(GX, "gy", None))
    out_specs = P(None, None, None, GX, "gy", None)
    return jax.shard_map(
        functools.partial(per_device, nx, ny, nx // 2),
        mesh=fine, in_specs=in_specs, out_specs=out_specs, check_vma=False,
    )
```

```python
import functools

import jax
import jax.numpy as jnp
import numpy as np
from jax import lax
from jax.experimental import pallas as pl
from jax.experimental.pallas import tpu as pltpu
from jax.sharding import Mesh, PartitionSpec as P

LX, LY, NZ = 4, 8, 128
NEAR, FAR = 4, 8
BLOCKS = 7
ROWS = 64
F32 = jnp.float32
BF16 = jnp.bfloat16
VMEM = pl.BlockSpec(memory_space=pltpu.VMEM)


BLOCK = LY * 8
HALF = NEAR * 8


def spans(halo, begin, end):
    found, place = [], 0
    for d in range(begin + 1, end + 1):
        found.append((d, halo - d, place))
        place += LY + 2 * (halo - d)
    return found, place


NEAR_SPANS, NEAR_SIZE = spans(NEAR, 0, LX)
SIDE_SPANS, SIDE_SIZE = spans(FAR, 0, LX)
FLAT_TILES = -(-SIDE_SIZE // 8)
SPLIT = NEAR_SPANS[-1][2]
FIRST_TILES = SIDE_SIZE + FLAT_TILES + NEAR_SIZE - SPLIT
SECOND_TILES = SPLIT + NEAR_SIZE


def sent_plane(inner, d):
    core = lax.axis_index("core")
    far = core if inner else 1 - core
    return (1 - far) * (LX - d) + far * (d - 1)


def halo_plane(inner, d):
    core = lax.axis_index("core")
    far = core if inner else 1 - core
    return (1 - far) * (NEAR + LX - 1 + d) + far * (NEAR - d)


def pack_columns(out, start, found, inner, rows, reach):
    (below, low_row), (own, own_row), (above, high_row) = rows
    for d, more, place in found:
        x = sent_plane(inner, d)
        spot = start + place
        size = more * 8
        if more:
            out[pl.ds(spot, more)] = below[x, pl.ds(low_row + reach * 8 - size, size), :].reshape(more, 8, NZ)
            out[pl.ds(spot + more + LY, more)] = above[x, pl.ds(high_row, size), :].reshape(more, 8, NZ)
        out[pl.ds(spot + more, LY)] = own[x, pl.ds(own_row, BLOCK), :].reshape(LY, 8, NZ)


def pack_coefficient(out, start, found, inner, below, own, above):
    for d, more, place in found:
        x = sent_plane(inner, d)
        for y in range(-more, LY + more):
            if y < 0:
                ref, row = below, 2 * HALF + BLOCK + LY + y
            elif y < LY:
                ref, row = own, 3 * BLOCK + y
            else:
                ref, row = above, 2 * HALF + BLOCK + y - LY
            spot = place + more + y
            out[start + spot // 8, pl.ds(spot % 8, 1), :] = ref[x, pl.ds(row, 1), :]


def column_kernel(own, below, above, outward, inward, old_outward):
    for first, second, later, inner in ((outward, old_outward, 0, False), (inward, inward, FIRST_TILES, True)):
        rows = [(below, 2 * HALF), (own, 2 * BLOCK), (above, 2 * HALF)]
        pack_columns(first, 0, SIDE_SPANS, inner, rows, FAR)
        if SIDE_SIZE % 8:
            first[SIDE_SIZE + FLAT_TILES - 1] = jnp.zeros((8, NZ), F32)
        pack_coefficient(first, SIDE_SIZE, SIDE_SPANS, inner, below, own, above)
        rows = [(below, 0), (own, 0), (above, 0)]
        pack_columns(second, later, NEAR_SPANS[:-1], inner, rows, NEAR)
        pack_columns(first, SIDE_SIZE + FLAT_TILES - SPLIT, NEAR_SPANS[-1:], inner, rows, NEAR)
        rows = [(below, HALF), (own, BLOCK), (above, HALF)]
        pack_columns(second, later + SPLIT, NEAR_SPANS, inner, rows, NEAR)


def pack_all(*args):
    shapes = tuple(jax.ShapeDtypeStruct((size, 8, NZ), F32) for size in (FIRST_TILES, FIRST_TILES + SECOND_TILES, SECOND_TILES))
    return pl.pallas_call(
        column_kernel,
        out_shape=shapes,
        in_specs=[VMEM] * 3,
        out_specs=(VMEM,) * 3,
        compiler_params=pltpu.CompilerParams(vmem_limit_bytes=1 << 20),
        name="pack_all",
    )(*args)


def fill_sides(wide, halo, sides):
    for outer, inner, start, inner_start, found in sides:
        for d, more, place in found:
            count = LY + 2 * more
            begin = halo - more
            wide[halo_plane(False, d), begin:begin + count] = outer[pl.ds(start + place, count)]
            wide[halo_plane(True, d), begin:begin + count] = inner[pl.ds(inner_start + place, count)]


def fill_block(wide, halo, rows, reach, sides):
    (below, low_row), (own, own_row), (above, high_row) = rows
    wide[...] = jnp.zeros(wide.shape, F32)
    for x in range(LX):
        size = halo * 8
        wide[NEAR + x, 0:halo] = below[x, pl.ds(low_row + reach * 8 - size, size), :].reshape(halo, 8, NZ)
        wide[NEAR + x, halo:halo + LY] = own[x, pl.ds(own_row, BLOCK), :].reshape(LY, 8, NZ)
        wide[NEAR + x, halo + LY:] = above[x, pl.ds(high_row, size), :].reshape(halo, 8, NZ)
    fill_sides(wide, halo, sides)


def fill_flat(wide, below, own, above, outer, inner):
    wide[...] = jnp.zeros(wide.shape, F32)
    for x in range(LX):
        wide[NEAR + x, 0:FAR] = below[x, pl.ds(2 * HALF + BLOCK, LY), :]
        wide[NEAR + x, FAR:FAR + LY] = own[x, pl.ds(3 * BLOCK, LY), :]
        wide[NEAR + x, FAR + LY:] = above[x, pl.ds(2 * HALF + BLOCK, LY), :]
    for d, more, place in SIDE_SPANS:
        for i in range(LY + 2 * more):
            tile, row = SIDE_SIZE + (place + i) // 8, (place + i) % 8
            y = FAR - more + i
            wide[halo_plane(False, d), pl.ds(y, 1), :] = outer[tile, pl.ds(row, 1), :]
            wide[halo_plane(True, d), pl.ds(y, 1), :] = inner[tile, pl.ds(row, 1), :]


def fill_tables(coef, skip, table_re, table_im, diag_re, diag_im):
    value = coef[...]
    real = 6.0 - value
    imag = 0.5 * value
    scale = jnp.where(value > 0.0, 0.8 / (real * real + imag * imag), 0.0)
    diag_re[...] = real * scale
    diag_im[...] = imag * scale
    sign = jnp.where(lax.broadcasted_iota(jnp.int32, (8, NZ), 0) < 4, 1.0, -1.0)
    size_x, size_y = table_re.shape[:2]

    def body(x, carry):
        for y in range(size_y):
            spot = pl.ds(y + skip, 1)
            table_re[x, y] = jnp.broadcast_to(diag_re[x, spot, :], (8, NZ))
            table_im[x, y] = jnp.broadcast_to(diag_im[x, spot, :], (8, NZ)) * sign
        return carry

    lax.fori_loop(0, size_x, body, 0, unroll=True)


def depth_sum(value):
    lane = lax.broadcasted_iota(jnp.int32, value.shape, 1)
    above = jnp.where(lane == 0, 0.0, pltpu.roll(value, 1, 1))
    below = jnp.where(lane == NZ - 1, 0.0, pltpu.roll(value, NZ - 1, 1))
    return above + below


def smooth(block, coef, skip, table_re, table_im, first, second, store):
    size_x, size_y = block.shape[:2]

    def solve(value, x, y):
        return table_re[x, y] * value + table_im[x, y] * pltpu.roll(value, 4, 0)

    def planes(k, body):
        lax.fori_loop(k, size_x - k, functools.partial(body, k, size_y - k), 0, unroll=True)

    def start(low, high, x, carry):
        for y in range(low, high):
            first[x, y] = solve(block[x, y], x, y)
        return carry

    def around(ref, x, low, high):
        line = [ref[x, y] for y in range(low - 1, high + 1)]
        for y in range(low, high):
            mid = line[y - low + 1]
            total = ref[x - 1, y] + ref[x + 1, y] + line[y - low] + line[y - low + 2]
            yield y, mid, total + depth_sum(mid)

    planes(0, start)
    here, there = first, second
    for k in range(1, 4):
        def sweep(low, high, x, carry, here=here, there=there):
            for y, mid, total in around(here, x, low, high):
                there[x, y] = 0.2 * mid + solve(block[x, y] + total, x, y)
            return carry

        planes(k, sweep)
        here, there = there, here

    def image(x, carry):
        for y, mid, total in around(here, x, 4, size_y - 4):
            diag = 6.0 - coef[x, pl.ds(y + skip, 1), :]
            store(x - 4, y - 4, diag * mid - total)
        return carry

    lax.fori_loop(4, size_x - 4, image, 0, unroll=True)


def wide_shape(halo):
    return (LX + 2 * NEAR, LY + 2 * halo)


FLAT = pltpu.VMEM((*wide_shape(FAR), NZ), F32)


def smooth_scratch(halo):
    return [pltpu.VMEM((*wide_shape(halo), 8, NZ), F32)] * 5 + [FLAT] * 2


def first_kernel(own, below, above, outer, inner, w, coef, outward, inward, block, first, second,
                 table_re, table_im, diag_re, diag_im):
    fill_flat(coef, below, own, above, outer, inner)
    fill_tables(coef, 0, table_re, table_im, diag_re, diag_im)
    rows = [(below, 2 * HALF), (own, 2 * BLOCK), (above, 2 * HALF)]
    fill_block(block, FAR, rows, FAR, [(outer, inner, 0, 0, SIDE_SPANS)])

    def store(x, y, value):
        w[x, y] = value

    smooth(block, coef, 0, table_re, table_im, first, second, store)
    for d, more, place in NEAR_SPANS:
        count = LY + 2 * more
        outward[pl.ds(place, count)] = w[sent_plane(False, d), pl.ds(NEAR - more, count)]
        inward[pl.ds(place, count)] = w[sent_plane(True, d), pl.ds(NEAR - more, count)]


def first_image(*args):
    side = jax.ShapeDtypeStruct((NEAR_SIZE, 8, NZ), F32)
    return pl.pallas_call(
        first_kernel,
        out_shape=(jax.ShapeDtypeStruct((LX, LY + 2 * NEAR, 8, NZ), F32),
                   jax.ShapeDtypeStruct((*wide_shape(FAR), NZ), F32), side, side),
        in_specs=[VMEM] * 5,
        out_specs=(VMEM,) * 4,
        scratch_shapes=smooth_scratch(FAR),
        compiler_params=pltpu.CompilerParams(vmem_limit_bytes=16 << 20),
        cost_estimate=pl.CostEstimate(flops=12_000_000, bytes_accessed=18_000_000, transcendentals=0),
        name="first_image",
    )(*args)


def old_kernel(coef, own, below, above, outer, first_outer, inner, out, block, first, second,
               table_re, table_im, diag_re, diag_im):
    fill_tables(coef, FAR - NEAR, table_re, table_im, diag_re, diag_im)
    for group in range(2):
        rows = [(below, group * HALF), (own, group * BLOCK), (above, group * HALF)]
        if group == 0:
            last = SIDE_SIZE + FLAT_TILES - SPLIT
            sides = [(outer, inner, 0, FIRST_TILES, NEAR_SPANS[:-1]),
                     (first_outer, inner, last, last, NEAR_SPANS[-1:])]
        else:
            sides = [(outer, inner, SPLIT, FIRST_TILES + SPLIT, NEAR_SPANS)]
        fill_block(block, NEAR, rows, NEAR, sides)

        def store(x, y, value, group=group):
            out[x, pl.ds(group * BLOCK + y * 8, 8), :] = value

        smooth(block, coef, FAR - NEAR, table_re, table_im, first, second, store)


def old_images(*args):
    return pl.pallas_call(
        old_kernel,
        out_shape=jax.ShapeDtypeStruct((LX, 2 * BLOCK, NZ), F32),
        in_specs=[VMEM] * 7,
        out_specs=VMEM,
        scratch_shapes=smooth_scratch(NEAR),
        compiler_params=pltpu.CompilerParams(vmem_limit_bytes=16 << 20),
        cost_estimate=pl.CostEstimate(flops=12_000_000, bytes_accessed=24_000_000, transcendentals=0),
        name="old_images",
    )(*args)


def split3(value):
    high = value.astype(BF16)
    rest = value - high.astype(F32)
    middle = rest.astype(BF16)
    low = (rest - middle.astype(F32)).astype(BF16)
    return high, middle, low


def basis_plane(start, w, old_image, w_image, x):
    refs = [(start, 0), (start, LY), (start, 2 * LY), (w, None), (old_image, 0), (old_image, LY), (w_image, 0)]
    rows = []
    for ref, first in refs:
        if first is None:
            tiles = [ref[x, NEAR + y] for y in range(LY)]
        else:
            tiles = [ref[x, pl.ds((first + y) * 8, 8), :] for y in range(LY)]
        rows.append(jnp.concatenate(tiles, axis=1))
    rows.append(jnp.zeros((8, LY * NZ), F32))
    return jnp.concatenate(rows, axis=0)


def lane_roll(value, amount):
    return pltpu.roll(value, amount % NZ, 1)


SLOTS = [(0, 0), (0, 56), (1, 0), (1, 40), (1, 72), (1, 96), (0, 104)]


def pack_gram(gram):
    lane = lax.broadcasted_iota(jnp.int32, (8, NZ), 1)
    row = lax.broadcasted_iota(jnp.int32, (8, NZ), 0)
    packed = jnp.zeros((8, NZ), F32)
    for b in range(BLOCKS):
        rows = gram[8 * b:8 * b + 8]
        turned = jnp.where(lane % 8 < 4, lane_roll(rows, -4), -lane_roll(rows, 4))
        both = rows + pltpu.roll(turned, 4, 0)
        half, start = SLOTS[b]
        moved = lane_roll(both, start - 8 * b)
        if half:
            moved = pltpu.roll(moved, 4, 0)
        keep = (lane >= start) & (lane < start + 8 * (BLOCKS - b)) & (row // 4 == half)
        packed = packed + jnp.where(keep, moved, 0.0)
    return packed


def unpack_gram(packed):
    lane = lax.broadcasted_iota(jnp.int32, (8, NZ), 1)
    row = lax.broadcasted_iota(jnp.int32, (8, NZ), 0)
    rows = []
    for b in range(BLOCKS):
        half, start = SLOTS[b]
        moved = lane_roll(packed, 8 * b - start)
        if half:
            moved = pltpu.roll(moved, 4, 0)
        keep = (lane >= 8 * b) & (lane < 8 * BLOCKS) & (row < 4)
        moved = jnp.where(keep, moved, 0.0)
        turned = jnp.where(lane % 8 < 4, -lane_roll(moved, -4), lane_roll(moved, 4))
        rows.append(moved + pltpu.roll(turned, 4, 0))
    rows.append(jnp.zeros((NZ - 8 * BLOCKS, NZ), F32))
    upper = jnp.concatenate(rows, axis=0)
    tall = lax.broadcasted_iota(jnp.int32, (NZ, NZ), 0)
    wide = lax.broadcasted_iota(jnp.int32, (NZ, NZ), 1)
    return jnp.where(tall // 8 <= wide // 8, upper, upper.T)


def gram_kernel(peers, w, coef, outer, inner, start, old_image, w_image, out,
                block, first, second, table_re, table_im, diag_re, diag_im):
    fill_tables(coef, FAR - NEAR, table_re, table_im, diag_re, diag_im)
    block[...] = jnp.zeros(block.shape, F32)
    for x in range(LX):
        block[NEAR + x] = w[x]
    fill_sides(block, NEAR, [(outer, inner, 0, 0, NEAR_SPANS)])

    def store(x, y, value):
        w_image[x, pl.ds(y * 8, 8), :] = value

    smooth(block, coef, FAR - NEAR, table_re, table_im, first, second, store)

    def plane(x, total):
        stacked = jnp.concatenate(split3(basis_plane(start, w, old_image, w_image, x)), axis=0)
        return total + lax.dot_general(stacked, stacked, (((1,), (1,)), ((), ())), preferred_element_type=F32)

    total = lax.fori_loop(0, LX, plane, jnp.zeros((3 * ROWS, 3 * ROWS), F32), unroll=True)
    tall = total[0:ROWS] + total[ROWS:2 * ROWS] + total[2 * ROWS:3 * ROWS]
    gram = tall[:, 0:ROWS] + tall[:, ROWS:2 * ROWS] + tall[:, 2 * ROWS:3 * ROWS]
    gram = jnp.concatenate([gram, jnp.zeros((ROWS, NZ - ROWS), F32)], axis=1)
    packed = pack_gram(gram)
    for peer in range(peers):
        out[peer] = packed


def image_and_gram(peers, *args):
    return pl.pallas_call(
        functools.partial(gram_kernel, peers),
        out_shape=(jax.ShapeDtypeStruct((LX, LY * 8, NZ), F32),
                   jax.ShapeDtypeStruct((peers, 8, NZ), F32)),
        in_specs=[VMEM] * 6,
        out_specs=(VMEM, VMEM),
        scratch_shapes=smooth_scratch(NEAR),
        compiler_params=pltpu.CompilerParams(vmem_limit_bytes=32 << 20),
        name="image_and_gram",
    )(*args)


def sum_kernel(parts, out):
    total = jnp.sum(parts[...], axis=0)
    for peer in range(out.shape[0]):
        out[peer] = total


def sum_and_spread(parts, peers):
    return pl.pallas_call(
        sum_kernel,
        out_shape=jax.ShapeDtypeStruct((peers, 8, NZ), F32),
        in_specs=[VMEM],
        out_specs=VMEM,
        compiler_params=pltpu.CompilerParams(vmem_limit_bytes=1 << 20),
        name="sum_and_spread",
    )(parts)


def exact(left, right, dims):
    parts = [part.astype(F32) for part in split3(left)]
    stacked = jnp.concatenate([*parts, jnp.zeros((8, NZ), F32)], axis=0).astype(BF16)
    high, middle, low = (
        lax.dot_general(stacked, part, (dims, ((), ())), preferred_element_type=F32) for part in split3(right)
    )
    small = low[0:8] + middle[8:16] + high[16:24]
    return small + (middle[0:8] + high[8:16]) + high[0:8]


def mul(left, right):
    return exact(left, right, ((1,), (0,)))


def mul_t(left, right):
    return exact(left, right, ((1,), (1,)))


def inverse_factor(gram):
    lane = lax.broadcasted_iota(jnp.int32, (8, NZ), 1)
    row = lax.broadcasted_iota(jnp.int32, (8, NZ), 0)
    work = jnp.where(lane < 8, gram, jnp.where(lane == row + 8, 1.0, 0.0))
    pivots = jnp.ones((8, NZ), F32)
    for s in range(4):
        pivot = jnp.broadcast_to(work[s:s + 1, s:s + 1], (8, NZ))
        pivots = jnp.where(row % 4 == s, pivot, pivots)
        if s < 3:
            change = work[:, s:s + 1] * work[s:s + 1, :] + work[:, 4 + s:5 + s] * work[4 + s:5 + s, :]
            work = jnp.where(row % 4 > s, work - change / pivot, work)
    return jnp.where(lane < 8, lane_roll(work, -8), 0.0) / jnp.sqrt(pivots)


def at_row(rows, start):
    parts = [rows, jnp.zeros((NZ - 8 - start, NZ), F32)]
    if start:
        parts.insert(0, jnp.zeros((start, NZ), F32))
    return jnp.concatenate(parts, axis=0)


def coefficients(gram):
    lane = lax.broadcasted_iota(jnp.int32, (8, NZ), 1)
    row = lax.broadcasted_iota(jnp.int32, (8, NZ), 0)
    new_at = 8 * BLOCKS

    once = jnp.where(lane < 24, gram[24:32], 0.0)
    again = jnp.where(lane < 24, mul(once, gram), 0.0)
    rows = jnp.where(lane == row + 24, 1.0, 0.0) - (2.0 * once - again)
    rows_gram = mul(rows, gram)
    spread = at_row(rows, 0)
    factor = inverse_factor(mul_t(rows_gram, spread))
    new = mul(factor, spread)
    new_gram = mul(factor, at_row(rows_gram, 0))
    new_rows = at_row(new, new_at)
    border = at_row(new_gram + mul_t(new_gram, new_rows), new_at)
    body = jnp.concatenate([gram[0:new_at], new_gram, gram[new_at + 8:]], axis=0)
    image = (jnp.where((lane >= 32) & (lane < 48), lane_roll(new, 32), 0.0)
             + jnp.where((lane >= 24) & (lane < 32), lane_roll(new, 8), 0.0)
             + jnp.where((lane >= 48) & (lane < 56), lane_roll(new, 24), 0.0))
    inside = ((lane >= 8) & (lane < 24)) | ((lane >= new_at) & (lane < new_at + 8))

    def times_gram(value):
        return mul(value, body) + mul_t(value, border)

    once = jnp.where(inside, times_gram(image), 0.0)
    again = jnp.where(inside, times_gram(once), 0.0)
    rows = image - (2.0 * once - again)
    spread = at_row(rows, 0)
    newest = mul(inverse_factor(mul_t(times_gram(rows), spread)), spread)
    on_new = jnp.where((lane >= new_at) & (lane < new_at + 8), newest, 0.0)
    return new, newest - on_new + mul(on_new, new_rows)


def final_kernel(cells, parts, start, w, old_image, w_image, out):
    gram = unpack_gram(jnp.sum(parts[...], axis=0) * (1.0 / cells))
    new, newest = coefficients(gram)
    mapping = jnp.concatenate([new, newest], axis=0)[:, 0:ROWS]
    pieces = [jnp.concatenate([piece] * 3, axis=1) for piece in split3(mapping)]
    stacked_map = jnp.concatenate(pieces, axis=0)

    def plane(x, carry):
        stacked = jnp.concatenate(split3(basis_plane(start, w, old_image, w_image, x)), axis=0)
        full = lax.dot_general(stacked_map, stacked, (((1,), (0,)), ((), ())), preferred_element_type=F32)
        result = full[32:48] + full[16:32] + full[0:16]
        for k in range(2):
            tiles = jnp.stack([result[8 * k:8 * k + 8, y * NZ:(y + 1) * NZ] for y in range(LY)])
            out[k, :, x] = jnp.swapaxes(tiles, 0, 1)
        return carry

    lax.fori_loop(0, LX, plane, 0, unroll=True)


def finish(cells, *args):
    return pl.pallas_call(
        functools.partial(final_kernel, cells),
        out_shape=jax.ShapeDtypeStruct((2, 8, LX, LY, NZ), F32),
        in_specs=[VMEM] * 5,
        out_specs=VMEM,
        compiler_params=pltpu.CompilerParams(vmem_limit_bytes=32 << 20),
        name="finish",
    )(*args)


GX = ("z", "core")


def from_both(axis, count, to_higher, to_lower):
    return (
        lax.ppermute(to_higher, axis, [(i, i + 1) for i in range(count - 1)]),
        lax.ppermute(to_lower, axis, [(i + 1, i) for i in range(count - 1)]),
    )


def swap_chips(count, value):
    return lax.ppermute(value, GX, [(i, i + 1 if i % 2 else i - 1) for i in range(1, count - 1)])


def swap_cores(count, value):
    return lax.ppermute(value, GX, [(i, i ^ 1) for i in range(count)])


def per_device(nx, ny, nz, prior, coefficient):
    cells = coefficient.size * nx * ny
    by_cell = prior.transpose(3, 0, 4, 1, 2, 5).reshape(LX, 3 * LY * 8, NZ)
    start = jnp.concatenate([by_cell, coefficient], axis=1)
    up = jnp.concatenate([start[:, HALF:BLOCK], start[:, BLOCK + HALF:]], axis=1)
    down = jnp.concatenate([start[:, :HALF], start[:, BLOCK:BLOCK + HALF], start[:, 2 * BLOCK:]], axis=1)
    rims = from_both("gy", ny, up, down)
    outward, inward, old_outward = pack_all(start, *rims)
    outer = swap_chips(nx, outward)
    inner = swap_cores(nx, inward)
    old_outer = swap_chips(nx, old_outward)
    w, coef, w_outward, w_inward = first_image(start, *rims, outer, inner)
    w_sides = swap_chips(nx, w_outward), swap_cores(nx, w_inward)
    old_image = old_images(coef, start, *rims, old_outer, outer, inner)

    w_image, spread = image_and_gram(2 * ny, w, coef, *w_sides, start, old_image)
    got = lax.all_to_all(spread, ("core", "gy"), 0, 0)
    got = lax.all_to_all(sum_and_spread(got, nz), "z", 0, 0)
    out = finish(cells, got, start, w, old_image, w_image)
    return out.reshape(2, 2, 4, LX, LY, NZ)


def solution(mesh):
    nx, ny = mesh.shape["gx"], mesh.shape["gy"]
    fine = Mesh(np.asarray(mesh.devices).reshape(nx // 2, 2, ny), ("z", "core", "gy"))
    in_specs = (P(None, None, None, GX, "gy", None), P(GX, "gy", None))
    out_specs = P(None, None, None, GX, "gy", None)
    return jax.shard_map(
        functools.partial(per_device, nx, ny, nx // 2),
        mesh=fine, in_specs=in_specs, out_specs=out_specs, check_vma=False,
    )
```

```python
import functools

import jax
import jax.numpy as jnp
import numpy as np
from jax import lax
from jax.experimental import pallas as pl
from jax.experimental.pallas import tpu as pltpu
from jax.sharding import Mesh, PartitionSpec as P

LX, LY, NZ = 4, 8, 128
NEAR, FAR = 4, 8
BLOCKS = 7
ROWS = 64
F32 = jnp.float32
BF16 = jnp.bfloat16
VMEM = pl.BlockSpec(memory_space=pltpu.VMEM)


BLOCK = LY * 8
HALF = NEAR * 8


def spans(halo, begin, end):
    found, place = [], 0
    for d in range(begin + 1, end + 1):
        found.append((d, halo - d, place))
        place += LY + 2 * (halo - d)
    return found, place


NEAR_SPANS, NEAR_SIZE = spans(NEAR, 0, LX)
SIDE_SPANS, SIDE_SIZE = spans(FAR, 0, LX)
FLAT_TILES = -(-SIDE_SIZE // 8)
SPLIT = NEAR_SPANS[-1][2]
FIRST_TILES = SIDE_SIZE + FLAT_TILES + NEAR_SIZE - SPLIT
SECOND_TILES = SPLIT + NEAR_SIZE


def sent_plane(inner, d):
    core = lax.axis_index("core")
    far = core if inner else 1 - core
    return (1 - far) * (LX - d) + far * (d - 1)


def halo_plane(inner, d):
    core = lax.axis_index("core")
    far = core if inner else 1 - core
    return (1 - far) * (NEAR + LX - 1 + d) + far * (NEAR - d)


def pack_columns(out, start, found, inner, rows, reach):
    (below, low_row), (own, own_row), (above, high_row) = rows
    for d, more, place in found:
        x = sent_plane(inner, d)
        spot = start + place
        size = more * 8
        if more:
            out[pl.ds(spot, more)] = below[x, pl.ds(low_row + reach * 8 - size, size), :].reshape(more, 8, NZ)
            out[pl.ds(spot + more + LY, more)] = above[x, pl.ds(high_row, size), :].reshape(more, 8, NZ)
        out[pl.ds(spot + more, LY)] = own[x, pl.ds(own_row, BLOCK), :].reshape(LY, 8, NZ)


def pack_coefficient(out, start, found, inner, below, own, above):
    for d, more, place in found:
        x = sent_plane(inner, d)
        for y in range(-more, LY + more):
            if y < 0:
                ref, row = below, 2 * HALF + BLOCK + LY + y
            elif y < LY:
                ref, row = own, 3 * BLOCK + y
            else:
                ref, row = above, 2 * HALF + BLOCK + y - LY
            spot = place + more + y
            out[start + spot // 8, pl.ds(spot % 8, 1), :] = ref[x, pl.ds(row, 1), :]


def column_kernel(own, below, above, outward, inward, old_outward, old_inward):
    for first, second, inner in ((outward, old_outward, False), (inward, old_inward, True)):
        rows = [(below, 2 * HALF), (own, 2 * BLOCK), (above, 2 * HALF)]
        pack_columns(first, 0, SIDE_SPANS, inner, rows, FAR)
        if SIDE_SIZE % 8:
            first[SIDE_SIZE + FLAT_TILES - 1] = jnp.zeros((8, NZ), F32)
        pack_coefficient(first, SIDE_SIZE, SIDE_SPANS, inner, below, own, above)
        rows = [(below, 0), (own, 0), (above, 0)]
        pack_columns(second, 0, NEAR_SPANS[:-1], inner, rows, NEAR)
        pack_columns(first, SIDE_SIZE + FLAT_TILES - SPLIT, NEAR_SPANS[-1:], inner, rows, NEAR)
        rows = [(below, HALF), (own, BLOCK), (above, HALF)]
        pack_columns(second, SPLIT, NEAR_SPANS, inner, rows, NEAR)


def pack_all(*args):
    shapes = tuple(jax.ShapeDtypeStruct((size, 8, NZ), F32) for size in [FIRST_TILES] * 2 + [SECOND_TILES] * 2)
    return pl.pallas_call(
        column_kernel,
        out_shape=shapes,
        in_specs=[VMEM] * 3,
        out_specs=(VMEM,) * 4,
        compiler_params=pltpu.CompilerParams(vmem_limit_bytes=1 << 20),
        name="pack_all",
    )(*args)


def fill_sides(wide, halo, sides):
    for outer, inner, start, found in sides:
        for d, more, place in found:
            count = LY + 2 * more
            begin = halo - more
            wide[halo_plane(False, d), begin:begin + count] = outer[pl.ds(start + place, count)]
            wide[halo_plane(True, d), begin:begin + count] = inner[pl.ds(start + place, count)]


def fill_block(wide, halo, rows, reach, sides):
    (below, low_row), (own, own_row), (above, high_row) = rows
    wide[...] = jnp.zeros(wide.shape, F32)
    for x in range(LX):
        size = halo * 8
        wide[NEAR + x, 0:halo] = below[x, pl.ds(low_row + reach * 8 - size, size), :].reshape(halo, 8, NZ)
        wide[NEAR + x, halo:halo + LY] = own[x, pl.ds(own_row, BLOCK), :].reshape(LY, 8, NZ)
        wide[NEAR + x, halo + LY:] = above[x, pl.ds(high_row, size), :].reshape(halo, 8, NZ)
    fill_sides(wide, halo, sides)


def fill_flat(wide, below, own, above, outer, inner):
    wide[...] = jnp.zeros(wide.shape, F32)
    for x in range(LX):
        wide[NEAR + x, 0:FAR] = below[x, pl.ds(2 * HALF + BLOCK, LY), :]
        wide[NEAR + x, FAR:FAR + LY] = own[x, pl.ds(3 * BLOCK, LY), :]
        wide[NEAR + x, FAR + LY:] = above[x, pl.ds(2 * HALF + BLOCK, LY), :]
    for d, more, place in SIDE_SPANS:
        for i in range(LY + 2 * more):
            tile, row = SIDE_SIZE + (place + i) // 8, (place + i) % 8
            y = FAR - more + i
            wide[halo_plane(False, d), pl.ds(y, 1), :] = outer[tile, pl.ds(row, 1), :]
            wide[halo_plane(True, d), pl.ds(y, 1), :] = inner[tile, pl.ds(row, 1), :]


def fill_tables(coef, skip, table_re, table_im, diag_re, diag_im):
    value = coef[...]
    real = 6.0 - value
    imag = 0.5 * value
    scale = jnp.where(value > 0.0, 0.8 / (real * real + imag * imag), 0.0)
    diag_re[...] = real * scale
    diag_im[...] = imag * scale
    sign = jnp.where(lax.broadcasted_iota(jnp.int32, (8, NZ), 0) < 4, 1.0, -1.0)
    size_x, size_y = table_re.shape[:2]

    def body(x, carry):
        for y in range(size_y):
            spot = pl.ds(y + skip, 1)
            table_re[x, y] = jnp.broadcast_to(diag_re[x, spot, :], (8, NZ))
            table_im[x, y] = jnp.broadcast_to(diag_im[x, spot, :], (8, NZ)) * sign
        return carry

    lax.fori_loop(0, size_x, body, 0, unroll=True)


def depth_sum(value):
    lane = lax.broadcasted_iota(jnp.int32, value.shape, 1)
    above = jnp.where(lane == 0, 0.0, pltpu.roll(value, 1, 1))
    below = jnp.where(lane == NZ - 1, 0.0, pltpu.roll(value, NZ - 1, 1))
    return above + below


def smooth(block, coef, skip, table_re, table_im, first, second, store):
    size_x, size_y = block.shape[:2]

    def solve(value, x, y):
        return table_re[x, y] * value + table_im[x, y] * pltpu.roll(value, 4, 0)

    def planes(k, body):
        lax.fori_loop(k, size_x - k, functools.partial(body, k, size_y - k), 0, unroll=True)

    def start(low, high, x, carry):
        for y in range(low, high):
            first[x, y] = solve(block[x, y], x, y)
        return carry

    def around(ref, x, low, high):
        line = [ref[x, y] for y in range(low - 1, high + 1)]
        for y in range(low, high):
            mid = line[y - low + 1]
            total = ref[x - 1, y] + ref[x + 1, y] + line[y - low] + line[y - low + 2]
            yield y, mid, total + depth_sum(mid)

    planes(0, start)
    here, there = first, second
    for k in range(1, 4):
        def sweep(low, high, x, carry, here=here, there=there):
            for y, mid, total in around(here, x, low, high):
                there[x, y] = 0.2 * mid + solve(block[x, y] + total, x, y)
            return carry

        planes(k, sweep)
        here, there = there, here

    def image(x, carry):
        for y, mid, total in around(here, x, 4, size_y - 4):
            diag = 6.0 - coef[x, pl.ds(y + skip, 1), :]
            store(x - 4, y - 4, diag * mid - total)
        return carry

    lax.fori_loop(4, size_x - 4, image, 0, unroll=True)


def wide_shape(halo):
    return (LX + 2 * NEAR, LY + 2 * halo)


FLAT = pltpu.VMEM((*wide_shape(FAR), NZ), F32)


def smooth_scratch(halo):
    return [pltpu.VMEM((*wide_shape(halo), 8, NZ), F32)] * 5 + [FLAT] * 2


def first_kernel(own, below, above, outer, inner, w, coef, outward, inward, block, first, second,
                 table_re, table_im, diag_re, diag_im):
    fill_flat(coef, below, own, above, outer, inner)
    fill_tables(coef, 0, table_re, table_im, diag_re, diag_im)
    rows = [(below, 2 * HALF), (own, 2 * BLOCK), (above, 2 * HALF)]
    fill_block(block, FAR, rows, FAR, [(outer, inner, 0, SIDE_SPANS)])

    def store(x, y, value):
        w[x, y] = value

    smooth(block, coef, 0, table_re, table_im, first, second, store)
    for d, more, place in NEAR_SPANS:
        count = LY + 2 * more
        outward[pl.ds(place, count)] = w[sent_plane(False, d), pl.ds(NEAR - more, count)]
        inward[pl.ds(place, count)] = w[sent_plane(True, d), pl.ds(NEAR - more, count)]


def first_image(*args):
    side = jax.ShapeDtypeStruct((NEAR_SIZE, 8, NZ), F32)
    return pl.pallas_call(
        first_kernel,
        out_shape=(jax.ShapeDtypeStruct((LX, LY + 2 * NEAR, 8, NZ), F32),
                   jax.ShapeDtypeStruct((*wide_shape(FAR), NZ), F32), side, side),
        in_specs=[VMEM] * 5,
        out_specs=(VMEM,) * 4,
        scratch_shapes=smooth_scratch(FAR),
        compiler_params=pltpu.CompilerParams(vmem_limit_bytes=16 << 20),
        cost_estimate=pl.CostEstimate(flops=12_000_000, bytes_accessed=18_000_000, transcendentals=0),
        name="first_image",
    )(*args)


def old_kernel(coef, own, below, above, outer, inner, first_outer, first_inner, out, block, first, second,
               table_re, table_im, diag_re, diag_im):
    fill_tables(coef, FAR - NEAR, table_re, table_im, diag_re, diag_im)
    for group in range(2):
        rows = [(below, group * HALF), (own, group * BLOCK), (above, group * HALF)]
        if group == 0:
            sides = [(outer, inner, 0, NEAR_SPANS[:-1]),
                     (first_outer, first_inner, SIDE_SIZE + FLAT_TILES - SPLIT, NEAR_SPANS[-1:])]
        else:
            sides = [(outer, inner, SPLIT, NEAR_SPANS)]
        fill_block(block, NEAR, rows, NEAR, sides)

        def store(x, y, value, group=group):
            out[x, pl.ds(group * BLOCK + y * 8, 8), :] = value

        smooth(block, coef, FAR - NEAR, table_re, table_im, first, second, store)


def old_images(*args):
    return pl.pallas_call(
        old_kernel,
        out_shape=jax.ShapeDtypeStruct((LX, 2 * BLOCK, NZ), F32),
        in_specs=[VMEM] * 8,
        out_specs=VMEM,
        scratch_shapes=smooth_scratch(NEAR),
        compiler_params=pltpu.CompilerParams(vmem_limit_bytes=16 << 20),
        cost_estimate=pl.CostEstimate(flops=12_000_000, bytes_accessed=24_000_000, transcendentals=0),
        name="old_images",
    )(*args)


def split3(value):
    high = value.astype(BF16)
    rest = value - high.astype(F32)
    middle = rest.astype(BF16)
    low = (rest - middle.astype(F32)).astype(BF16)
    return high, middle, low


def basis_plane(start, w, old_image, w_image, x):
    refs = [(start, 0), (start, LY), (start, 2 * LY), (w, None), (old_image, 0), (old_image, LY), (w_image, 0)]
    rows = []
    for ref, first in refs:
        if first is None:
            tiles = [ref[x, NEAR + y] for y in range(LY)]
        else:
            tiles = [ref[x, pl.ds((first + y) * 8, 8), :] for y in range(LY)]
        rows.append(jnp.concatenate(tiles, axis=1))
    rows.append(jnp.zeros((8, LY * NZ), F32))
    return jnp.concatenate(rows, axis=0)


def lane_roll(value, amount):
    return pltpu.roll(value, amount % NZ, 1)


SLOTS = [(0, 0), (0, 56), (1, 0), (1, 40), (1, 72), (1, 96), (0, 104)]


def pack_gram(gram):
    lane = lax.broadcasted_iota(jnp.int32, (8, NZ), 1)
    row = lax.broadcasted_iota(jnp.int32, (8, NZ), 0)
    packed = jnp.zeros((8, NZ), F32)
    for b in range(BLOCKS):
        rows = gram[8 * b:8 * b + 8]
        turned = jnp.where(lane % 8 < 4, lane_roll(rows, -4), -lane_roll(rows, 4))
        both = rows + pltpu.roll(turned, 4, 0)
        half, start = SLOTS[b]
        moved = lane_roll(both, start - 8 * b)
        if half:
            moved = pltpu.roll(moved, 4, 0)
        keep = (lane >= start) & (lane < start + 8 * (BLOCKS - b)) & (row // 4 == half)
        packed = packed + jnp.where(keep, moved, 0.0)
    return packed


def unpack_gram(packed):
    lane = lax.broadcasted_iota(jnp.int32, (8, NZ), 1)
    row = lax.broadcasted_iota(jnp.int32, (8, NZ), 0)
    rows = []
    for b in range(BLOCKS):
        half, start = SLOTS[b]
        moved = lane_roll(packed, 8 * b - start)
        if half:
            moved = pltpu.roll(moved, 4, 0)
        keep = (lane >= 8 * b) & (lane < 8 * BLOCKS) & (row < 4)
        moved = jnp.where(keep, moved, 0.0)
        turned = jnp.where(lane % 8 < 4, -lane_roll(moved, -4), lane_roll(moved, 4))
        rows.append(moved + pltpu.roll(turned, 4, 0))
    rows.append(jnp.zeros((NZ - 8 * BLOCKS, NZ), F32))
    upper = jnp.concatenate(rows, axis=0)
    tall = lax.broadcasted_iota(jnp.int32, (NZ, NZ), 0)
    wide = lax.broadcasted_iota(jnp.int32, (NZ, NZ), 1)
    return jnp.where(tall // 8 <= wide // 8, upper, upper.T)


def gram_kernel(peers, w, coef, outer, inner, start, old_image, w_image, out,
                block, first, second, table_re, table_im, diag_re, diag_im):
    fill_tables(coef, FAR - NEAR, table_re, table_im, diag_re, diag_im)
    block[...] = jnp.zeros(block.shape, F32)
    for x in range(LX):
        block[NEAR + x] = w[x]
    fill_sides(block, NEAR, [(outer, inner, 0, NEAR_SPANS)])

    def store(x, y, value):
        w_image[x, pl.ds(y * 8, 8), :] = value

    smooth(block, coef, FAR - NEAR, table_re, table_im, first, second, store)

    def plane(x, total):
        stacked = jnp.concatenate(split3(basis_plane(start, w, old_image, w_image, x)), axis=0)
        return total + lax.dot_general(stacked, stacked, (((1,), (1,)), ((), ())), preferred_element_type=F32)

    total = lax.fori_loop(0, LX, plane, jnp.zeros((3 * ROWS, 3 * ROWS), F32), unroll=True)
    tall = total[0:ROWS] + total[ROWS:2 * ROWS] + total[2 * ROWS:3 * ROWS]
    gram = tall[:, 0:ROWS] + tall[:, ROWS:2 * ROWS] + tall[:, 2 * ROWS:3 * ROWS]
    gram = jnp.concatenate([gram, jnp.zeros((ROWS, NZ - ROWS), F32)], axis=1)
    packed = pack_gram(gram)
    for peer in range(peers):
        out[peer] = packed


def image_and_gram(peers, *args):
    return pl.pallas_call(
        functools.partial(gram_kernel, peers),
        out_shape=(jax.ShapeDtypeStruct((LX, LY * 8, NZ), F32),
                   jax.ShapeDtypeStruct((peers, 8, NZ), F32)),
        in_specs=[VMEM] * 6,
        out_specs=(VMEM, VMEM),
        scratch_shapes=smooth_scratch(NEAR),
        compiler_params=pltpu.CompilerParams(vmem_limit_bytes=32 << 20),
        name="image_and_gram",
    )(*args)


def sum_kernel(parts, out):
    total = jnp.sum(parts[...], axis=0)
    for peer in range(out.shape[0]):
        out[peer] = total


def sum_and_spread(parts, peers):
    return pl.pallas_call(
        sum_kernel,
        out_shape=jax.ShapeDtypeStruct((peers, 8, NZ), F32),
        in_specs=[VMEM],
        out_specs=VMEM,
        compiler_params=pltpu.CompilerParams(vmem_limit_bytes=1 << 20),
        name="sum_and_spread",
    )(parts)


def exact(left, right, dims):
    parts = [part.astype(F32) for part in split3(left)]
    stacked = jnp.concatenate([*parts, jnp.zeros((8, NZ), F32)], axis=0).astype(BF16)
    high, middle, low = (
        lax.dot_general(stacked, part, (dims, ((), ())), preferred_element_type=F32) for part in split3(right)
    )
    small = low[0:8] + middle[8:16] + high[16:24]
    return small + (middle[0:8] + high[8:16]) + high[0:8]


def mul(left, right):
    return exact(left, right, ((1,), (0,)))


def mul_t(left, right):
    return exact(left, right, ((1,), (1,)))


def inverse_factor(gram):
    lane = lax.broadcasted_iota(jnp.int32, (8, NZ), 1)
    row = lax.broadcasted_iota(jnp.int32, (8, NZ), 0)
    work = jnp.where(lane < 8, gram, jnp.where(lane == row + 8, 1.0, 0.0))
    pivots = jnp.ones((8, NZ), F32)
    for s in range(4):
        pivot = jnp.broadcast_to(work[s:s + 1, s:s + 1], (8, NZ))
        pivots = jnp.where(row % 4 == s, pivot, pivots)
        if s < 3:
            change = work[:, s:s + 1] * work[s:s + 1, :] + work[:, 4 + s:5 + s] * work[4 + s:5 + s, :]
            work = jnp.where(row % 4 > s, work - change / pivot, work)
    return jnp.where(lane < 8, lane_roll(work, -8), 0.0) / jnp.sqrt(pivots)


def at_row(rows, start):
    parts = [rows, jnp.zeros((NZ - 8 - start, NZ), F32)]
    if start:
        parts.insert(0, jnp.zeros((start, NZ), F32))
    return jnp.concatenate(parts, axis=0)


def coefficients(gram):
    lane = lax.broadcasted_iota(jnp.int32, (8, NZ), 1)
    row = lax.broadcasted_iota(jnp.int32, (8, NZ), 0)
    new_at = 8 * BLOCKS

    once = jnp.where(lane < 24, gram[24:32], 0.0)
    again = jnp.where(lane < 24, mul(once, gram), 0.0)
    rows = jnp.where(lane == row + 24, 1.0, 0.0) - (2.0 * once - again)
    rows_gram = mul(rows, gram)
    spread = at_row(rows, 0)
    factor = inverse_factor(mul_t(rows_gram, spread))
    new = mul(factor, spread)
    new_gram = mul(factor, at_row(rows_gram, 0))
    new_rows = at_row(new, new_at)
    border = at_row(new_gram + mul_t(new_gram, new_rows), new_at)
    body = jnp.concatenate([gram[0:new_at], new_gram, gram[new_at + 8:]], axis=0)
    image = (jnp.where((lane >= 32) & (lane < 48), lane_roll(new, 32), 0.0)
             + jnp.where((lane >= 24) & (lane < 32), lane_roll(new, 8), 0.0)
             + jnp.where((lane >= 48) & (lane < 56), lane_roll(new, 24), 0.0))
    inside = ((lane >= 8) & (lane < 24)) | ((lane >= new_at) & (lane < new_at + 8))

    def times_gram(value):
        return mul(value, body) + mul_t(value, border)

    once = jnp.where(inside, times_gram(image), 0.0)
    again = jnp.where(inside, times_gram(once), 0.0)
    rows = image - (2.0 * once - again)
    spread = at_row(rows, 0)
    newest = mul(inverse_factor(mul_t(times_gram(rows), spread)), spread)
    on_new = jnp.where((lane >= new_at) & (lane < new_at + 8), newest, 0.0)
    return new, newest - on_new + mul(on_new, new_rows)


def final_kernel(cells, parts, start, w, old_image, w_image, out):
    gram = unpack_gram(jnp.sum(parts[...], axis=0) * (1.0 / cells))
    new, newest = coefficients(gram)
    mapping = jnp.concatenate([new, newest], axis=0)[:, 0:ROWS]
    pieces = [jnp.concatenate([piece] * 3, axis=1) for piece in split3(mapping)]
    stacked_map = jnp.concatenate(pieces, axis=0)

    def plane(x, carry):
        stacked = jnp.concatenate(split3(basis_plane(start, w, old_image, w_image, x)), axis=0)
        full = lax.dot_general(stacked_map, stacked, (((1,), (0,)), ((), ())), preferred_element_type=F32)
        result = full[32:48] + full[16:32] + full[0:16]
        for k in range(2):
            tiles = jnp.stack([result[8 * k:8 * k + 8, y * NZ:(y + 1) * NZ] for y in range(LY)])
            out[k, :, x] = jnp.swapaxes(tiles, 0, 1)
        return carry

    lax.fori_loop(0, LX, plane, 0, unroll=True)


def finish(cells, *args):
    return pl.pallas_call(
        functools.partial(final_kernel, cells),
        out_shape=jax.ShapeDtypeStruct((2, 8, LX, LY, NZ), F32),
        in_specs=[VMEM] * 5,
        out_specs=VMEM,
        compiler_params=pltpu.CompilerParams(vmem_limit_bytes=32 << 20),
        name="finish",
    )(*args)


GX = ("z", "core")


def turn_kernel(prior, coefficient, start, up, down):
    for x in range(LX):
        for k in range(3):
            block = jnp.swapaxes(prior[k, :, :, x].reshape(8, LY, NZ), 0, 1).reshape(BLOCK, NZ)
            start[x, pl.ds(k * BLOCK, BLOCK), :] = block
            if k < 2:
                up[x, pl.ds(k * HALF, HALF), :] = block[HALF:]
                down[x, pl.ds(k * HALF, HALF), :] = block[:HALF]
            else:
                up[x, pl.ds(2 * HALF, BLOCK), :] = block
                down[x, pl.ds(2 * HALF, BLOCK), :] = block
        value = coefficient[x]
        start[x, pl.ds(3 * BLOCK, LY), :] = value
        up[x, pl.ds(2 * HALF + BLOCK, LY), :] = value
        down[x, pl.ds(2 * HALF + BLOCK, LY), :] = value


def turn(prior, coefficient):
    message = jax.ShapeDtypeStruct((LX, 2 * HALF + BLOCK + LY, NZ), F32)
    return pl.pallas_call(
        turn_kernel,
        out_shape=(jax.ShapeDtypeStruct((LX, 3 * BLOCK + LY, NZ), F32), message, message),
        in_specs=[VMEM] * 2,
        out_specs=(VMEM,) * 3,
        compiler_params=pltpu.CompilerParams(vmem_limit_bytes=1 << 20),
        name="turn",
    )(prior, coefficient)


def from_both(axis, count, to_higher, to_lower):
    return (
        lax.ppermute(to_higher, axis, [(i, i + 1) for i in range(count - 1)]),
        lax.ppermute(to_lower, axis, [(i + 1, i) for i in range(count - 1)]),
    )


def exchange(count, outward, inward):
    inner = [(i, i ^ 1) for i in range(count)]
    outer = [(i, i + 1 if i % 2 else i - 1) for i in range(1, count - 1)]
    return lax.ppermute(outward, GX, outer), lax.ppermute(inward, GX, inner)


def per_device(nx, ny, nz, prior, coefficient):
    cells = coefficient.size * nx * ny
    start, up, down = turn(prior, coefficient)
    rims = from_both("gy", ny, up, down)
    outward, inward, old_outward, old_inward = pack_all(start, *rims)
    sides = exchange(nx, outward, inward)
    old_sides = exchange(nx, old_outward, old_inward)
    w, coef, w_outward, w_inward = first_image(start, *rims, *sides)
    w_sides = exchange(nx, w_outward, w_inward)
    old_image = old_images(coef, start, *rims, *old_sides, *sides)

    w_image, spread = image_and_gram(2 * ny, w, coef, *w_sides, start, old_image)
    got = lax.all_to_all(spread, ("core", "gy"), 0, 0)
    got = lax.all_to_all(sum_and_spread(got, nz), "z", 0, 0)
    out = finish(cells, got, start, w, old_image, w_image)
    return out.reshape(2, 2, 4, LX, LY, NZ)


def solution(mesh):
    nx, ny = mesh.shape["gx"], mesh.shape["gy"]
    fine = Mesh(np.asarray(mesh.devices).reshape(nx // 2, 2, ny), ("z", "core", "gy"))
    in_specs = (P(None, None, None, GX, "gy", None), P(GX, "gy", None))
    out_specs = P(None, None, None, GX, "gy", None)
    return jax.shard_map(
        functools.partial(per_device, nx, ny, nx // 2),
        mesh=fine, in_specs=in_specs, out_specs=out_specs, check_vma=False,
    )
```

```python
import functools

import jax
import jax.numpy as jnp
import numpy as np
from jax import lax
from jax.experimental import pallas as pl
from jax.experimental.pallas import tpu as pltpu
from jax.sharding import Mesh, PartitionSpec as P

LX, LY, NZ = 4, 8, 128
NEAR, FAR = 4, 8
BLOCKS = 7
ROWS = 64
F32 = jnp.float32
BF16 = jnp.bfloat16
VMEM = pl.BlockSpec(memory_space=pltpu.VMEM)


BLOCK = LY * 8
HALF = NEAR * 8


def spans(halo, begin, end):
    found, place = [], 0
    for d in range(begin + 1, end + 1):
        found.append((d, halo - d, place))
        place += LY + 2 * (halo - d)
    return found, place


NEAR_SPANS, NEAR_SIZE = spans(NEAR, 0, LX)
SIDE_SPANS, SIDE_SIZE = spans(FAR, 0, LX)
FLAT_TILES = -(-SIDE_SIZE // 8)
SPLIT = NEAR_SPANS[-1][2]
FIRST_TILES = SIDE_SIZE + FLAT_TILES + NEAR_SIZE - SPLIT
SECOND_TILES = SPLIT + NEAR_SIZE


def sent_plane(inner, d):
    core = lax.axis_index("core")
    far = core if inner else 1 - core
    return (1 - far) * (LX - d) + far * (d - 1)


def halo_plane(inner, d):
    core = lax.axis_index("core")
    far = core if inner else 1 - core
    return (1 - far) * (NEAR + LX - 1 + d) + far * (NEAR - d)


def pack_columns(out, start, found, inner, rows, reach):
    (below, low_row), (own, own_row), (above, high_row) = rows
    for d, more, place in found:
        x = sent_plane(inner, d)
        spot = start + place
        size = more * 8
        if more:
            out[pl.ds(spot, more)] = below[x, pl.ds(low_row + reach * 8 - size, size), :].reshape(more, 8, NZ)
            out[pl.ds(spot + more + LY, more)] = above[x, pl.ds(high_row, size), :].reshape(more, 8, NZ)
        out[pl.ds(spot + more, LY)] = own[x, pl.ds(own_row, BLOCK), :].reshape(LY, 8, NZ)


def pack_coefficient(out, start, found, inner, below, own, above):
    for d, more, place in found:
        x = sent_plane(inner, d)
        for y in range(-more, LY + more):
            if y < 0:
                ref, row = below, 2 * HALF + BLOCK + LY + y
            elif y < LY:
                ref, row = own, 3 * BLOCK + y
            else:
                ref, row = above, 2 * HALF + BLOCK + y - LY
            spot = place + more + y
            out[start + spot // 8, pl.ds(spot % 8, 1), :] = ref[x, pl.ds(row, 1), :]


def column_kernel(own, below, above, outward, inward, old_outward, old_inward):
    for first, second, inner in ((outward, old_outward, False), (inward, old_inward, True)):
        rows = [(below, 2 * HALF), (own, 2 * BLOCK), (above, 2 * HALF)]
        pack_columns(first, 0, SIDE_SPANS, inner, rows, FAR)
        if SIDE_SIZE % 8:
            first[SIDE_SIZE + FLAT_TILES - 1] = jnp.zeros((8, NZ), F32)
        pack_coefficient(first, SIDE_SIZE, SIDE_SPANS, inner, below, own, above)
        rows = [(below, 0), (own, 0), (above, 0)]
        pack_columns(second, 0, NEAR_SPANS[:-1], inner, rows, NEAR)
        pack_columns(first, SIDE_SIZE + FLAT_TILES - SPLIT, NEAR_SPANS[-1:], inner, rows, NEAR)
        rows = [(below, HALF), (own, BLOCK), (above, HALF)]
        pack_columns(second, SPLIT, NEAR_SPANS, inner, rows, NEAR)


def pack_all(*args):
    shapes = tuple(jax.ShapeDtypeStruct((size, 8, NZ), F32) for size in [FIRST_TILES] * 2 + [SECOND_TILES] * 2)
    return pl.pallas_call(
        column_kernel,
        out_shape=shapes,
        in_specs=[VMEM] * 3,
        out_specs=(VMEM,) * 4,
        compiler_params=pltpu.CompilerParams(vmem_limit_bytes=1 << 20),
        name="pack_all",
    )(*args)


def fill_sides(wide, halo, sides):
    for outer, inner, start, found in sides:
        for d, more, place in found:
            count = LY + 2 * more
            begin = halo - more
            wide[halo_plane(False, d), begin:begin + count] = outer[pl.ds(start + place, count)]
            wide[halo_plane(True, d), begin:begin + count] = inner[pl.ds(start + place, count)]


def fill_block(wide, halo, rows, reach, sides):
    (below, low_row), (own, own_row), (above, high_row) = rows
    wide[...] = jnp.zeros(wide.shape, F32)
    for x in range(LX):
        size = halo * 8
        wide[NEAR + x, 0:halo] = below[x, pl.ds(low_row + reach * 8 - size, size), :].reshape(halo, 8, NZ)
        wide[NEAR + x, halo:halo + LY] = own[x, pl.ds(own_row, BLOCK), :].reshape(LY, 8, NZ)
        wide[NEAR + x, halo + LY:] = above[x, pl.ds(high_row, size), :].reshape(halo, 8, NZ)
    fill_sides(wide, halo, sides)


def fill_flat(wide, below, own, above, outer, inner):
    wide[...] = jnp.zeros(wide.shape, F32)
    for x in range(LX):
        wide[NEAR + x, 0:FAR] = below[x, pl.ds(2 * HALF + BLOCK, LY), :]
        wide[NEAR + x, FAR:FAR + LY] = own[x, pl.ds(3 * BLOCK, LY), :]
        wide[NEAR + x, FAR + LY:] = above[x, pl.ds(2 * HALF + BLOCK, LY), :]
    for d, more, place in SIDE_SPANS:
        for i in range(LY + 2 * more):
            tile, row = SIDE_SIZE + (place + i) // 8, (place + i) % 8
            y = FAR - more + i
            wide[halo_plane(False, d), pl.ds(y, 1), :] = outer[tile, pl.ds(row, 1), :]
            wide[halo_plane(True, d), pl.ds(y, 1), :] = inner[tile, pl.ds(row, 1), :]


def fill_tables(coef, skip, table_re, table_im, diag_re, diag_im):
    value = coef[...]
    real = 6.0 - value
    imag = 0.5 * value
    scale = jnp.where(value > 0.0, 0.8 / (real * real + imag * imag), 0.0)
    diag_re[...] = real * scale
    diag_im[...] = imag * scale
    sign = jnp.where(lax.broadcasted_iota(jnp.int32, (8, NZ), 0) < 4, 1.0, -1.0)
    size_x, size_y = table_re.shape[:2]

    def body(x, carry):
        for y in range(size_y):
            spot = pl.ds(y + skip, 1)
            table_re[x, y] = jnp.broadcast_to(diag_re[x, spot, :], (8, NZ))
            table_im[x, y] = jnp.broadcast_to(diag_im[x, spot, :], (8, NZ)) * sign
        return carry

    lax.fori_loop(0, size_x, body, 0, unroll=True)


def depth_sum(value):
    lane = lax.broadcasted_iota(jnp.int32, value.shape, 1)
    above = jnp.where(lane == 0, 0.0, pltpu.roll(value, 1, 1))
    below = jnp.where(lane == NZ - 1, 0.0, pltpu.roll(value, NZ - 1, 1))
    return above + below


def smooth(block, coef, skip, table_re, table_im, first, second, store):
    size_x, size_y = block.shape[:2]

    def solve(value, x, y):
        return table_re[x, y] * value + table_im[x, y] * pltpu.roll(value, 4, 0)

    def planes(k, body):
        lax.fori_loop(k, size_x - k, functools.partial(body, k, size_y - k), 0, unroll=True)

    def start(low, high, x, carry):
        for y in range(low, high):
            first[x, y] = solve(block[x, y], x, y)
        return carry

    def around(ref, x, low, high):
        line = [ref[x, y] for y in range(low - 1, high + 1)]
        for y in range(low, high):
            mid = line[y - low + 1]
            total = ref[x - 1, y] + ref[x + 1, y] + line[y - low] + line[y - low + 2]
            yield y, mid, total + depth_sum(mid)

    planes(0, start)
    here, there = first, second
    for k in range(1, 4):
        def sweep(low, high, x, carry, here=here, there=there):
            for y, mid, total in around(here, x, low, high):
                there[x, y] = 0.2 * mid + solve(block[x, y] + total, x, y)
            return carry

        planes(k, sweep)
        here, there = there, here

    def image(x, carry):
        for y, mid, total in around(here, x, 4, size_y - 4):
            diag = 6.0 - coef[x, pl.ds(y + skip, 1), :]
            store(x - 4, y - 4, diag * mid - total)
        return carry

    lax.fori_loop(4, size_x - 4, image, 0, unroll=True)


def wide_shape(halo):
    return (LX + 2 * NEAR, LY + 2 * halo)


FLAT = pltpu.VMEM((*wide_shape(FAR), NZ), F32)


def smooth_scratch(halo):
    return [pltpu.VMEM((*wide_shape(halo), 8, NZ), F32)] * 5 + [FLAT] * 2


def first_kernel(own, below, above, outer, inner, w, coef, outward, inward, block, first, second,
                 table_re, table_im, diag_re, diag_im):
    fill_flat(coef, below, own, above, outer, inner)
    fill_tables(coef, 0, table_re, table_im, diag_re, diag_im)
    rows = [(below, 2 * HALF), (own, 2 * BLOCK), (above, 2 * HALF)]
    fill_block(block, FAR, rows, FAR, [(outer, inner, 0, SIDE_SPANS)])

    def store(x, y, value):
        w[x, y] = value

    smooth(block, coef, 0, table_re, table_im, first, second, store)
    for d, more, place in NEAR_SPANS:
        count = LY + 2 * more
        outward[pl.ds(place, count)] = w[sent_plane(False, d), pl.ds(NEAR - more, count)]
        inward[pl.ds(place, count)] = w[sent_plane(True, d), pl.ds(NEAR - more, count)]


def first_image(*args):
    side = jax.ShapeDtypeStruct((NEAR_SIZE, 8, NZ), F32)
    return pl.pallas_call(
        first_kernel,
        out_shape=(jax.ShapeDtypeStruct((LX, LY + 2 * NEAR, 8, NZ), F32),
                   jax.ShapeDtypeStruct((*wide_shape(FAR), NZ), F32), side, side),
        in_specs=[VMEM] * 5,
        out_specs=(VMEM,) * 4,
        scratch_shapes=smooth_scratch(FAR),
        compiler_params=pltpu.CompilerParams(vmem_limit_bytes=16 << 20),
        cost_estimate=pl.CostEstimate(flops=12_000_000, bytes_accessed=18_000_000, transcendentals=0),
        name="first_image",
    )(*args)


def old_kernel(coef, own, below, above, outer, inner, first_outer, first_inner, out, block, first, second,
               table_re, table_im, diag_re, diag_im):
    fill_tables(coef, FAR - NEAR, table_re, table_im, diag_re, diag_im)
    for group in range(2):
        rows = [(below, group * HALF), (own, group * BLOCK), (above, group * HALF)]
        if group == 0:
            sides = [(outer, inner, 0, NEAR_SPANS[:-1]),
                     (first_outer, first_inner, SIDE_SIZE + FLAT_TILES - SPLIT, NEAR_SPANS[-1:])]
        else:
            sides = [(outer, inner, SPLIT, NEAR_SPANS)]
        fill_block(block, NEAR, rows, NEAR, sides)

        def store(x, y, value, group=group):
            out[x, pl.ds(group * BLOCK + y * 8, 8), :] = value

        smooth(block, coef, FAR - NEAR, table_re, table_im, first, second, store)


def old_images(*args):
    return pl.pallas_call(
        old_kernel,
        out_shape=jax.ShapeDtypeStruct((LX, 2 * BLOCK, NZ), F32),
        in_specs=[VMEM] * 8,
        out_specs=VMEM,
        scratch_shapes=smooth_scratch(NEAR),
        compiler_params=pltpu.CompilerParams(vmem_limit_bytes=16 << 20),
        cost_estimate=pl.CostEstimate(flops=12_000_000, bytes_accessed=24_000_000, transcendentals=0),
        name="old_images",
    )(*args)


def split3(value):
    high = value.astype(BF16)
    rest = value - high.astype(F32)
    middle = rest.astype(BF16)
    low = (rest - middle.astype(F32)).astype(BF16)
    return high, middle, low


def basis_plane(start, w, old_image, w_image, x):
    refs = [(start, 0), (start, LY), (start, 2 * LY), (w, None), (old_image, 0), (old_image, LY), (w_image, 0)]
    rows = []
    for ref, first in refs:
        if first is None:
            tiles = [ref[x, NEAR + y] for y in range(LY)]
        else:
            tiles = [ref[x, pl.ds((first + y) * 8, 8), :] for y in range(LY)]
        rows.append(jnp.concatenate(tiles, axis=1))
    rows.append(jnp.zeros((8, LY * NZ), F32))
    return jnp.concatenate(rows, axis=0)


def lane_roll(value, amount):
    return pltpu.roll(value, amount % NZ, 1)


SLOTS = [(0, 0), (0, 56), (1, 0), (1, 40), (1, 72), (1, 96), (0, 104)]


def pack_gram(gram):
    lane = lax.broadcasted_iota(jnp.int32, (8, NZ), 1)
    row = lax.broadcasted_iota(jnp.int32, (8, NZ), 0)
    packed = jnp.zeros((8, NZ), F32)
    for b in range(BLOCKS):
        rows = gram[8 * b:8 * b + 8]
        turned = jnp.where(lane % 8 < 4, lane_roll(rows, -4), -lane_roll(rows, 4))
        both = rows + pltpu.roll(turned, 4, 0)
        half, start = SLOTS[b]
        moved = lane_roll(both, start - 8 * b)
        if half:
            moved = pltpu.roll(moved, 4, 0)
        keep = (lane >= start) & (lane < start + 8 * (BLOCKS - b)) & (row // 4 == half)
        packed = packed + jnp.where(keep, moved, 0.0)
    return packed


def unpack_gram(packed):
    lane = lax.broadcasted_iota(jnp.int32, (8, NZ), 1)
    row = lax.broadcasted_iota(jnp.int32, (8, NZ), 0)
    rows = []
    for b in range(BLOCKS):
        half, start = SLOTS[b]
        moved = lane_roll(packed, 8 * b - start)
        if half:
            moved = pltpu.roll(moved, 4, 0)
        keep = (lane >= 8 * b) & (lane < 8 * BLOCKS) & (row < 4)
        moved = jnp.where(keep, moved, 0.0)
        turned = jnp.where(lane % 8 < 4, -lane_roll(moved, -4), lane_roll(moved, 4))
        rows.append(moved + pltpu.roll(turned, 4, 0))
    rows.append(jnp.zeros((NZ - 8 * BLOCKS, NZ), F32))
    upper = jnp.concatenate(rows, axis=0)
    tall = lax.broadcasted_iota(jnp.int32, (NZ, NZ), 0)
    wide = lax.broadcasted_iota(jnp.int32, (NZ, NZ), 1)
    return jnp.where(tall // 8 <= wide // 8, upper, upper.T)


def gram_kernel(peers, w, coef, outer, inner, start, old_image, w_image, out,
                block, first, second, table_re, table_im, diag_re, diag_im):
    fill_tables(coef, FAR - NEAR, table_re, table_im, diag_re, diag_im)
    block[...] = jnp.zeros(block.shape, F32)
    for x in range(LX):
        block[NEAR + x] = w[x]
    fill_sides(block, NEAR, [(outer, inner, 0, NEAR_SPANS)])

    def store(x, y, value):
        w_image[x, pl.ds(y * 8, 8), :] = value

    smooth(block, coef, FAR - NEAR, table_re, table_im, first, second, store)

    def plane(x, total):
        stacked = jnp.concatenate(split3(basis_plane(start, w, old_image, w_image, x)), axis=0)
        return total + lax.dot_general(stacked, stacked, (((1,), (1,)), ((), ())), preferred_element_type=F32)

    total = lax.fori_loop(0, LX, plane, jnp.zeros((3 * ROWS, 3 * ROWS), F32), unroll=True)
    tall = total[0:ROWS] + total[ROWS:2 * ROWS] + total[2 * ROWS:3 * ROWS]
    gram = tall[:, 0:ROWS] + tall[:, ROWS:2 * ROWS] + tall[:, 2 * ROWS:3 * ROWS]
    gram = jnp.concatenate([gram, jnp.zeros((ROWS, NZ - ROWS), F32)], axis=1)
    packed = pack_gram(gram)
    for peer in range(peers):
        out[peer] = packed


def image_and_gram(peers, *args):
    return pl.pallas_call(
        functools.partial(gram_kernel, peers),
        out_shape=(jax.ShapeDtypeStruct((LX, LY * 8, NZ), F32),
                   jax.ShapeDtypeStruct((peers, 8, NZ), F32)),
        in_specs=[VMEM] * 6,
        out_specs=(VMEM, VMEM),
        scratch_shapes=smooth_scratch(NEAR),
        compiler_params=pltpu.CompilerParams(vmem_limit_bytes=32 << 20),
        name="image_and_gram",
    )(*args)


def sum_kernel(parts, out):
    total = jnp.sum(parts[...], axis=0)
    for peer in range(out.shape[0]):
        out[peer] = total


def sum_and_spread(parts, peers):
    return pl.pallas_call(
        sum_kernel,
        out_shape=jax.ShapeDtypeStruct((peers, 8, NZ), F32),
        in_specs=[VMEM],
        out_specs=VMEM,
        compiler_params=pltpu.CompilerParams(vmem_limit_bytes=1 << 20),
        name="sum_and_spread",
    )(parts)


def exact(left, right, dims):
    parts = [part.astype(F32) for part in split3(left)]
    stacked = jnp.concatenate([*parts, jnp.zeros((8, NZ), F32)], axis=0).astype(BF16)
    high, middle, low = (
        lax.dot_general(stacked, part, (dims, ((), ())), preferred_element_type=F32) for part in split3(right)
    )
    small = low[0:8] + middle[8:16] + high[16:24]
    return small + (middle[0:8] + high[8:16]) + high[0:8]


def mul(left, right):
    return exact(left, right, ((1,), (0,)))


def mul_t(left, right):
    return exact(left, right, ((1,), (1,)))


def inverse_factor(gram):
    lane = lax.broadcasted_iota(jnp.int32, (8, NZ), 1)
    row = lax.broadcasted_iota(jnp.int32, (8, NZ), 0)
    work = jnp.where(lane < 8, gram, jnp.where(lane == row + 8, 1.0, 0.0))
    pivots = jnp.ones((8, NZ), F32)
    for s in range(4):
        pivot = jnp.broadcast_to(work[s:s + 1, s:s + 1], (8, NZ))
        pivots = jnp.where(row % 4 == s, pivot, pivots)
        if s < 3:
            change = work[:, s:s + 1] * work[s:s + 1, :] + work[:, 4 + s:5 + s] * work[4 + s:5 + s, :]
            work = jnp.where(row % 4 > s, work - change / pivot, work)
    return jnp.where(lane < 8, lane_roll(work, -8), 0.0) / jnp.sqrt(pivots)


def at_row(rows, start):
    parts = [rows, jnp.zeros((NZ - 8 - start, NZ), F32)]
    if start:
        parts.insert(0, jnp.zeros((start, NZ), F32))
    return jnp.concatenate(parts, axis=0)


def coefficients(gram):
    lane = lax.broadcasted_iota(jnp.int32, (8, NZ), 1)
    row = lax.broadcasted_iota(jnp.int32, (8, NZ), 0)
    new_at = 8 * BLOCKS

    once = jnp.where(lane < 24, gram[24:32], 0.0)
    again = jnp.where(lane < 24, mul(once, gram), 0.0)
    rows = jnp.where(lane == row + 24, 1.0, 0.0) - (2.0 * once - again)
    rows_gram = mul(rows, gram)
    spread = at_row(rows, 0)
    factor = inverse_factor(mul_t(rows_gram, spread))
    new = mul(factor, spread)
    new_gram = mul(factor, at_row(rows_gram, 0))
    new_rows = at_row(new, new_at)
    border = at_row(new_gram + mul_t(new_gram, new_rows), new_at)
    body = jnp.concatenate([gram[0:new_at], new_gram, gram[new_at + 8:]], axis=0)
    image = (jnp.where((lane >= 32) & (lane < 48), lane_roll(new, 32), 0.0)
             + jnp.where((lane >= 24) & (lane < 32), lane_roll(new, 8), 0.0)
             + jnp.where((lane >= 48) & (lane < 56), lane_roll(new, 24), 0.0))
    inside = ((lane >= 8) & (lane < 24)) | ((lane >= new_at) & (lane < new_at + 8))

    def times_gram(value):
        return mul(value, body) + mul_t(value, border)

    once = jnp.where(inside, times_gram(image), 0.0)
    again = jnp.where(inside, times_gram(once), 0.0)
    rows = image - (2.0 * once - again)
    spread = at_row(rows, 0)
    newest = mul(inverse_factor(mul_t(times_gram(rows), spread)), spread)
    on_new = jnp.where((lane >= new_at) & (lane < new_at + 8), newest, 0.0)
    return new, newest - on_new + mul(on_new, new_rows)


def final_kernel(cells, parts, start, w, old_image, w_image, out):
    gram = unpack_gram(jnp.sum(parts[...], axis=0) * (1.0 / cells))
    new, newest = coefficients(gram)
    mapping = jnp.concatenate([new, newest], axis=0)[:, 0:ROWS]
    pieces = [jnp.concatenate([piece] * 3, axis=1) for piece in split3(mapping)]
    stacked_map = jnp.concatenate(pieces, axis=0)

    def plane(x, carry):
        stacked = jnp.concatenate(split3(basis_plane(start, w, old_image, w_image, x)), axis=0)
        full = lax.dot_general(stacked_map, stacked, (((1,), (0,)), ((), ())), preferred_element_type=F32)
        result = full[32:48] + full[16:32] + full[0:16]
        for k in range(2):
            tiles = jnp.stack([result[8 * k:8 * k + 8, y * NZ:(y + 1) * NZ] for y in range(LY)])
            out[k, :, x] = jnp.swapaxes(tiles, 0, 1)
        return carry

    lax.fori_loop(0, LX, plane, 0, unroll=True)


def finish(cells, *args):
    return pl.pallas_call(
        functools.partial(final_kernel, cells),
        out_shape=jax.ShapeDtypeStruct((2, 8, LX, LY, NZ), F32),
        in_specs=[VMEM] * 5,
        out_specs=VMEM,
        compiler_params=pltpu.CompilerParams(vmem_limit_bytes=32 << 20),
        name="finish",
    )(*args)


GX = ("z", "core")


def turn_kernel(prior_hbm, coefficient_hbm, start, up, down, prior, coefficient, arrived):
    copies = (pltpu.make_async_copy(prior_hbm, prior, arrived.at[0]),
              pltpu.make_async_copy(coefficient_hbm, coefficient, arrived.at[1]))
    for copy in copies:
        copy.start()
    for copy in copies:
        copy.wait()
    for x in range(LX):
        for k in range(3):
            block = jnp.swapaxes(prior[k, :, :, x].reshape(8, LY, NZ), 0, 1).reshape(BLOCK, NZ)
            start[x, pl.ds(k * BLOCK, BLOCK), :] = block
            if k < 2:
                up[x, pl.ds(k * HALF, HALF), :] = block[HALF:]
                down[x, pl.ds(k * HALF, HALF), :] = block[:HALF]
            else:
                up[x, pl.ds(2 * HALF, BLOCK), :] = block
                down[x, pl.ds(2 * HALF, BLOCK), :] = block
        value = coefficient[x]
        start[x, pl.ds(3 * BLOCK, LY), :] = value
        up[x, pl.ds(2 * HALF + BLOCK, LY), :] = value
        down[x, pl.ds(2 * HALF + BLOCK, LY), :] = value


def turn(prior, coefficient):
    message = jax.ShapeDtypeStruct((LX, 2 * HALF + BLOCK + LY, NZ), F32)
    return pl.pallas_call(
        turn_kernel,
        out_shape=(jax.ShapeDtypeStruct((LX, 3 * BLOCK + LY, NZ), F32), message, message),
        in_specs=[pl.BlockSpec(memory_space=pl.ANY)] * 2,
        out_specs=(VMEM,) * 3,
        scratch_shapes=[pltpu.VMEM(prior.shape, F32), pltpu.VMEM(coefficient.shape, F32),
                        pltpu.SemaphoreType.DMA((2,))],
        compiler_params=pltpu.CompilerParams(vmem_limit_bytes=1 << 20),
        name="turn",
    )(prior, coefficient)


def from_both(axis, count, to_higher, to_lower):
    return (
        lax.ppermute(to_higher, axis, [(i, i + 1) for i in range(count - 1)]),
        lax.ppermute(to_lower, axis, [(i + 1, i) for i in range(count - 1)]),
    )


def exchange(count, outward, inward):
    inner = [(i, i ^ 1) for i in range(count)]
    outer = [(i, i + 1 if i % 2 else i - 1) for i in range(1, count - 1)]
    return lax.ppermute(outward, GX, outer), lax.ppermute(inward, GX, inner)


def per_device(nx, ny, nz, prior, coefficient):
    cells = coefficient.size * nx * ny
    start, up, down = turn(prior, coefficient)
    rims = from_both("gy", ny, up, down)
    outward, inward, old_outward, old_inward = pack_all(start, *rims)
    sides = exchange(nx, outward, inward)
    old_sides = exchange(nx, old_outward, old_inward)
    w, coef, w_outward, w_inward = first_image(start, *rims, *sides)
    w_sides = exchange(nx, w_outward, w_inward)
    old_image = old_images(coef, start, *rims, *old_sides, *sides)

    w_image, spread = image_and_gram(2 * ny, w, coef, *w_sides, start, old_image)
    got = lax.all_to_all(spread, ("core", "gy"), 0, 0)
    got = lax.all_to_all(sum_and_spread(got, nz), "z", 0, 0)
    out = finish(cells, got, start, w, old_image, w_image)
    return out.reshape(2, 2, 4, LX, LY, NZ)


def solution(mesh):
    nx, ny = mesh.shape["gx"], mesh.shape["gy"]
    fine = Mesh(np.asarray(mesh.devices).reshape(nx // 2, 2, ny), ("z", "core", "gy"))
    in_specs = (P(None, None, None, GX, "gy", None), P(GX, "gy", None))
    out_specs = P(None, None, None, GX, "gy", None)
    return jax.shard_map(
        functools.partial(per_device, nx, ny, nx // 2),
        mesh=fine, in_specs=in_specs, out_specs=out_specs, check_vma=False,
    )
```

```python
import functools

import jax
import jax.numpy as jnp
import numpy as np
from jax import lax
from jax.experimental import pallas as pl
from jax.experimental.pallas import tpu as pltpu
from jax.sharding import Mesh, PartitionSpec as P

LX, LY, NZ = 4, 8, 128
NEAR, FAR = 4, 8
BLOCKS = 7
ROWS = 64
F32 = jnp.float32
BF16 = jnp.bfloat16
VMEM = pl.BlockSpec(memory_space=pltpu.VMEM)


BLOCK = LY * 8
HALF = NEAR * 8


def spans(halo, begin, end):
    found, place = [], 0
    for d in range(begin + 1, end + 1):
        found.append((d, halo - d, place))
        place += LY + 2 * (halo - d)
    return found, place


NEAR_SPANS, NEAR_SIZE = spans(NEAR, 0, LX)
SIDE_SPANS, SIDE_SIZE = spans(FAR, 0, LX)
FLAT_TILES = -(-SIDE_SIZE // 8)
SPLIT = NEAR_SPANS[-1][2]
FIRST_TILES = SIDE_SIZE + FLAT_TILES + NEAR_SIZE - SPLIT
SECOND_TILES = SPLIT + NEAR_SIZE


def sent_plane(inner, d):
    core = lax.axis_index("core")
    far = core if inner else 1 - core
    return (1 - far) * (LX - d) + far * (d - 1)


def halo_plane(inner, d):
    core = lax.axis_index("core")
    far = core if inner else 1 - core
    return (1 - far) * (NEAR + LX - 1 + d) + far * (NEAR - d)


def pack_columns(out, start, found, inner, rows, reach):
    (below, low_row), (own, own_row), (above, high_row) = rows
    for d, more, place in found:
        x = sent_plane(inner, d)
        spot = start + place
        size = more * 8
        if more:
            out[pl.ds(spot, more)] = below[x, pl.ds(low_row + reach * 8 - size, size), :].reshape(more, 8, NZ)
            out[pl.ds(spot + more + LY, more)] = above[x, pl.ds(high_row, size), :].reshape(more, 8, NZ)
        out[pl.ds(spot + more, LY)] = own[x, pl.ds(own_row, BLOCK), :].reshape(LY, 8, NZ)


def pack_coefficient(out, start, found, inner, below, own, above):
    for d, more, place in found:
        x = sent_plane(inner, d)
        for y in range(-more, LY + more):
            if y < 0:
                ref, row = below, 2 * HALF + BLOCK + LY + y
            elif y < LY:
                ref, row = own, 3 * BLOCK + y
            else:
                ref, row = above, 2 * HALF + BLOCK + y - LY
            spot = place + more + y
            out[start + spot // 8, pl.ds(spot % 8, 1), :] = ref[x, pl.ds(row, 1), :]


def column_kernel(own, below, above, outward, inward, old_outward, old_inward):
    for first, second, inner in ((outward, old_outward, False), (inward, old_inward, True)):
        rows = [(below, 2 * HALF), (own, 2 * BLOCK), (above, 2 * HALF)]
        pack_columns(first, 0, SIDE_SPANS, inner, rows, FAR)
        if SIDE_SIZE % 8:
            first[SIDE_SIZE + FLAT_TILES - 1] = jnp.zeros((8, NZ), F32)
        pack_coefficient(first, SIDE_SIZE, SIDE_SPANS, inner, below, own, above)
        rows = [(below, 0), (own, 0), (above, 0)]
        pack_columns(second, 0, NEAR_SPANS[:-1], inner, rows, NEAR)
        pack_columns(first, SIDE_SIZE + FLAT_TILES - SPLIT, NEAR_SPANS[-1:], inner, rows, NEAR)
        rows = [(below, HALF), (own, BLOCK), (above, HALF)]
        pack_columns(second, SPLIT, NEAR_SPANS, inner, rows, NEAR)


def pack_all(*args):
    shapes = tuple(jax.ShapeDtypeStruct((size, 8, NZ), F32) for size in [FIRST_TILES] * 2 + [SECOND_TILES] * 2)
    return pl.pallas_call(
        column_kernel,
        out_shape=shapes,
        in_specs=[VMEM] * 3,
        out_specs=(VMEM,) * 4,
        compiler_params=pltpu.CompilerParams(vmem_limit_bytes=1 << 20),
        name="pack_all",
    )(*args)


def fill_sides(wide, halo, sides):
    for outer, inner, start, found in sides:
        for d, more, place in found:
            count = LY + 2 * more
            begin = halo - more
            wide[halo_plane(False, d), begin:begin + count] = outer[pl.ds(start + place, count)]
            wide[halo_plane(True, d), begin:begin + count] = inner[pl.ds(start + place, count)]


def fill_block(wide, halo, rows, reach, sides):
    (below, low_row), (own, own_row), (above, high_row) = rows
    wide[...] = jnp.zeros(wide.shape, F32)
    for x in range(LX):
        size = halo * 8
        wide[NEAR + x, 0:halo] = below[x, pl.ds(low_row + reach * 8 - size, size), :].reshape(halo, 8, NZ)
        wide[NEAR + x, halo:halo + LY] = own[x, pl.ds(own_row, BLOCK), :].reshape(LY, 8, NZ)
        wide[NEAR + x, halo + LY:] = above[x, pl.ds(high_row, size), :].reshape(halo, 8, NZ)
    fill_sides(wide, halo, sides)


def fill_flat(wide, below, own, above, outer, inner):
    wide[...] = jnp.zeros(wide.shape, F32)
    for x in range(LX):
        wide[NEAR + x, 0:FAR] = below[x, pl.ds(2 * HALF + BLOCK, LY), :]
        wide[NEAR + x, FAR:FAR + LY] = own[x, pl.ds(3 * BLOCK, LY), :]
        wide[NEAR + x, FAR + LY:] = above[x, pl.ds(2 * HALF + BLOCK, LY), :]
    for d, more, place in SIDE_SPANS:
        for i in range(LY + 2 * more):
            tile, row = SIDE_SIZE + (place + i) // 8, (place + i) % 8
            y = FAR - more + i
            wide[halo_plane(False, d), pl.ds(y, 1), :] = outer[tile, pl.ds(row, 1), :]
            wide[halo_plane(True, d), pl.ds(y, 1), :] = inner[tile, pl.ds(row, 1), :]


def fill_tables(coef, skip, table_re, table_im, diag_re, diag_im):
    value = coef[...]
    real = 6.0 - value
    imag = 0.5 * value
    scale = jnp.where(value > 0.0, 0.8 / (real * real + imag * imag), 0.0)
    diag_re[...] = real * scale
    diag_im[...] = imag * scale
    sign = jnp.where(lax.broadcasted_iota(jnp.int32, (8, NZ), 0) < 4, 1.0, -1.0)
    size_x, size_y = table_re.shape[:2]

    def body(x, carry):
        for y in range(size_y):
            spot = pl.ds(y + skip, 1)
            table_re[x, y] = jnp.broadcast_to(diag_re[x, spot, :], (8, NZ))
            table_im[x, y] = jnp.broadcast_to(diag_im[x, spot, :], (8, NZ)) * sign
        return carry

    lax.fori_loop(0, size_x, body, 0, unroll=True)


def depth_sum(value):
    lane = lax.broadcasted_iota(jnp.int32, value.shape, 1)
    above = jnp.where(lane == 0, 0.0, pltpu.roll(value, 1, 1))
    below = jnp.where(lane == NZ - 1, 0.0, pltpu.roll(value, NZ - 1, 1))
    return above + below


def smooth(block, coef, skip, table_re, table_im, first, second, store):
    size_x, size_y = block.shape[:2]

    def solve(value, x, y):
        return table_re[x, y] * value + table_im[x, y] * pltpu.roll(value, 4, 0)

    def planes(k, body):
        lax.fori_loop(k, size_x - k, functools.partial(body, k, size_y - k), 0, unroll=True)

    def start(low, high, x, carry):
        for y in range(low, high):
            first[x, y] = solve(block[x, y], x, y)
        return carry

    def around(ref, x, low, high):
        line = [ref[x, y] for y in range(low - 1, high + 1)]
        for y in range(low, high):
            mid = line[y - low + 1]
            total = ref[x - 1, y] + ref[x + 1, y] + line[y - low] + line[y - low + 2]
            yield y, mid, total + depth_sum(mid)

    planes(0, start)
    here, there = first, second
    for k in range(1, 4):
        def sweep(low, high, x, carry, here=here, there=there):
            for y, mid, total in around(here, x, low, high):
                there[x, y] = 0.2 * mid + solve(block[x, y] + total, x, y)
            return carry

        planes(k, sweep)
        here, there = there, here

    def image(x, carry):
        for y, mid, total in around(here, x, 4, size_y - 4):
            diag = 6.0 - coef[x, pl.ds(y + skip, 1), :]
            store(x - 4, y - 4, diag * mid - total)
        return carry

    lax.fori_loop(4, size_x - 4, image, 0, unroll=True)


def wide_shape(halo):
    return (LX + 2 * NEAR, LY + 2 * halo)


FLAT = pltpu.VMEM((*wide_shape(FAR), NZ), F32)


def smooth_scratch(halo):
    return [pltpu.VMEM((*wide_shape(halo), 8, NZ), F32)] * 5 + [FLAT] * 2


def first_kernel(own, below, above, outer, inner, w, coef, outward, inward, block, first, second,
                 table_re, table_im, diag_re, diag_im):
    fill_flat(coef, below, own, above, outer, inner)
    fill_tables(coef, 0, table_re, table_im, diag_re, diag_im)
    rows = [(below, 2 * HALF), (own, 2 * BLOCK), (above, 2 * HALF)]
    fill_block(block, FAR, rows, FAR, [(outer, inner, 0, SIDE_SPANS)])

    def store(x, y, value):
        w[x, y] = value

    smooth(block, coef, 0, table_re, table_im, first, second, store)
    for d, more, place in NEAR_SPANS:
        count = LY + 2 * more
        outward[pl.ds(place, count)] = w[sent_plane(False, d), pl.ds(NEAR - more, count)]
        inward[pl.ds(place, count)] = w[sent_plane(True, d), pl.ds(NEAR - more, count)]


def first_image(*args):
    side = jax.ShapeDtypeStruct((NEAR_SIZE, 8, NZ), F32)
    return pl.pallas_call(
        first_kernel,
        out_shape=(jax.ShapeDtypeStruct((LX, LY + 2 * NEAR, 8, NZ), F32),
                   jax.ShapeDtypeStruct((*wide_shape(FAR), NZ), F32), side, side),
        in_specs=[VMEM] * 5,
        out_specs=(VMEM,) * 4,
        scratch_shapes=smooth_scratch(FAR),
        compiler_params=pltpu.CompilerParams(vmem_limit_bytes=16 << 20),
        cost_estimate=pl.CostEstimate(flops=12_000_000, bytes_accessed=18_000_000, transcendentals=0),
        name="first_image",
    )(*args)


def old_kernel(coef, own, below, above, outer, inner, first_outer, first_inner, out, block, first, second,
               table_re, table_im, diag_re, diag_im):
    fill_tables(coef, FAR - NEAR, table_re, table_im, diag_re, diag_im)
    for group in range(2):
        rows = [(below, group * HALF), (own, group * BLOCK), (above, group * HALF)]
        if group == 0:
            sides = [(outer, inner, 0, NEAR_SPANS[:-1]),
                     (first_outer, first_inner, SIDE_SIZE + FLAT_TILES - SPLIT, NEAR_SPANS[-1:])]
        else:
            sides = [(outer, inner, SPLIT, NEAR_SPANS)]
        fill_block(block, NEAR, rows, NEAR, sides)

        def store(x, y, value, group=group):
            out[x, pl.ds(group * BLOCK + y * 8, 8), :] = value

        smooth(block, coef, FAR - NEAR, table_re, table_im, first, second, store)


def old_images(*args):
    return pl.pallas_call(
        old_kernel,
        out_shape=jax.ShapeDtypeStruct((LX, 2 * BLOCK, NZ), F32),
        in_specs=[VMEM] * 8,
        out_specs=VMEM,
        scratch_shapes=smooth_scratch(NEAR),
        compiler_params=pltpu.CompilerParams(vmem_limit_bytes=16 << 20),
        cost_estimate=pl.CostEstimate(flops=12_000_000, bytes_accessed=24_000_000, transcendentals=0),
        name="old_images",
    )(*args)


def split3(value):
    high = value.astype(BF16)
    rest = value - high.astype(F32)
    middle = rest.astype(BF16)
    low = (rest - middle.astype(F32)).astype(BF16)
    return high, middle, low


def basis_plane(start, w, old_image, w_image, x):
    refs = [(start, 0), (start, LY), (start, 2 * LY), (w, None), (old_image, 0), (old_image, LY), (w_image, 0)]
    rows = []
    for ref, first in refs:
        if first is None:
            tiles = [ref[x, NEAR + y] for y in range(LY)]
        else:
            tiles = [ref[x, pl.ds((first + y) * 8, 8), :] for y in range(LY)]
        rows.append(jnp.concatenate(tiles, axis=1))
    rows.append(jnp.zeros((8, LY * NZ), F32))
    return jnp.concatenate(rows, axis=0)


def lane_roll(value, amount):
    return pltpu.roll(value, amount % NZ, 1)


SLOTS = [(0, 0), (0, 56), (1, 0), (1, 40), (1, 72), (1, 96), (0, 104)]


def pack_gram(gram):
    lane = lax.broadcasted_iota(jnp.int32, (8, NZ), 1)
    row = lax.broadcasted_iota(jnp.int32, (8, NZ), 0)
    packed = jnp.zeros((8, NZ), F32)
    for b in range(BLOCKS):
        rows = gram[8 * b:8 * b + 8]
        turned = jnp.where(lane % 8 < 4, lane_roll(rows, -4), -lane_roll(rows, 4))
        both = rows + pltpu.roll(turned, 4, 0)
        half, start = SLOTS[b]
        moved = lane_roll(both, start - 8 * b)
        if half:
            moved = pltpu.roll(moved, 4, 0)
        keep = (lane >= start) & (lane < start + 8 * (BLOCKS - b)) & (row // 4 == half)
        packed = packed + jnp.where(keep, moved, 0.0)
    return packed


def unpack_gram(packed):
    lane = lax.broadcasted_iota(jnp.int32, (8, NZ), 1)
    row = lax.broadcasted_iota(jnp.int32, (8, NZ), 0)
    rows = []
    for b in range(BLOCKS):
        half, start = SLOTS[b]
        moved = lane_roll(packed, 8 * b - start)
        if half:
            moved = pltpu.roll(moved, 4, 0)
        keep = (lane >= 8 * b) & (lane < 8 * BLOCKS) & (row < 4)
        moved = jnp.where(keep, moved, 0.0)
        turned = jnp.where(lane % 8 < 4, -lane_roll(moved, -4), lane_roll(moved, 4))
        rows.append(moved + pltpu.roll(turned, 4, 0))
    rows.append(jnp.zeros((NZ - 8 * BLOCKS, NZ), F32))
    upper = jnp.concatenate(rows, axis=0)
    tall = lax.broadcasted_iota(jnp.int32, (NZ, NZ), 0)
    wide = lax.broadcasted_iota(jnp.int32, (NZ, NZ), 1)
    return jnp.where(tall // 8 <= wide // 8, upper, upper.T)


def gram_kernel(peers, w, coef, outer, inner, start, old_image, w_image, out,
                block, first, second, table_re, table_im, diag_re, diag_im):
    fill_tables(coef, FAR - NEAR, table_re, table_im, diag_re, diag_im)
    block[...] = jnp.zeros(block.shape, F32)
    for x in range(LX):
        block[NEAR + x] = w[x]
    fill_sides(block, NEAR, [(outer, inner, 0, NEAR_SPANS)])

    def store(x, y, value):
        w_image[x, pl.ds(y * 8, 8), :] = value

    smooth(block, coef, FAR - NEAR, table_re, table_im, first, second, store)

    def plane(x, total):
        stacked = jnp.concatenate(split3(basis_plane(start, w, old_image, w_image, x)), axis=0)
        return total + lax.dot_general(stacked, stacked, (((1,), (1,)), ((), ())), preferred_element_type=F32)

    total = lax.fori_loop(0, LX, plane, jnp.zeros((3 * ROWS, 3 * ROWS), F32), unroll=True)
    tall = total[0:ROWS] + total[ROWS:2 * ROWS] + total[2 * ROWS:3 * ROWS]
    gram = tall[:, 0:ROWS] + tall[:, ROWS:2 * ROWS] + tall[:, 2 * ROWS:3 * ROWS]
    gram = jnp.concatenate([gram, jnp.zeros((ROWS, NZ - ROWS), F32)], axis=1)
    packed = pack_gram(gram)
    for peer in range(peers):
        out[peer] = packed


def image_and_gram(peers, *args):
    return pl.pallas_call(
        functools.partial(gram_kernel, peers),
        out_shape=(jax.ShapeDtypeStruct((LX, LY * 8, NZ), F32),
                   jax.ShapeDtypeStruct((peers, 8, NZ), F32)),
        in_specs=[VMEM] * 6,
        out_specs=(VMEM, VMEM),
        scratch_shapes=smooth_scratch(NEAR),
        compiler_params=pltpu.CompilerParams(vmem_limit_bytes=32 << 20),
        name="image_and_gram",
    )(*args)


def sum_kernel(parts, out):
    total = jnp.sum(parts[...], axis=0)
    for peer in range(out.shape[0]):
        out[peer] = total


def sum_and_spread(parts, peers):
    return pl.pallas_call(
        sum_kernel,
        out_shape=jax.ShapeDtypeStruct((peers, 8, NZ), F32),
        in_specs=[VMEM],
        out_specs=VMEM,
        compiler_params=pltpu.CompilerParams(vmem_limit_bytes=1 << 20),
        name="sum_and_spread",
    )(parts)


def exact(left, right, dims):
    parts = [part.astype(F32) for part in split3(left)]
    stacked = jnp.concatenate([*parts, jnp.zeros((8, NZ), F32)], axis=0).astype(BF16)
    high, middle, low = (
        lax.dot_general(stacked, part, (dims, ((), ())), preferred_element_type=F32) for part in split3(right)
    )
    small = low[0:8] + middle[8:16] + high[16:24]
    return small + (middle[0:8] + high[8:16]) + high[0:8]


def mul(left, right):
    return exact(left, right, ((1,), (0,)))


def mul_t(left, right):
    return exact(left, right, ((1,), (1,)))


def inverse_factor(gram):
    lane = lax.broadcasted_iota(jnp.int32, (8, NZ), 1)
    row = lax.broadcasted_iota(jnp.int32, (8, NZ), 0)
    work = jnp.where(lane < 8, gram, jnp.where(lane == row + 8, 1.0, 0.0))
    pivots = jnp.ones((8, NZ), F32)
    for s in range(4):
        pivot = jnp.broadcast_to(work[s:s + 1, s:s + 1], (8, NZ))
        pivots = jnp.where(row % 4 == s, pivot, pivots)
        if s < 3:
            change = work[:, s:s + 1] * work[s:s + 1, :] + work[:, 4 + s:5 + s] * work[4 + s:5 + s, :]
            work = jnp.where(row % 4 > s, work - change / pivot, work)
    return jnp.where(lane < 8, lane_roll(work, -8), 0.0) / jnp.sqrt(pivots)


def at_row(rows, start):
    parts = [rows, jnp.zeros((NZ - 8 - start, NZ), F32)]
    if start:
        parts.insert(0, jnp.zeros((start, NZ), F32))
    return jnp.concatenate(parts, axis=0)


def coefficients(gram):
    lane = lax.broadcasted_iota(jnp.int32, (8, NZ), 1)
    row = lax.broadcasted_iota(jnp.int32, (8, NZ), 0)
    new_at = 8 * BLOCKS

    once = jnp.where(lane < 24, gram[24:32], 0.0)
    again = jnp.where(lane < 24, mul(once, gram), 0.0)
    rows = jnp.where(lane == row + 24, 1.0, 0.0) - (2.0 * once - again)
    rows_gram = mul(rows, gram)
    spread = at_row(rows, 0)
    factor = inverse_factor(mul_t(rows_gram, spread))
    new = mul(factor, spread)
    new_gram = mul(factor, at_row(rows_gram, 0))
    new_rows = at_row(new, new_at)
    border = at_row(new_gram + mul_t(new_gram, new_rows), new_at)
    body = jnp.concatenate([gram[0:new_at], new_gram, gram[new_at + 8:]], axis=0)
    image = (jnp.where((lane >= 32) & (lane < 48), lane_roll(new, 32), 0.0)
             + jnp.where((lane >= 24) & (lane < 32), lane_roll(new, 8), 0.0)
             + jnp.where((lane >= 48) & (lane < 56), lane_roll(new, 24), 0.0))
    inside = ((lane >= 8) & (lane < 24)) | ((lane >= new_at) & (lane < new_at + 8))

    def times_gram(value):
        return mul(value, body) + mul_t(value, border)

    once = jnp.where(inside, times_gram(image), 0.0)
    again = jnp.where(inside, times_gram(once), 0.0)
    rows = image - (2.0 * once - again)
    spread = at_row(rows, 0)
    newest = mul(inverse_factor(mul_t(times_gram(rows), spread)), spread)
    on_new = jnp.where((lane >= new_at) & (lane < new_at + 8), newest, 0.0)
    return new, newest - on_new + mul(on_new, new_rows)


def final_kernel(cells, parts, start, w, old_image, w_image, out):
    gram = unpack_gram(jnp.sum(parts[...], axis=0) * (1.0 / cells))
    new, newest = coefficients(gram)
    mapping = jnp.concatenate([new, newest], axis=0)[:, 0:ROWS]
    pieces = [jnp.concatenate([piece] * 3, axis=1) for piece in split3(mapping)]
    stacked_map = jnp.concatenate(pieces, axis=0)

    def plane(x, carry):
        stacked = jnp.concatenate(split3(basis_plane(start, w, old_image, w_image, x)), axis=0)
        full = lax.dot_general(stacked_map, stacked, (((1,), (0,)), ((), ())), preferred_element_type=F32)
        result = full[32:48] + full[16:32] + full[0:16]
        for k in range(2):
            tiles = jnp.stack([result[8 * k:8 * k + 8, y * NZ:(y + 1) * NZ] for y in range(LY)])
            out[k, :, x] = jnp.swapaxes(tiles, 0, 1)
        return carry

    lax.fori_loop(0, LX, plane, 0, unroll=True)


def finish(cells, *args):
    return pl.pallas_call(
        functools.partial(final_kernel, cells),
        out_shape=jax.ShapeDtypeStruct((2, 8, LX, LY, NZ), F32),
        in_specs=[VMEM] * 5,
        out_specs=VMEM,
        compiler_params=pltpu.CompilerParams(vmem_limit_bytes=32 << 20),
        name="finish",
    )(*args)


GX = ("z", "core")


def turn_kernel(prior, coefficient, start, up, down):
    for x in range(LX):
        for k in range(3):
            block = jnp.swapaxes(prior[k, :, :, x].reshape(8, LY, NZ), 0, 1).reshape(BLOCK, NZ)
            start[x, pl.ds(k * BLOCK, BLOCK), :] = block
            if k < 2:
                up[x, pl.ds(k * HALF, HALF), :] = block[HALF:]
                down[x, pl.ds(k * HALF, HALF), :] = block[:HALF]
            else:
                up[x, pl.ds(2 * HALF, BLOCK), :] = block
                down[x, pl.ds(2 * HALF, BLOCK), :] = block
        value = coefficient[x]
        start[x, pl.ds(3 * BLOCK, LY), :] = value
        up[x, pl.ds(2 * HALF + BLOCK, LY), :] = value
        down[x, pl.ds(2 * HALF + BLOCK, LY), :] = value


def turn(prior, coefficient):
    message = jax.ShapeDtypeStruct((LX, 2 * HALF + BLOCK + LY, NZ), F32)
    return pl.pallas_call(
        turn_kernel,
        out_shape=(jax.ShapeDtypeStruct((LX, 3 * BLOCK + LY, NZ), F32), message, message),
        in_specs=[VMEM] * 2,
        out_specs=(VMEM,) * 3,
        compiler_params=pltpu.CompilerParams(vmem_limit_bytes=1 << 20),
        name="turn",
    )(prior, coefficient)


def from_both(axis, count, to_higher, to_lower):
    return (
        lax.ppermute(to_higher, axis, [(i, i + 1) for i in range(count - 1)]),
        lax.ppermute(to_lower, axis, [(i + 1, i) for i in range(count - 1)]),
    )


def exchange(count, outward, inward):
    inner = [(i, i ^ 1) for i in range(count)]
    outer = [(i, i + 1 if i % 2 else i - 1) for i in range(1, count - 1)]
    return lax.ppermute(outward, GX, outer), lax.ppermute(inward, GX, inner)


def per_device(nx, ny, nz, prior, coefficient):
    cells = coefficient.size * nx * ny
    start, up, down = turn(prior, coefficient)
    rims = from_both("gy", ny, up, down)
    outward, inward, old_outward, old_inward = pack_all(start, *rims)
    sides = exchange(nx, outward, inward)
    old_sides = exchange(nx, old_outward, old_inward)
    w, coef, w_outward, w_inward = first_image(start, *rims, *sides)
    w_sides = exchange(nx, w_outward, w_inward)
    old_image = old_images(coef, start, *rims, *old_sides, *sides)

    w_image, spread = image_and_gram(nz, w, coef, *w_sides, start, old_image)
    got = lax.all_to_all(spread, "z", 0, 0)
    got = lax.all_to_all(sum_and_spread(got, 2 * ny), ("core", "gy"), 0, 0)
    out = finish(cells, got, start, w, old_image, w_image)
    return out.reshape(2, 2, 4, LX, LY, NZ)


def solution(mesh):
    nx, ny = mesh.shape["gx"], mesh.shape["gy"]
    fine = Mesh(np.asarray(mesh.devices).reshape(nx // 2, 2, ny), ("z", "core", "gy"))
    in_specs = (P(None, None, None, GX, "gy", None), P(GX, "gy", None))
    out_specs = P(None, None, None, GX, "gy", None)
    return jax.shard_map(
        functools.partial(per_device, nx, ny, nx // 2),
        mesh=fine, in_specs=in_specs, out_specs=out_specs, check_vma=False,
    )
```
